32 devices in a mesh: dp: 8 (over y, x, core), chan: 4 (over z).
Axes of the slice: x: 2, y: 2, z: 4, core: 2. Of those that a mesh axis runs over, the one named last changes fastest.
Arguments:
- hidden: bfloat16 [16, 14, 14, 3072], P('dp', None, None, 'chan'), may hold values from -6 to 6
- conv_weight: bfloat16 [3, 3, 64, 3072], P(None, None, None, 'chan'), may hold values from -0.25 to 0.25
- se_down: bfloat16 [3072, 1024], P('chan'), may hold values from -0.875 to 0.875
- se_up: bfloat16 [1024, 3072], P(None, 'chan'), may hold values from -0.75 to 0.75
- proj_weight: bfloat16 [3072, 3072], P('chan'), may hold values from -0.109375 to 0.109375
- grad_out: bfloat16 [16, 14, 14, 3072], P('dp', None, None, 'chan'), may hold values from -6 to 6
Outputs:
- projected: bfloat16 [16, 14, 14, 3072], P('dp', None, None, 'chan')
- grad_hidden: bfloat16 [16, 14, 14, 3072], P('dp', None, None, 'chan')
- grad_proj: float32 [3072, 3072], P('chan', 'dp')
The draws below stay inside these ranges and needn't reach their ends.
All inputs are finite; a program needn't handle non-finite values.
Results may differ from the reference program's by a relative error of at most 0.024.
Values may be sent and summed in bfloat16 or wider, within the bound.
No kernel may reach another device: no remote copies, remote signals or barrier semaphores. Data moves between devices by JAX's collectives and lax.ppermute only.
A program may use at most 64 MiB of HBM per device.

```python
import jax
import jax.numpy as jnp
from jax import lax

C = 3072
GW = 64
SE = 1024
H = 14
W = 14
IMAGES = 16


def raised(values, key, source, target, shards_of, factor):
    def block_of(position):
        return (jnp.arange(values.shape[position]) // (values.shape[position] // shards_of)).reshape((-1,) + (1,) * (values.ndim - 1 - position))

    near = jax.random.permutation(key, shards_of)[block_of(target)]
    far = (block_of(target) + shards_of // 2) % shards_of
    return jnp.where((block_of(source) == near) | (block_of(source) == far), factor * values, values)


def block_levels(stream_key, shape, shards, least, top_value):
    level = 1.0
    for position, parts in shards:
        heights = jax.random.uniform(jax.random.fold_in(jax.random.fold_in(stream_key, 6), position), (parts,), jnp.float32, least / len(shards), top_value / len(shards))
        level = level * jnp.repeat(jnp.exp(heights), shape[position] // parts).reshape((-1,) + (1,) * (len(shape) - 1 - position))
    return level


def gaussian(own_key, dims, scale, reach, shards=(), kind=jnp.bfloat16):
    entries = jax.random.normal(own_key, dims, jnp.float32) * scale
    if len(shards) > 0:
        entries = block_levels(own_key, dims, shards, -0.22, 0.18) * entries
    return jnp.clip(entries, min=-reach, max=reach).astype(kind)


def bell_draw_with(own_key, extent, width, reach, pieces, heavy, held_as=jnp.bfloat16):
    array = width * jax.random.normal(own_key, extent, jnp.float32)
    if pieces:
        array = array * block_levels(own_key, extent, pieces, -0.22, 0.18)
    return jnp.clip(raised(array, jax.random.fold_in(own_key, 3), *heavy), -reach, reach).astype(held_as)


def setup_inputs(seed: int = 0) -> dict:
    key_of = jax.random.split(jax.random.key(seed), 7)
    return {
        "hidden": gaussian(key_of[0], (IMAGES, H, W, C), 1.0, 6.0, ((0, 8), (3, 4))),
        "conv_weight": gaussian(key_of[1], (3, 3, GW, C), (9 * GW) ** -0.5, 0.25, ((3, 4),)),
        "se_down": gaussian(key_of[2], (C, SE), (C // 64) ** -0.5, 0.875, ((0, 4),)),
        "se_up": gaussian(key_of[3], (SE, C), (SE // 16) ** -0.5, 0.75, ((1, 4),)),
        "proj_weight": gaussian(key_of[4], (C, C), C ** -0.5, 0.109375, ((0, 4),)),
        "grad_out": bell_draw_with(key_of[5], (IMAGES, H, W, C), 1.0, 6.0, ((0, 8), (3, 4)), (0, 3, 8, 2.0)),
    }


def grouped(inputs, kernel):
    return lax.conv_general_dilated(inputs, kernel, (1, 1), 'SAME', dimension_numbers=('NHWC', 'HWIO', 'NHWC'), feature_group_count=kernel.shape[3] // kernel.shape[2], preferred_element_type=jnp.float32)

def turned(kernel):
    size_in = kernel.shape[2]
    group_count = kernel.shape[3] // size_in
    split = kernel.reshape(3, 3, size_in, group_count, size_in)
    return jnp.transpose(split, (0, 1, 4, 3, 2))[::-1, ::-1].reshape(kernel.shape)

def silu_grad(values):
    logistic = jax.nn.sigmoid(values)
    return logistic * (1.0 + values * (1.0 - logistic))

def reference(hidden, conv_weight, se_down, se_up, proj_weight, grad_out):
    highest = lax.Precision.HIGHEST
    convolved = grouped(hidden, conv_weight)
    activated = jax.nn.silu(convolved).astype(jnp.bfloat16)
    act_float = activated.astype(jnp.float32)
    squeezed = lax.optimization_barrier(jnp.mean(act_float, axis=(1, 2)))
    excite_pre = jnp.dot(squeezed, se_down.astype(jnp.float32), precision=highest)
    gating = jax.nn.sigmoid(jnp.dot(jax.nn.silu(excite_pre), se_up.astype(jnp.float32), precision=highest))
    scaled = (act_float * gating[:, None, None, :]).astype(jnp.bfloat16)
    act_rows = scaled.reshape(-1, C)
    projected = jnp.dot(act_rows, proj_weight, preferred_element_type=jnp.float32).astype(jnp.bfloat16).reshape(hidden.shape)
    grad_rows = grad_out.reshape(-1, C)
    grad_proj = jnp.dot(act_rows.T, grad_rows, preferred_element_type=jnp.float32)
    scaled_grad = jnp.dot(grad_rows, proj_weight.T, preferred_element_type=jnp.float32).reshape(hidden.shape)
    gate_grad = lax.optimization_barrier(jnp.sum(scaled_grad * act_float, axis=(1, 2)))
    pre_grad = gate_grad * gating * (1.0 - gating)
    excite_grad = jnp.dot(pre_grad, se_up.astype(jnp.float32).T, precision=highest) * silu_grad(excite_pre)
    squeeze_grad = jnp.dot(excite_grad, se_down.astype(jnp.float32).T, precision=highest)
    act_grad = scaled_grad * gating[:, None, None, :] + squeeze_grad[:, None, None, :] / (H * W)
    conv_grad = (act_grad * silu_grad(convolved)).astype(jnp.bfloat16)
    grad_hidden = grouped(conv_grad, turned(conv_weight)).astype(jnp.bfloat16)
    return (projected, grad_hidden, grad_proj)
```

```python
import functools

import jax
import jax.numpy as jnp
from jax import lax
from jax.experimental import pallas as pl
from jax.experimental.pallas import tpu as pltpu
from jax.sharding import PartitionSpec as P

LANES = 256
VMEM = 40 * 1024 * 1024
F32 = jnp.float32
BF16 = jnp.bfloat16
HIGHEST = lax.Precision.HIGHEST


def params(**more):
    return pltpu.CompilerParams(vmem_limit_bytes=VMEM, **more)


def cost(flops, moved):
    return pl.CostEstimate(flops=flops, bytes_accessed=moved, transcendentals=0)


def silu_grad(values):
    logistic = jax.nn.sigmoid(values)
    return logistic * (1.0 + values * (1.0 - logistic))


def to_rows(images):
    return jnp.transpose(images, (1, 2, 0, 3)).reshape(-1, images.shape[3])


def from_rows(rows, shape):
    count, height, width, channels = shape
    return jnp.transpose(rows.reshape(height, width, count, channels), (1 + 1, 0, 1, 3))


def per_row(values, rows):
    tiled = jnp.concatenate([values] * (8 // values.shape[0]), axis=0)
    return jnp.broadcast_to(tiled[None], (rows // 8, 8, values.shape[1])).reshape(rows, -1)


def image_sum(values, images):
    folded = values.reshape(-1, 8, values.shape[1]).sum(axis=0)
    total = folded[:images]
    for start in range(images, 8, images):
        total = total + folded[start : start + images]
    return total


def convolve(rows_ref, pad_ref, weight_ref, height, width, images, turn):
    line, unit = width * images, 16 * images
    group = weight_ref.shape[2]
    pad_ref[...] = jnp.zeros_like(pad_ref)
    for h in range(height):
        pad_ref[pl.ds(8 + (h + 1) * unit + images, line), :] = rows_ref[pl.ds(h * line, line), :]
    row_group = lax.broadcasted_iota(jnp.int32, (LANES, LANES), 0) // group
    col_group = lax.broadcasted_iota(jnp.int32, (LANES, LANES), 1) // group
    mask = (row_group == col_group).astype(F32).astype(BF16)
    total = None
    for dw in range(3):
        shifted = pad_ref[pl.ds(8 + images * (dw - 1), (height + 2) * unit), :].astype(BF16)
        for dh in range(3):
            tap = weight_ref[2 - dh, 2 - dw] if turn else weight_ref[dh, dw]
            dense = jnp.concatenate([tap] * (LANES // group), axis=0) * mask
            part = lax.dot_general(
                shifted[dh * unit : (dh + height) * unit],
                dense,
                (((1,), (1 if turn else 0,)), ((), ())),
                preferred_element_type=F32,
            )
            total = part if total is None else total + part
    pad_ref[pl.ds(0, height * unit), :] = total
    for h in range(height):
        rows_ref[pl.ds(h * line, line), :] = pad_ref[pl.ds(h * unit + images, line), :]


def conv_forward_body(x_ref, w_ref, conv_ref, act_ref, mean_ref, pad_ref, *, height, width, images):
    conv_ref[...] = x_ref[...].astype(F32)
    convolve(conv_ref, pad_ref, w_ref, height, width, images, False)
    conv = conv_ref[...]
    act = (conv * jax.nn.sigmoid(conv)).astype(BF16)
    act_ref[...] = act
    mean_ref[...] = image_sum(act.astype(F32), images) / (height * width)


def conv_forward(rows, weight, shape):
    images, height, width, channels = shape
    count = rows.shape[0]
    block = pl.BlockSpec((count, LANES), lambda i: (0, i))
    return pl.pallas_call(
        functools.partial(conv_forward_body, height=height, width=width, images=images),
        grid=(channels // LANES,),
        in_specs=[block, pl.BlockSpec((3, 3, weight.shape[2], LANES), lambda i: (0, 0, 0, i))],
        out_specs=[block, block, pl.BlockSpec((images, LANES), lambda i: (0, i))],
        out_shape=[
            jax.ShapeDtypeStruct((count, channels), F32),
            jax.ShapeDtypeStruct((count, channels), BF16),
            jax.ShapeDtypeStruct((images, channels), F32),
        ],
        scratch_shapes=[pltpu.VMEM((16 + (height + 2) * 16 * images, LANES), F32)],
        compiler_params=params(),
        cost_estimate=cost(2 * 9 * count * LANES * channels, 8 * count * channels),
        name="conv_forward",
    )(rows, weight)


def conv_backward_body(
    grad_ref, gate_ref, squeeze_ref, conv_ref, w_ref, out_ref, rows_ref, pad_ref, *, height, width, images
):
    count = grad_ref.shape[0]
    gate = per_row(gate_ref[...], count)
    squeeze = per_row(squeeze_ref[...], count)
    act_grad = grad_ref[...] * gate + squeeze / (height * width)
    rows_ref[...] = act_grad * silu_grad(conv_ref[...])
    convolve(rows_ref, pad_ref, w_ref, height, width, images, True)
    out_ref[...] = rows_ref[...].astype(BF16)


def conv_backward(scaled_grad, gating, squeeze_grad, convolved, weight, shape):
    images, height, width, channels = shape
    count = convolved.shape[0]
    block = pl.BlockSpec((count, LANES), lambda i: (0, i))
    small = pl.BlockSpec((images, LANES), lambda i: (0, i))
    return pl.pallas_call(
        functools.partial(conv_backward_body, height=height, width=width, images=images),
        grid=(channels // LANES,),
        in_specs=[
            block,
            small,
            small,
            block,
            pl.BlockSpec((3, 3, weight.shape[2], LANES), lambda i: (0, 0, 0, i)),
        ],
        out_specs=block,
        out_shape=jax.ShapeDtypeStruct((count, channels), BF16),
        scratch_shapes=[
            pltpu.VMEM((count, LANES), F32),
            pltpu.VMEM((16 + (height + 2) * 16 * images, LANES), F32),
        ],
        compiler_params=params(),
        cost_estimate=cost(2 * 9 * count * LANES * channels, 12 * count * channels),
        name="conv_backward",
    )(scaled_grad, gating, squeeze_grad, convolved, weight)


def project_body(order_ref, act_ref, gate_ref, w_ref, scaled_ref, *out_refs):
    step = pl.program_id(0)

    @pl.when(step == 0)
    def _():
        gate = per_row(gate_ref[...], act_ref.shape[0])
        scaled_ref[...] = (act_ref[...].astype(F32) * gate).astype(BF16)

    part = jnp.dot(scaled_ref[...], w_ref[...], preferred_element_type=F32).astype(BF16)
    for k, out_ref in enumerate(out_refs):

        @pl.when(step == k)
        def _():
            out_ref[...] = part


def project(order, act, gating, weight):
    count, channels = act.shape
    parts = weight.shape[1] // channels
    whole = pl.BlockSpec((count, channels), lambda i, order: (0, 0))
    array = jax.ShapeDtypeStruct((count, channels), BF16)
    return pl.pallas_call(
        project_body,
        grid_spec=pltpu.PrefetchScalarGridSpec(
            num_scalar_prefetch=1,
            grid=(parts,),
            in_specs=[
                whole,
                pl.BlockSpec(gating.shape, lambda i, order: (0, 0)),
                pl.BlockSpec((channels, channels), lambda i, order: (0, order[i])),
            ],
            out_specs=[whole] * (parts + 1),
        ),
        out_shape=[array] * (parts + 1),
        compiler_params=params(),
        cost_estimate=cost(2 * count * weight.size, 2 * weight.size + 12 * count * channels),
        name="project",
    )(order, act, gating, weight)


def input_grad_body(order_ref, *refs, pieces, last, images):
    piece_refs, refs = refs[:pieces], refs[pieces:]
    w_ref, refs = refs[0], refs[1:]
    step = pl.program_id(0)
    if last:
        start_ref, act_ref, out_ref, gate_ref = refs
    else:
        (out_ref,) = refs

    for k, piece_ref in enumerate(piece_refs):

        @pl.when(step == k)
        def _():
            part = lax.dot_general(
                piece_ref[...], w_ref[...], (((1,), (1,)), ((), ())), preferred_element_type=F32
            )
            if k > 0:
                part = out_ref[...] + part
            elif last:
                part = start_ref[...] + part
            out_ref[...] = part
            if last and k == pieces - 1:
                gate_ref[...] = image_sum(part * act_ref[...].astype(F32), images)


def input_grad(order, pieces, weight, images, start=None, act=None):
    count, channels = pieces[0].shape
    last = start is not None
    whole = pl.BlockSpec((count, channels), lambda i, order: (0, 0))
    out_shape = [jax.ShapeDtypeStruct((count, channels), F32)]
    out_specs = [whole]
    operands = list(pieces) + [weight]
    in_specs = [whole] * len(pieces) + [
        pl.BlockSpec((channels, channels), lambda i, order: (0, order[i]))
    ]
    if last:
        operands += [start, act]
        in_specs += [whole, whole]
        out_shape.append(jax.ShapeDtypeStruct((images, channels), F32))
        out_specs.append(pl.BlockSpec((images, channels), lambda i, order: (0, 0)))
    return pl.pallas_call(
        functools.partial(input_grad_body, pieces=len(pieces), last=last, images=images),
        grid_spec=pltpu.PrefetchScalarGridSpec(
            num_scalar_prefetch=1, grid=(len(pieces),), in_specs=in_specs, out_specs=out_specs
        ),
        out_shape=out_shape,
        compiler_params=params(),
        cost_estimate=cost(
            2 * len(pieces) * count * channels * channels,
            len(pieces) * 2 * channels * channels + 8 * count * channels,
        ),
        name="input_grad_last" if last else "input_grad",
    )(order, *operands)


def weight_grad_body(place_ref, own_ref, other_ref, *refs, pieces):
    mine, theirs = refs[:pieces], refs[pieces : 2 * pieces]
    x_send, x_keep, y_send, y_keep = refs[2 * pieces :]
    half = own_ref.shape[1] // 2
    lanes = (((0,), (0,)), ((), ()))
    for k in range(pieces):
        total = lax.dot_general(own_ref[...], mine[k][...], lanes, preferred_element_type=F32)
        total += lax.dot_general(other_ref[...], theirs[k][...], lanes, preferred_element_type=F32)
        total = total.astype(BF16)
        block = place_ref[k]
        to_x, to_y = block % 2, block // 2

        @pl.when(to_x != place_ref[pieces])
        def _():
            x_send[to_y] = total[:half]

        @pl.when(to_x == place_ref[pieces])
        def _():
            x_keep[to_y] = total[:half]

        @pl.when(to_y != place_ref[pieces + 1])
        def _():
            y_send[to_x] = total[half:]

        @pl.when(to_y == place_ref[pieces + 1])
        def _():
            y_keep[to_x] = total[half:]


def weight_grad(place, own, other, mine, theirs):
    channels, columns = own.shape[1], mine[0].shape[1]
    array = jax.ShapeDtypeStruct((2, channels // 2, columns), BF16)
    vmem = pl.BlockSpec(memory_space=pltpu.VMEM)
    pieces = len(mine)
    return pl.pallas_call(
        functools.partial(weight_grad_body, pieces=pieces),
        in_specs=[pl.BlockSpec(memory_space=pltpu.SMEM)] + [vmem] * (2 + 2 * pieces),
        out_specs=[vmem] * 4,
        out_shape=[array] * 4,
        compiler_params=params(),
        cost_estimate=cost(
            4 * pieces * own.shape[0] * channels * columns, 4 * pieces * channels * columns
        ),
        name="weight_grad",
    )(place, own, other, *mine, *theirs)


OUTER = [(0, 1), (1, 0), (2, 3), (3, 2)]
INWARD = [(0, 1), (3, 2)]
OUTWARD = [(1, 0), (2, 3)]
MIDDLE = [(1, 2), (2, 1)]
CROSS = [(0, 3), (3, 0), (1, 2), (2, 1)]


def along_chan(array, pairs):
    return lax.ppermute(array, "chan", pairs)


def along_dp(array, bit):
    return lax.ppermute(array, "dp", [(i, i ^ bit) for i in range(8)])


def small_sum(values):
    values = values + along_chan(values, OUTER)
    return values + along_chan(values, CROSS)


def on_line(hidden, conv_weight, se_down, se_up, proj_weight, grad_out):
    shape = hidden.shape
    images = shape[0]
    z, place = lax.axis_index("chan"), lax.axis_index("dp")
    at_end = (z == 0) | (z == 3)
    core, x, y = place % 2, (place // 2) % 2, place // 4
    order = jnp.array([[0, 1, 2, 3], [1, 0, 2, 3], [2, 3, 1, 0], [3, 2, 1, 0]], jnp.int32)[z]

    own = to_rows(grad_out)
    outer = along_chan(own, OUTER)
    middle = along_chan(own, MIDDLE)

    convolved, act, squeezed = conv_forward(to_rows(hidden), conv_weight, shape)
    excite_pre = small_sum(jnp.dot(squeezed, se_down.astype(F32), precision=HIGHEST))
    gating = jax.nn.sigmoid(jnp.dot(jax.nn.silu(excite_pre), se_up.astype(F32), precision=HIGHEST))

    third = along_chan(middle, OUTWARD)
    far = along_chan(outer, MIDDLE)
    fourth = along_chan(far, OUTWARD)
    third = jnp.where(at_end, third, middle)
    fourth = jnp.where(at_end, fourth, far)
    pieces = [own, outer, third, fourth]

    scaled, p_own, p_outer, p_third, p_fourth = project(order, act, gating, proj_weight)

    def add(a, b):
        return (a.astype(F32) + b.astype(F32)).astype(BF16)

    to_far = add(p_fourth, along_chan(p_fourth, INWARD))
    to_mid = add(p_third, along_chan(p_third, INWARD))
    u_outer = add(p_outer, along_chan(to_far, MIDDLE))
    u_own = add(p_own, along_chan(to_mid, MIDDLE))
    came = along_chan(jnp.where(at_end, p_outer, u_outer), OUTER)
    projected = from_rows(add(jnp.where(at_end, p_own, u_own), came), shape)

    half = shape[3] // 2
    other = along_dp(scaled, 1)
    mine = [lax.dynamic_slice_in_dim(piece, core * half, half, 1) for piece in pieces]
    give = [lax.dynamic_slice_in_dim(piece, (1 - core) * half, half, 1) for piece in pieces]
    theirs = [along_dp(piece, 1) for piece in give]
    slots = jnp.concatenate([order, jnp.stack([x, y]).astype(jnp.int32)])
    x_send, x_keep, y_send, y_keep = weight_grad(slots, scaled, other, mine, theirs)
    x_sum = x_keep.astype(F32) + along_dp(x_send, 2).astype(F32)
    y_sum = y_keep.astype(F32) + along_dp(y_send, 4).astype(F32)

    def pick(array, index):
        return lax.dynamic_index_in_dim(array, index, 0, keepdims=False)

    top = pick(x_sum, y) + along_dp(pick(x_sum, 1 - y).astype(BF16), 4).astype(F32)
    bottom = pick(y_sum, x) + along_dp(pick(y_sum, 1 - x).astype(BF16), 2).astype(F32)
    grad_proj = jnp.concatenate([top, bottom], axis=0)

    (begun,) = input_grad(order[:3], pieces[:3], proj_weight, images)
    scaled_grad, gate_grad = input_grad(order[3:], pieces[3:], proj_weight, images, begun, act)
    pre_grad = gate_grad * gating * (1.0 - gating)
    excite_sum = small_sum(jnp.dot(pre_grad, se_up.astype(F32).T, precision=HIGHEST))
    excite_grad = excite_sum * silu_grad(excite_pre)
    squeeze_grad = jnp.dot(excite_grad, se_down.astype(F32).T, precision=HIGHEST)
    grad_hidden = conv_backward(scaled_grad, gating, squeeze_grad, convolved, conv_weight, shape)
    return (projected, from_rows(grad_hidden, shape), grad_proj)


def on_any(hidden, conv_weight, se_down, se_up, proj_weight, grad_out):
    shape = hidden.shape
    images = shape[0]
    convolved, act, squeezed = conv_forward(to_rows(hidden), conv_weight, shape)
    excite_pre = lax.psum(jnp.dot(squeezed, se_down.astype(F32), precision=HIGHEST), "chan")
    gating = jax.nn.sigmoid(jnp.dot(jax.nn.silu(excite_pre), se_up.astype(F32), precision=HIGHEST))
    count = act.shape[0]
    act_float = act.astype(F32)
    scaled = (act_float * per_row(gating, count)).astype(BF16)
    terms = jnp.dot(scaled, proj_weight, preferred_element_type=F32).astype(BF16)
    projected = lax.psum_scatter(terms, "chan", scatter_dimension=1, tiled=True)
    pieces = lax.all_gather(to_rows(grad_out), "chan", axis=1, tiled=True)
    scaled_grad = lax.dot_general(
        pieces, proj_weight, (((1,), (1,)), ((), ())), preferred_element_type=F32
    )
    terms = lax.dot_general(scaled, pieces, (((0,), (0,)), ((), ())), preferred_element_type=F32)
    grad_proj = lax.psum_scatter(terms, "dp", scatter_dimension=1, tiled=True)
    gate_grad = image_sum(scaled_grad * act_float, images)
    pre_grad = gate_grad * gating * (1.0 - gating)
    excite_sum = lax.psum(jnp.dot(pre_grad, se_up.astype(F32).T, precision=HIGHEST), "chan")
    excite_grad = excite_sum * silu_grad(excite_pre)
    squeeze_grad = jnp.dot(excite_grad, se_down.astype(F32).T, precision=HIGHEST)
    grad_hidden = conv_backward(scaled_grad, gating, squeeze_grad, convolved, conv_weight, shape)
    return (from_rows(projected, shape), from_rows(grad_hidden, shape), grad_proj)


def solution(mesh):
    in_specs = (
        P("dp", None, None, "chan"),
        P(None, None, None, "chan"),
        P("chan", None),
        P(None, "chan"),
        P("chan", None),
        P("dp", None, None, "chan"),
    )
    out_specs = (P("dp", None, None, "chan"), P("dp", None, None, "chan"), P("chan", "dp"))
    on_device = on_line if (mesh.shape["dp"], mesh.shape["chan"]) == (8, 4) else on_any
    return jax.shard_map(
        on_device, mesh=mesh, in_specs=in_specs, out_specs=out_specs, check_vma=False
    )
```

```python
import functools

import jax
import jax.numpy as jnp
from jax import lax
from jax.experimental import pallas as pl
from jax.experimental.pallas import tpu as pltpu
from jax.sharding import PartitionSpec as P

LANES = 256
VMEM = 20 * 1024 * 1024
F32 = jnp.float32
BF16 = jnp.bfloat16
HIGHEST = lax.Precision.HIGHEST


def params(**more):
    return pltpu.CompilerParams(vmem_limit_bytes=VMEM, **more)


SCALE = 0.3


def cost(micros):
    return pl.CostEstimate(
        flops=int(micros * SCALE * 1.15e9), bytes_accessed=1, transcendentals=0
    )


def exact_dot(values, weight, dims):
    high = values.astype(BF16).astype(F32)
    rest = values - high
    middle = rest.astype(BF16).astype(F32)
    count = values.shape[0]
    terms = [high, middle, rest - middle, jnp.zeros_like(values)]
    stacked = jnp.concatenate(terms, axis=0).astype(BF16)
    out = lax.dot_general(stacked, weight, (dims, ((), ())), preferred_element_type=F32)
    return out[:count] + out[count : 2 * count] + out[2 * count : 3 * count]


def silu_grad(values):
    logistic = jax.nn.sigmoid(values)
    return logistic * (1.0 + values * (1.0 - logistic))


def to_rows(images):
    return jnp.transpose(images, (1, 2, 0, 3)).reshape(-1, images.shape[3])


def from_rows(rows, shape):
    count, height, width, channels = shape
    return jnp.transpose(rows.reshape(height, width, count, channels), (1 + 1, 0, 1, 3))


def per_row(values, rows):
    tiled = jnp.concatenate([values] * (8 // values.shape[0]), axis=0)
    return jnp.broadcast_to(tiled[None], (rows // 8, 8, values.shape[1])).reshape(rows, -1)


def image_sum(values, images):
    folded = values.reshape(-1, 8, values.shape[1]).sum(axis=0)
    total = folded[:images]
    for start in range(images, 8, images):
        total = total + folded[start : start + images]
    return total


def convolve(rows_ref, pad_ref, weight_ref, height, width, images, turn):
    line, unit = width * images, 16 * images
    group = weight_ref.shape[2]
    pad_ref[...] = jnp.zeros_like(pad_ref)
    for h in range(height):
        pad_ref[pl.ds(8 + (h + 1) * unit + images, line), :] = rows_ref[pl.ds(h * line, line), :]
    row_group = lax.broadcasted_iota(jnp.int32, (LANES, LANES), 0) // group
    col_group = lax.broadcasted_iota(jnp.int32, (LANES, LANES), 1) // group
    mask = (row_group == col_group).astype(F32).astype(BF16)
    total = None
    for dw in range(3):
        shifted = pad_ref[pl.ds(8 + images * (dw - 1), (height + 2) * unit), :].astype(BF16)
        for dh in range(3):
            tap = weight_ref[2 - dh, 2 - dw] if turn else weight_ref[dh, dw]
            dense = jnp.concatenate([tap] * (LANES // group), axis=0) * mask
            part = lax.dot_general(
                shifted[dh * unit : (dh + height) * unit],
                dense,
                (((1,), (1 if turn else 0,)), ((), ())),
                preferred_element_type=F32,
            )
            total = part if total is None else total + part
    pad_ref[pl.ds(0, height * unit), :] = total
    for h in range(height):
        rows_ref[pl.ds(h * line, line), :] = pad_ref[pl.ds(h * unit + images, line), :]


HBM = pl.BlockSpec(memory_space=pltpu.HBM)
HERE = pl.BlockSpec(memory_space=pltpu.VMEM)


def lanes_of(i):
    return pl.ds(i * LANES, LANES)


def fetch(source, target, sem):
    copy = pltpu.make_async_copy(source, target, sem)
    copy.start()
    return copy


def conv_forward_body(
    x_hbm,
    w_hbm,
    down_hbm,
    conv_ref,
    act_ref,
    pre_ref,
    x_buf,
    w_buf,
    down_buf,
    rows_ref,
    pad_ref,
    sems,
    *,
    height,
    width,
    images,
):
    blocks = conv_ref.shape[1] // LANES
    copies = [fetch(x_hbm, x_buf, sems.at[0])]
    for i in range(blocks):
        part = w_hbm.at[:, :, :, lanes_of(i)]
        copies.append(fetch(part, w_buf.at[i], sems.at[2 + i]))
    down_copy = fetch(down_hbm, down_buf, sems.at[1])
    copies[0].wait()
    means = []
    for i in range(blocks):
        rows_ref[...] = x_buf[:, lanes_of(i)].astype(F32)
        copies[1 + i].wait()
        convolve(rows_ref, pad_ref, w_buf.at[i], height, width, images, False)
        conv = rows_ref[...]
        conv_ref[:, lanes_of(i)] = conv
        act = (conv * jax.nn.sigmoid(conv)).astype(BF16)
        act_ref[:, lanes_of(i)] = act
        means.append(image_sum(act.astype(F32), images) / (height * width))
    down_copy.wait()
    pre_ref[...] = exact_dot(jnp.concatenate(means, axis=1), down_buf[...], ((1,), (0,)))


def conv_forward(rows, weight, down, shape):
    images, height, width, channels = shape
    count, inner = rows.shape[0], down.shape[1]
    blocks = channels // LANES
    return pl.pallas_call(
        functools.partial(conv_forward_body, height=height, width=width, images=images),
        in_specs=[HBM, HBM, HBM],
        out_specs=[HERE, HERE, HERE],
        out_shape=[
            jax.ShapeDtypeStruct((count, channels), F32),
            jax.ShapeDtypeStruct((count, channels), BF16),
            jax.ShapeDtypeStruct((images, inner), F32),
        ],
        scratch_shapes=[
            pltpu.VMEM((count, channels), BF16),
            pltpu.VMEM((blocks, 3, 3, weight.shape[2], LANES), BF16),
            pltpu.VMEM(down.shape, BF16),
            pltpu.VMEM((count, LANES), F32),
            pltpu.VMEM((16 + (height + 2) * 16 * images, LANES), F32),
            pltpu.SemaphoreType.DMA((2 + blocks,)),
        ],
        compiler_params=params(),
        cost_estimate=cost(3),
        name="conv_forward",
    )(rows, weight, down)


def conv_backward_body(
    grad_ref,
    gate_ref,
    sum_ref,
    pre_ref,
    down_hbm,
    conv_ref,
    w_hbm,
    out_hbm,
    down_buf,
    w_buf,
    out_buf,
    rows_ref,
    pad_ref,
    sems,
    *,
    height,
    width,
    images,
):
    count, channels = grad_ref.shape
    blocks = channels // LANES
    down_copy = fetch(down_hbm, down_buf, sems.at[0])
    copies = []
    for i in range(blocks):
        part = w_hbm.at[:, :, :, lanes_of(i)]
        copies.append(fetch(part, w_buf.at[i], sems.at[1 + i]))
    excite_grad = sum_ref[...] * silu_grad(pre_ref[...])
    down_copy.wait()
    squeeze_grad = exact_dot(excite_grad, down_buf[...], ((1,), (1,))) / (height * width)
    outs = []
    for i in range(blocks):
        gate = per_row(gate_ref[:, lanes_of(i)], count)
        squeeze = per_row(squeeze_grad[:, i * LANES : (i + 1) * LANES], count)
        act_grad = grad_ref[:, lanes_of(i)] * gate + squeeze
        rows_ref[...] = act_grad * silu_grad(conv_ref[:, lanes_of(i)])
        copies[i].wait()
        convolve(rows_ref, pad_ref, w_buf.at[i], height, width, images, True)
        out_buf[:, lanes_of(i)] = rows_ref[...].astype(BF16)
        target = out_hbm.at[:, lanes_of(i)]
        outs.append(fetch(out_buf.at[:, lanes_of(i)], target, sems.at[1 + blocks + i]))
    for out in outs:
        out.wait()


def conv_backward(scaled_grad, gating, excite_sum, excite_pre, down, convolved, weight, shape):
    images, height, width, channels = shape
    count = convolved.shape[0]
    blocks = channels // LANES
    return pl.pallas_call(
        functools.partial(conv_backward_body, height=height, width=width, images=images),
        in_specs=[HERE, HERE, HERE, HERE, HBM, HERE, HBM],
        out_specs=HBM,
        out_shape=jax.ShapeDtypeStruct((count, channels), BF16),
        scratch_shapes=[
            pltpu.VMEM(down.shape, BF16),
            pltpu.VMEM((blocks, 3, 3, weight.shape[2], LANES), BF16),
            pltpu.VMEM((count, channels), BF16),
            pltpu.VMEM((count, LANES), F32),
            pltpu.VMEM((16 + (height + 2) * 16 * images, LANES), F32),
            pltpu.SemaphoreType.DMA((1 + 2 * blocks,)),
        ],
        compiler_params=params(),
        cost_estimate=cost(3),
        name="conv_backward",
    )(scaled_grad, gating, excite_sum, excite_pre, down, convolved, weight)


def block_of(weight_ref, block, width):
    return weight_ref.at[:, pl.ds(pl.multiple_of(block * width, width), width)]


def scale_body(
    order_ref,
    act_ref,
    pre_ref,
    up_hbm,
    w_hbm,
    middle_hbm,
    gate_ref,
    scaled_hbm,
    far_hbm,
    send_hbm,
    up_buf,
    w_buf,
    middle_buf,
    scaled_buf,
    far_buf,
    sems,
):
    channels = act_ref.shape[1]
    up_copy = fetch(up_hbm, up_buf, sems.at[0])
    w_copy = fetch(block_of(w_hbm, order_ref[3], channels), w_buf, sems.at[1])
    middle_copy = fetch(middle_hbm, middle_buf, sems.at[2])
    pre = pre_ref[...]
    excited = pre * jax.nn.sigmoid(pre)
    up_copy.wait()
    gate_ref[...] = jax.nn.sigmoid(exact_dot(excited, up_buf[...], ((1,), (0,))))
    gate = per_row(gate_ref[...], act_ref.shape[0])
    scaled_buf[...] = (act_ref[...].astype(F32) * gate).astype(BF16)
    sent = [fetch(scaled_buf, scaled_hbm, sems.at[3])]
    w_copy.wait()
    far = jnp.dot(scaled_buf[...], w_buf[...], preferred_element_type=F32).astype(BF16)
    far_buf[...] = far
    sent.append(fetch(far_buf, far_hbm, sems.at[4]))
    middle_copy.wait()

    @pl.when(order_ref[4] == 1)
    def _():
        middle_buf[...] = far

    sent.append(fetch(middle_buf, send_hbm, sems.at[5]))
    for copy in sent:
        copy.wait()


def scale(order, act, excite_pre, up, weight, middle):
    count, channels = act.shape
    gates = (excite_pre.shape[0], channels)
    array = jax.ShapeDtypeStruct((count, channels), BF16)
    return pl.pallas_call(
        scale_body,
        in_specs=[pl.BlockSpec(memory_space=pltpu.SMEM), HERE, HERE, HBM, HBM, HBM],
        out_specs=[HERE, HBM, HBM, HBM],
        out_shape=[jax.ShapeDtypeStruct(gates, F32)] + [array] * 3,
        scratch_shapes=[
            pltpu.VMEM(up.shape, BF16),
            pltpu.VMEM((channels, channels), BF16),
            pltpu.VMEM((count, channels), BF16),
            pltpu.VMEM((count, channels), BF16),
            pltpu.VMEM((count, channels), BF16),
            pltpu.SemaphoreType.DMA((6,)),
        ],
        compiler_params=params(),
        cost_estimate=cost(3),
        name="scale",
    )(order, act, excite_pre, up, weight, middle)


def project_body(order_ref, scaled_hbm, w_hbm, *refs, parts):
    outs, (scaled_buf, w_buf, out_buf, sems) = refs[:parts], refs[parts:]
    channels = scaled_buf.shape[1]
    scaled_copy = fetch(scaled_hbm, scaled_buf, sems.at[0])
    copies = [
        fetch(block_of(w_hbm, order_ref[k], channels), w_buf.at[k], sems.at[1 + k])
        for k in range(parts)
    ]
    scaled_copy.wait()
    sent = []
    for k in range(parts):
        copies[k].wait()
        part = jnp.dot(scaled_buf[...], w_buf[k], preferred_element_type=F32)
        out_buf[k] = part.astype(BF16)
        sent.append(fetch(out_buf.at[k], outs[k], sems.at[1 + parts + k]))
    for copy in sent:
        copy.wait()


def project(order, parts, scaled, weight):
    count, channels = scaled.shape
    array = jax.ShapeDtypeStruct((count, channels), BF16)
    return pl.pallas_call(
        functools.partial(project_body, parts=parts),
        in_specs=[pl.BlockSpec(memory_space=pltpu.SMEM), HBM, HBM],
        out_specs=[HBM] * parts,
        out_shape=[array] * parts,
        scratch_shapes=[
            pltpu.VMEM((count, channels), BF16),
            pltpu.VMEM((parts, channels, channels), BF16),
            pltpu.VMEM((parts, count, channels), BF16),
            pltpu.SemaphoreType.DMA((1 + 2 * parts,)),
        ],
        compiler_params=params(),
        cost_estimate=cost(3),
        name="project",
    )(order, scaled, weight)


def second_body(end_ref, came, middle, far, p_fourth, p_third, third, to_far, send):
    at_end = end_ref[0] == 1
    to_far[...] = (p_fourth[...].astype(F32) + came[...].astype(F32)).astype(BF16)

    @pl.when(at_end)
    def _():
        third[...] = came[...]
        send[...] = p_third[...]

    @pl.when(jnp.logical_not(at_end))
    def _():
        third[...] = middle[...]
        send[...] = far[...]


def third_body(end_ref, came, crossed, far, p_outer, p_third, fourth, to_mid, send):
    at_end = end_ref[0] == 1
    to_mid[...] = (p_third[...].astype(F32) + came[...].astype(F32)).astype(BF16)

    @pl.when(at_end)
    def _():
        fourth[...] = came[...]
        send[...] = p_outer[...]

    @pl.when(jnp.logical_not(at_end))
    def _():
        fourth[...] = far[...]
        send[...] = (p_outer[...].astype(F32) + crossed[...].astype(F32)).astype(BF16)


def between(body, at_end, *arrays):
    shape = arrays[0].shape
    block = pl.BlockSpec(shape, lambda i: (0, 0))
    return pl.pallas_call(
        body,
        grid=(1,),
        in_specs=[pl.BlockSpec(memory_space=pltpu.SMEM)] + [block] * 5,
        out_specs=[block] * 3,
        out_shape=[jax.ShapeDtypeStruct(shape, BF16)] * 3,
        compiler_params=params(),
        cost_estimate=cost(2),
        name="between",
    )(at_end, *arrays)


def input_grad_body(order_ref, *refs, pieces, started, last, images):
    piece_refs, w_hbm, refs = refs[:pieces], refs[pieces], refs[pieces + 1 :]
    if started:
        start_ref, refs = refs[0], refs[1:]
    if last:
        act_ref, gate_ref, up_hbm, out_ref, excite_ref, piece_buf, w_buf, sems, up_buf = refs
    else:
        out_ref, piece_buf, w_buf, sems = refs
    width = out_ref.shape[1]
    copies = []
    for k, piece_ref in enumerate(piece_refs):
        block = block_of(w_hbm, order_ref[k], width)
        copies.append(
            (
                fetch(piece_ref, piece_buf.at[k], sems.at[2 * k]),
                fetch(block, w_buf.at[k], sems.at[2 * k + 1]),
            )
        )
    if last:
        up_copy = fetch(up_hbm, up_buf, sems.at[2 * pieces])
    for k in range(pieces):
        for copy in copies[k]:
            copy.wait()
        part = lax.dot_general(
            piece_buf[k], w_buf[k], (((1,), (1,)), ((), ())), preferred_element_type=F32
        )
        if k > 0:
            part = out_ref[...] + part
        elif started:
            part = start_ref[...] + part
        out_ref[...] = part
    if last:
        gating = gate_ref[...]
        gate_grad = image_sum(out_ref[...] * act_ref[...].astype(F32), images)
        pre_grad = gate_grad * gating * (1.0 - gating)
        up_copy.wait()
        excite_ref[...] = exact_dot(pre_grad, up_buf[...], ((1,), (1,)))


def input_grad(order, pieces, weight, images, start=None, act=None, gating=None, up=None):
    count, channels = pieces[0].shape
    started, last = start is not None, act is not None
    operands = list(pieces) + [weight]
    in_specs = [pl.BlockSpec(memory_space=pltpu.SMEM)] + [HBM] * (len(pieces) + 1)
    out_shape = [jax.ShapeDtypeStruct((count, channels), F32)]
    scratch = [
        pltpu.VMEM((len(pieces), count, channels), BF16),
        pltpu.VMEM((len(pieces), channels, channels), BF16),
        pltpu.SemaphoreType.DMA((2 * len(pieces) + 1,)),
    ]
    if started:
        operands.append(start)
        in_specs.append(HERE)
    if last:
        operands += [act, gating, up]
        in_specs += [HERE, HERE, HBM]
        out_shape.append(jax.ShapeDtypeStruct((images, up.shape[0]), F32))
        scratch.append(pltpu.VMEM(up.shape, BF16))
    return pl.pallas_call(
        functools.partial(
            input_grad_body, pieces=len(pieces), started=started, last=last, images=images
        ),
        in_specs=in_specs,
        out_specs=[HERE] * len(out_shape),
        out_shape=out_shape,
        scratch_shapes=scratch,
        compiler_params=params(),
        cost_estimate=cost(len(pieces)),
        name="input_grad_last" if last else "input_grad",
    )(order, *operands)


def place_block(total, block, x, y, x_send, x_keep, y_send, y_keep, store):
    half = total.shape[0] // 2
    to_x, to_y = block % 2, block // 2

    @pl.when(to_x != x)
    def _():
        store(x_send, to_y, total[:half])

    @pl.when(to_x == x)
    def _():
        store(x_keep, to_y, total[:half])

    @pl.when(to_y != y)
    def _():
        store(y_send, to_x, total[half:])

    @pl.when(to_y == y)
    def _():
        store(y_keep, to_x, total[half:])


def put(ref, index, values):
    ref[index] = values


def weight_grad_body(place_ref, own_ref, other_ref, *refs, pieces):
    mine, theirs, outs = refs[:pieces], refs[pieces : 2 * pieces], refs[2 * pieces :]
    x, y = place_ref[pieces], place_ref[pieces + 1]
    own, other = own_ref[...].T, other_ref[...].T
    for k in range(pieces):
        total = jnp.dot(own, mine[k][...], preferred_element_type=F32)
        total += jnp.dot(other, theirs[k][...], preferred_element_type=F32)
        place_block(total.astype(BF16), place_ref[k], x, y, *outs, put)


def weight_grad_more_body(place_ref, own_ref, other_ref, mine, theirs, *refs):
    outs = refs[4:8]
    buffer, sem = refs[8:]
    x, y = place_ref[1], place_ref[2]
    half = own_ref.shape[1] // 2
    total = jnp.dot(own_ref[...].T, mine[...], preferred_element_type=F32)
    total += jnp.dot(other_ref[...].T, theirs[...], preferred_element_type=F32)
    buffer[0] = total[:half].astype(BF16)
    buffer[1] = total[half:].astype(BF16)
    block = place_ref[0]
    to_x, to_y = block % 2, block // 2

    def move(ref, index, part):
        copy = pltpu.make_async_copy(buffer.at[part], ref.at[index], sem)
        copy.start()
        copy.wait()

    @pl.when(to_x != x)
    def _():
        move(outs[0], to_y, 0)

    @pl.when(to_x == x)
    def _():
        move(outs[1], to_y, 0)

    @pl.when(to_y != y)
    def _():
        move(outs[2], to_x, 1)

    @pl.when(to_y == y)
    def _():
        move(outs[3], to_x, 1)


def weight_grad(place, own, other, mine, theirs, begun=None):
    count, channels = own.shape
    columns = channels // 2
    array = jax.ShapeDtypeStruct((2, channels // 2, columns), BF16)
    pieces = len(mine)
    whole = pl.BlockSpec((count, channels), lambda i, place: (0, 0))
    part = pl.BlockSpec((count, columns), lambda i, place: (0, place[pieces + 2]))
    out = pl.BlockSpec(array.shape, lambda i, place: (0, 0, 0))
    scratch = []
    if begun is not None:
        out = pl.BlockSpec(memory_space=pl.ANY)
        scratch = [pltpu.VMEM(array.shape, BF16), pltpu.SemaphoreType.DMA]
    body = functools.partial(weight_grad_body, pieces=pieces)
    return pl.pallas_call(
        body if begun is None else weight_grad_more_body,
        grid_spec=pltpu.PrefetchScalarGridSpec(
            num_scalar_prefetch=1,
            grid=(1,),
            in_specs=[whole] * 2 + [part] * (2 * pieces) + [out] * len(begun or ()),
            out_specs=[out] * 4,
            scratch_shapes=scratch,
        ),
        out_shape=[array] * 4,
        input_output_aliases={} if begun is None else {5 + k: k for k in range(4)},
        compiler_params=params(),
        cost_estimate=cost(2 * pieces),
        name="weight_grad" if begun is None else "weight_grad_more",
    )(place, own, other, *mine, *theirs, *(begun or ()))


def merge_body(place_ref, x_keep, x_came, y_keep, y_came, top, to_y, bottom, to_x):
    x, y = place_ref[0], place_ref[1]
    top[...] = x_keep[y].astype(F32) + x_came[y].astype(F32)
    to_y[...] = (x_keep[1 - y].astype(F32) + x_came[1 - y].astype(F32)).astype(BF16)
    bottom[...] = y_keep[x].astype(F32) + y_came[x].astype(F32)
    to_x[...] = (y_keep[1 - x].astype(F32) + y_came[1 - x].astype(F32)).astype(BF16)


def merge(place, x_keep, x_came, y_keep, y_came):
    rows, columns = x_keep.shape[1:]
    pair = pl.BlockSpec((2, rows, columns), lambda i, place: (0, 0, 0))
    one = pl.BlockSpec((rows, columns), lambda i, place: (0, 0))
    kept = jax.ShapeDtypeStruct((rows, columns), F32)
    sent = jax.ShapeDtypeStruct((rows, columns), BF16)
    return pl.pallas_call(
        merge_body,
        grid_spec=pltpu.PrefetchScalarGridSpec(
            num_scalar_prefetch=1, grid=(1,), in_specs=[pair] * 4, out_specs=[one] * 4
        ),
        out_shape=[kept, sent, kept, sent],
        compiler_params=params(),
        cost_estimate=cost(2),
        name="merge",
    )(place, x_keep, x_came, y_keep, y_came)


def finish_body(top, top_came, bottom, bottom_came, out):
    rows = top.shape[0]
    out[:rows] = top[...] + top_came[...].astype(F32)
    out[rows:] = bottom[...] + bottom_came[...].astype(F32)


def finish(top, top_came, bottom, bottom_came):
    rows, columns = top.shape
    one = pl.BlockSpec((rows, columns), lambda i: (0, 0))
    return pl.pallas_call(
        finish_body,
        grid=(1,),
        in_specs=[one] * 4,
        out_specs=pl.BlockSpec((2 * rows, columns), lambda i: (0, 0)),
        out_shape=jax.ShapeDtypeStruct((2 * rows, columns), F32),
        compiler_params=params(),
        cost_estimate=cost(2),
        name="finish",
    )(top, top_came, bottom, bottom_came)


def add_body(a, b, out):
    out[...] = (a[...].astype(F32) + b[...].astype(F32)).astype(BF16)


def add(a, b):
    block = pl.BlockSpec(a.shape, lambda i: (0, 0))
    return pl.pallas_call(
        add_body,
        grid=(1,),
        in_specs=[block, block],
        out_specs=block,
        out_shape=jax.ShapeDtypeStruct(a.shape, BF16),
        compiler_params=params(),
        cost_estimate=cost(1),
        name="add",
    )(a, b)


OUTER = [(0, 1), (1, 0), (2, 3), (3, 2)]
INWARD = [(0, 1), (3, 2)]
OUTWARD = [(1, 0), (2, 3)]
MIDDLE = [(1, 2), (2, 1)]
OVER = [(0, 2), (2, 0), (1, 3), (3, 1)]
CROSS = [(0, 3), (3, 0), (1, 2), (2, 1)]


def along_chan(array, pairs):
    return lax.ppermute(array, "chan", pairs)


def along_dp(array, bit):
    return lax.ppermute(array, "dp", [(i, i ^ bit) for i in range(8)])


def small_sum(values):
    near, across, over = (along_chan(values, pairs) for pairs in (OUTER, CROSS, OVER))
    return (values + near) + (across + over)


def after(array, *others):
    return lax.optimization_barrier((array, *others))[0]


def on_line(hidden, conv_weight, se_down, se_up, proj_weight, grad_out):
    shape = hidden.shape
    images = shape[0]
    z, place = lax.axis_index("chan"), lax.axis_index("dp")
    at_end = (z == 0) | (z == 3)
    core, x, y = place % 2, (place // 2) % 2, place // 4
    spot = jnp.stack([x, y, core]).astype(jnp.int32)
    order = jnp.array([[0, 1, 2, 3], [1, 0, 2, 3], [2, 3, 1, 0], [3, 2, 1, 0]], jnp.int32)[z]

    own = to_rows(grad_out)
    outer = along_chan(own, OUTER)
    middle = along_chan(own, MIDDLE)

    convolved, act, terms = conv_forward(to_rows(hidden), conv_weight, se_down, shape)
    excite_pre = small_sum(terms)

    role = jnp.concatenate([order, at_end.astype(jnp.int32)[None]])
    gating, scaled, p_fourth, send = scale(role, act, excite_pre, se_up, proj_weight, middle)
    came = along_chan(send, OUTER)
    far = along_chan(after(outer, send), MIDDLE)
    other = along_dp(scaled, 1)
    theirs = [along_dp(piece, 1) for piece in (own, outer)]
    p_own, p_outer, p_third = project(order[:3], 3, scaled, proj_weight)
    (begun,) = input_grad(order[:2], [after(own, p_own), outer], proj_weight, images)

    came, far = lax.optimization_barrier((came, far, begun))[:2]
    third, to_far, send = between(second_body, role[4:], came, middle, far, p_fourth, p_third)
    came = along_chan(send, OUTER)
    crossed = along_chan(to_far, MIDDLE)
    theirs.append(along_dp(third, 1))
    pieces = [own, outer, third]
    weights = weight_grad(jnp.concatenate([order[:3], spot]), scaled, other, pieces, theirs)
    (begun,) = input_grad(order[2:3], [third], proj_weight, images, begun)

    came, crossed = lax.optimization_barrier((came, crossed, begun, *weights))[:2]
    fourth, to_mid, send = between(third_body, role[4:], came, crossed, far, p_outer, p_third)
    came = along_chan(send, OUTER)
    crossed = along_chan(to_mid, MIDDLE)
    weights = weight_grad(
        jnp.concatenate([order[3:], spot]), scaled, other, [fourth], [along_dp(fourth, 1)], weights
    )
    x_send, x_keep, y_send, y_keep = weights
    x_came, y_came = along_dp(x_send, 2), along_dp(y_send, 4)
    scaled_grad, terms = input_grad(
        order[3:], [after(fourth, *weights)], proj_weight, images, begun, act, gating, se_up
    )

    terms, came, crossed = lax.optimization_barrier((terms, came, crossed))
    excite_sum = small_sum(terms)
    total = p_own.astype(F32) + came.astype(F32)
    total = total + jnp.where(at_end, 0.0, crossed.astype(F32))
    projected = from_rows(total.astype(BF16), shape)

    top, to_y, bottom, to_x = merge(spot, x_keep, x_came, y_keep, y_came)
    excite_sum = after(excite_sum, to_x)
    grad_hidden = conv_backward(
        scaled_grad, gating, excite_sum, excite_pre, se_down, convolved, conv_weight, shape
    )
    grad_proj = finish(top, along_dp(to_y, 4), bottom, along_dp(to_x, 2))
    return (projected, from_rows(grad_hidden, shape), grad_proj)


def on_any(hidden, conv_weight, se_down, se_up, proj_weight, grad_out):
    shape = hidden.shape
    images = shape[0]
    convolved, act, terms = conv_forward(to_rows(hidden), conv_weight, se_down, shape)
    excite_pre = lax.psum(terms, "chan")
    gating = jax.nn.sigmoid(jnp.dot(jax.nn.silu(excite_pre), se_up.astype(F32), precision=HIGHEST))
    count = act.shape[0]
    act_float = act.astype(F32)
    scaled = (act_float * per_row(gating, count)).astype(BF16)
    terms = jnp.dot(scaled, proj_weight, preferred_element_type=F32).astype(BF16)
    projected = lax.psum_scatter(terms, "chan", scatter_dimension=1, tiled=True)
    pieces = lax.all_gather(to_rows(grad_out), "chan", axis=1, tiled=True)
    scaled_grad = lax.dot_general(
        pieces, proj_weight, (((1,), (1,)), ((), ())), preferred_element_type=F32
    )
    terms = lax.dot_general(scaled, pieces, (((0,), (0,)), ((), ())), preferred_element_type=F32)
    grad_proj = lax.psum_scatter(terms, "dp", scatter_dimension=1, tiled=True)
    gate_grad = image_sum(scaled_grad * act_float, images)
    pre_grad = gate_grad * gating * (1.0 - gating)
    excite_sum = lax.psum(jnp.dot(pre_grad, se_up.astype(F32).T, precision=HIGHEST), "chan")
    grad_hidden = conv_backward(
        scaled_grad, gating, excite_sum, excite_pre, se_down, convolved, conv_weight, shape
    )
    return (from_rows(projected, shape), from_rows(grad_hidden, shape), grad_proj)


def solution(mesh):
    in_specs = (
        P("dp", None, None, "chan"),
        P(None, None, None, "chan"),
        P("chan", None),
        P(None, "chan"),
        P("chan", None),
        P("dp", None, None, "chan"),
    )
    out_specs = (P("dp", None, None, "chan"), P("dp", None, None, "chan"), P("chan", "dp"))
    on_device = on_line if (mesh.shape["dp"], mesh.shape["chan"]) == (8, 4) else on_any
    return jax.shard_map(
        on_device, mesh=mesh, in_specs=in_specs, out_specs=out_specs, check_vma=False
    )
```

```python
import functools

import jax
import jax.numpy as jnp
import numpy as np
from jax import lax
from jax.experimental import pallas as pl
from jax.experimental.pallas import tpu as pltpu
from jax.sharding import PartitionSpec as P

LANES = 256
F32 = jnp.float32
BF16 = jnp.bfloat16
HIGHEST = lax.Precision.HIGHEST


def params(mebibytes=20):
    return pltpu.CompilerParams(vmem_limit_bytes=mebibytes * 1024 * 1024)


SCALE = 0.3
CONV_MIB = 62


def cost(micros):
    return pl.CostEstimate(
        flops=int(micros * SCALE * 1.15e9), bytes_accessed=1, transcendentals=0
    )


def exact_dot(values, weight, dims):
    high = values.astype(BF16).astype(F32)
    rest = values - high
    middle = rest.astype(BF16).astype(F32)
    count = values.shape[0]
    terms = [high, middle, rest - middle, jnp.zeros_like(values)]
    stacked = jnp.concatenate(terms, axis=0).astype(BF16)
    out = lax.dot_general(stacked, weight, (dims, ((), ())), preferred_element_type=F32)
    return out[:count] + out[count : 2 * count] + out[2 * count : 3 * count]


def silu_grad(values):
    logistic = jax.nn.sigmoid(values)
    return logistic * (1.0 + values * (1.0 - logistic))


def to_cells(images):
    return jnp.transpose(images, (1, 2, 0, 3))


def from_cells(cells):
    return jnp.transpose(cells, (2, 0, 1, 3))


def as_rows(values):
    return values.reshape(-1, values.shape[-1])


def whole(shape):
    return pl.BlockSpec(shape, lambda *_: (0,) * len(shape))


def per_row(values, rows):
    tiled = jnp.concatenate([values] * (8 // values.shape[0]), axis=0)
    return jnp.broadcast_to(tiled[None], (rows // 8, 8, values.shape[1])).reshape(rows, -1)


def image_sum(values, images):
    folded = values.reshape(-1, 8, values.shape[1]).sum(axis=0)
    total = folded[:images]
    for start in range(images, 8, images):
        total = total + folded[start : start + images]
    return total


def convolve(rows_ref, pad_ref, weight_ref, height, width, images, turn):
    line, unit = width * images, 16 * images
    group = weight_ref.shape[2]
    pad_ref[...] = jnp.zeros_like(pad_ref)
    for h in range(height):
        pad_ref[pl.ds(8 + (h + 1) * unit + images, line), :] = rows_ref[pl.ds(h * line, line), :]
    row_group = lax.broadcasted_iota(jnp.int32, (LANES, LANES), 0) // group
    col_group = lax.broadcasted_iota(jnp.int32, (LANES, LANES), 1) // group
    mask = (row_group == col_group).astype(F32).astype(BF16)
    total = None
    for dw in range(3):
        shifted = pad_ref[pl.ds(8 + images * (dw - 1), (height + 2) * unit), :].astype(BF16)
        for dh in range(3):
            tap = weight_ref[2 - dh, 2 - dw] if turn else weight_ref[dh, dw]
            dense = jnp.concatenate([tap] * (LANES // group), axis=0) * mask
            part = lax.dot_general(
                shifted[dh * unit : (dh + height) * unit],
                dense,
                (((1,), (1 if turn else 0,)), ((), ())),
                preferred_element_type=F32,
            )
            total = part if total is None else total + part
    pad_ref[pl.ds(0, height * unit), :] = total
    for h in range(height):
        rows_ref[pl.ds(h * line, line), :] = pad_ref[pl.ds(h * unit + images, line), :]


HBM = pl.BlockSpec(memory_space=pltpu.HBM)
HERE = pl.BlockSpec(memory_space=pltpu.VMEM)


def lanes_of(i):
    return pl.ds(i * LANES, LANES)


def fetch(source, target, sem):
    copy = pltpu.make_async_copy(source, target, sem)
    copy.start()
    return copy


def conv_forward_body(
    x_hbm,
    w_hbm,
    down_hbm,
    *refs,
    height,
    width,
    images,
):
    conv_hbm, act_ref, pre_ref, x_buf, w_buf, down_buf, conv_buf, rows_ref, pad_ref, sems = refs
    blocks = act_ref.shape[1] // LANES
    copies = [fetch(x_hbm, x_buf, sems.at[0])]
    for i in range(blocks):
        part = w_hbm.at[:, :, :, lanes_of(i)]
        copies.append(fetch(part, w_buf.at[i], sems.at[2 + i]))
    copies[0].wait()
    means = []
    for i in range(blocks):
        rows_ref[...] = as_rows(x_buf[:, :, :, lanes_of(i)]).astype(F32)
        copies[1 + i].wait()
        if i == 0:
            last = [fetch(down_hbm, down_buf, sems.at[1])]
        convolve(rows_ref, pad_ref, w_buf.at[i], height, width, images, False)
        conv = rows_ref[...]
        conv_buf[i] = conv
        last.append(fetch(conv_buf.at[i], conv_hbm.at[:, lanes_of(i)], sems.at[2 + blocks + i]))
        act = (conv * jax.nn.sigmoid(conv)).astype(BF16)
        act_ref[:, lanes_of(i)] = act
        means.append(image_sum(act.astype(F32), images) / (height * width))
    last[0].wait()
    pre_ref[...] = exact_dot(jnp.concatenate(means, axis=1), down_buf[...], ((1,), (0,)))
    for copy in last[1:]:
        copy.wait()


def conv_forward(cells, weight, down):
    height, width, images, channels = cells.shape
    count, inner = height * width * images, down.shape[1]
    blocks = channels // LANES
    return pl.pallas_call(
        functools.partial(conv_forward_body, height=height, width=width, images=images),
        in_specs=[HBM] * 3,
        out_specs=[HBM, HERE, HERE],
        out_shape=[
            jax.ShapeDtypeStruct((count, channels), F32),
            jax.ShapeDtypeStruct((count, channels), BF16),
            jax.ShapeDtypeStruct((images, inner), F32),
        ],
        scratch_shapes=[
            pltpu.VMEM(cells.shape, BF16),
            pltpu.VMEM((blocks, 3, 3, weight.shape[2], LANES), BF16),
            pltpu.VMEM(down.shape, BF16),
            pltpu.VMEM((blocks, count, LANES), F32),
            pltpu.VMEM((count, LANES), F32),
            pltpu.VMEM((16 + (height + 2) * 16 * images, LANES), F32),
            pltpu.SemaphoreType.DMA((2 + 2 * blocks,)),
        ],
        compiler_params=params(CONV_MIB),
        cost_estimate=cost(3),
        name="conv_forward",
    )(cells, weight, down)


def conv_backward_body(
    grad_ref,
    gate_ref,
    sum_ref,
    pre_ref,
    down_hbm,
    conv_ref,
    w_hbm,
    out_hbm,
    down_buf,
    w_buf,
    out_buf,
    rows_ref,
    pad_ref,
    sems,
    *,
    height,
    width,
    images,
):
    count, channels = grad_ref.shape
    blocks = channels // LANES
    down_copy = fetch(down_hbm, down_buf, sems.at[0])
    copies = []
    for i in range(blocks):
        part = w_hbm.at[:, :, :, lanes_of(i)]
        copies.append(fetch(part, w_buf.at[i], sems.at[1 + i]))
    excite_grad = sum_ref[...] * silu_grad(pre_ref[...])
    down_copy.wait()
    squeeze_grad = exact_dot(excite_grad, down_buf[...], ((1,), (1,))) / (height * width)
    outs = []
    for i in range(blocks):
        gate = per_row(gate_ref[:, lanes_of(i)], count)
        squeeze = per_row(squeeze_grad[:, i * LANES : (i + 1) * LANES], count)
        act_grad = grad_ref[:, lanes_of(i)] * gate + squeeze
        rows_ref[...] = act_grad * silu_grad(conv_ref[:, lanes_of(i)])
        copies[i].wait()
        convolve(rows_ref, pad_ref, w_buf.at[i], height, width, images, True)
        part = rows_ref[...].astype(BF16).reshape(height, width, images, LANES)
        out_buf[:, :, :, lanes_of(i)] = part
        target = out_hbm.at[:, :, :, lanes_of(i)]
        outs.append(fetch(out_buf.at[:, :, :, lanes_of(i)], target, sems.at[1 + blocks + i]))
    for out in outs:
        out.wait()


def conv_backward(scaled_grad, gating, excite_sum, excite_pre, down, convolved, weight, shape):
    height, width, images, channels = shape
    count = convolved.shape[0]
    blocks = channels // LANES
    return pl.pallas_call(
        functools.partial(conv_backward_body, height=height, width=width, images=images),
        in_specs=[HERE, HERE, HERE, HERE, HBM, HERE, HBM],
        out_specs=HBM,
        out_shape=jax.ShapeDtypeStruct(shape, BF16),
        scratch_shapes=[
            pltpu.VMEM(down.shape, BF16),
            pltpu.VMEM((blocks, 3, 3, weight.shape[2], LANES), BF16),
            pltpu.VMEM(shape, BF16),
            pltpu.VMEM((count, LANES), F32),
            pltpu.VMEM((16 + (height + 2) * 16 * images, LANES), F32),
            pltpu.SemaphoreType.DMA((1 + 2 * blocks,)),
        ],
        compiler_params=params(),
        cost_estimate=cost(3),
        name="conv_backward",
    )(scaled_grad, gating, excite_sum, excite_pre, down, convolved, weight)


def block_of(weight_ref, block, width):
    return weight_ref.at[:, pl.ds(pl.multiple_of(block * width, width), width)]


def scale_body(
    role_ref,
    act_ref,
    pre_ref,
    up_ref,
    w_ref,
    middle_hbm,
    gate_ref,
    scaled_hbm,
    far_hbm,
    send_hbm,
    middle_buf,
    send_buf,
    scaled_buf,
    far_buf,
    sems,
):
    middle_copy = fetch(middle_hbm, middle_buf, sems.at[0])
    pre = pre_ref[...]
    excited = pre * jax.nn.sigmoid(pre)
    gate_ref[...] = jax.nn.sigmoid(exact_dot(excited, up_ref[...], ((1,), (0,))))
    gate = per_row(gate_ref[...], act_ref.shape[0])
    scaled_buf[...] = (act_ref[...].astype(F32) * gate).astype(BF16)
    far = jnp.dot(scaled_buf[...], w_ref[...], preferred_element_type=F32).astype(BF16)
    far_buf[...] = far
    middle_copy.wait()

    @pl.when(role_ref[4] == 1)
    def _():
        send_buf[...] = far

    @pl.when(role_ref[4] == 0)
    def _():
        send_buf[...] = as_rows(middle_buf[...])

    sent = [
        fetch(send_buf, send_hbm, sems.at[1]),
        fetch(scaled_buf, scaled_hbm, sems.at[2]),
        fetch(far_buf, far_hbm, sems.at[3]),
    ]
    for copy in sent:
        copy.wait()


def scale(role, act, excite_pre, up, w_far, middle):
    count, channels = act.shape
    gates = (excite_pre.shape[0], channels)
    array = jax.ShapeDtypeStruct((count, channels), BF16)
    return pl.pallas_call(
        scale_body,
        in_specs=[pl.BlockSpec(memory_space=pltpu.SMEM), HERE, HERE, HERE, HERE, HBM],
        out_specs=[HERE, HBM, HBM, HBM],
        out_shape=[jax.ShapeDtypeStruct(gates, F32)] + [array] * 3,
        scratch_shapes=[
            pltpu.VMEM(middle.shape, BF16),
            pltpu.VMEM((count, channels), BF16),
            pltpu.VMEM((count, channels), BF16),
            pltpu.VMEM((count, channels), BF16),
            pltpu.SemaphoreType.DMA((4,)),
        ],
        compiler_params=params(),
        cost_estimate=cost(3),
        name="scale",
    )(role, act, excite_pre, up, w_far, middle)


def project_body(order_ref, scaled_hbm, w_hbm, *refs, parts):
    outs, (scaled_buf, w_buf, out_buf, sems) = refs[:parts], refs[parts:]
    channels = scaled_buf.shape[1]
    scaled_copy = fetch(scaled_hbm, scaled_buf, sems.at[0])
    copies = [
        fetch(block_of(w_hbm, order_ref[k], channels), w_buf.at[k], sems.at[1 + k])
        for k in range(parts)
    ]
    scaled_copy.wait()
    sent = []
    for k in range(parts):
        copies[k].wait()
        part = jnp.dot(scaled_buf[...], w_buf[k], preferred_element_type=F32)
        out_buf[k] = part.astype(BF16)
        sent.append(fetch(out_buf.at[k], outs[k], sems.at[1 + parts + k]))
    for copy in sent:
        copy.wait()


def project(order, parts, scaled, weight):
    count, channels = scaled.shape
    array = jax.ShapeDtypeStruct((count, channels), BF16)
    return pl.pallas_call(
        functools.partial(project_body, parts=parts),
        in_specs=[pl.BlockSpec(memory_space=pltpu.SMEM), HBM, HBM],
        out_specs=[HBM] * parts,
        out_shape=[array] * parts,
        scratch_shapes=[
            pltpu.VMEM((count, channels), BF16),
            pltpu.VMEM((parts, channels, channels), BF16),
            pltpu.VMEM((parts, count, channels), BF16),
            pltpu.SemaphoreType.DMA((1 + 2 * parts,)),
        ],
        compiler_params=params(),
        cost_estimate=cost(3),
        name="project",
    )(order, scaled, weight)


def second_body(role_ref, came, held, far, p_fourth, p_third, third, to_far, send):
    at_end = role_ref[4] == 1
    to_far[...] = (p_fourth[...].astype(F32) + came[...].astype(F32)).astype(BF16)

    @pl.when(at_end)
    def _():
        third[...] = came[...]
        send[...] = p_third[...]

    @pl.when(jnp.logical_not(at_end))
    def _():
        third[...] = held[...]
        send[...] = as_rows(far[...])


def third_body(role_ref, came, crossed, held, p_outer, p_third, fourth, to_mid, send, give):
    at_end = role_ref[4] == 1
    to_mid[...] = (p_third[...].astype(F32) + came[...].astype(F32)).astype(BF16)

    @pl.when(at_end)
    def _():
        fourth[...] = came[...]
        send[...] = p_outer[...]

    @pl.when(jnp.logical_not(at_end))
    def _():
        fourth[...] = held[...]
        send[...] = (p_outer[...].astype(F32) + crossed[...].astype(F32)).astype(BF16)

    half = give.shape[1]
    give[...] = fourth[:, pl.ds(pl.multiple_of((1 - role_ref[5]) * half, half), half)]


def fourth_body(role_ref, p_own, came, crossed, total):
    at_end = role_ref[4] == 1
    near = p_own[...].astype(F32) + came[...].astype(F32)

    @pl.when(at_end)
    def _():
        total[...] = near.astype(BF16).reshape(total.shape)

    @pl.when(jnp.logical_not(at_end))
    def _():
        total[...] = (near + crossed[...].astype(F32)).astype(BF16).reshape(total.shape)


def between(body, extents, role, *arrays):
    return pl.pallas_call(
        body,
        grid=(1,),
        in_specs=[pl.BlockSpec(memory_space=pltpu.SMEM)] + [whole(a.shape) for a in arrays],
        out_specs=[whole(extent) for extent in extents],
        out_shape=[jax.ShapeDtypeStruct(extent, BF16) for extent in extents],
        compiler_params=params(),
        cost_estimate=cost(0.02),
        name="between",
    )(role, *arrays)


def input_grad_body(role_ref, *refs, first, pieces, started, last, images):
    piece_refs, w_hbm, refs = refs[:pieces], refs[pieces], refs[pieces + 1 :]
    if started:
        start_ref, refs = refs[0], refs[1:]
    if last:
        act_ref, gate_ref, up_hbm, out_ref, excite_ref, w_buf, sems, up_buf = refs[:8]
    else:
        out_ref, w_buf, sems = refs[:3]
    piece_bufs = refs[-pieces:]
    width = out_ref.shape[1]
    copies = []
    for k, piece_ref in enumerate(piece_refs):
        block = block_of(w_hbm, role_ref[first + k], width)
        copies.append(
            (
                fetch(piece_ref, piece_bufs[k], sems.at[2 * k]),
                fetch(block, w_buf.at[k], sems.at[2 * k + 1]),
            )
        )
    if last:
        up_copy = fetch(up_hbm, up_buf, sems.at[2 * pieces])
    for k in range(pieces):
        for copy in copies[k]:
            copy.wait()
        part = lax.dot_general(
            as_rows(piece_bufs[k][...]),
            w_buf[k],
            (((1,), (1,)), ((), ())),
            preferred_element_type=F32,
        )
        if k > 0:
            part = out_ref[...] + part
        elif started:
            part = start_ref[...] + part
        out_ref[...] = part
    if last:
        gating = gate_ref[...]
        gate_grad = image_sum(out_ref[...] * act_ref[...].astype(F32), images)
        pre_grad = gate_grad * gating * (1.0 - gating)
        up_copy.wait()
        excite_ref[...] = exact_dot(pre_grad, up_buf[...], ((1,), (1,)))


def input_grad(role, first, pieces, weight, start=None, act=None, gating=None, up=None):
    channels = weight.shape[0]
    count = pieces[0].size // channels
    images = 1 if gating is None else gating.shape[0]
    started, last = start is not None, act is not None
    operands = list(pieces) + [weight]
    in_specs = [pl.BlockSpec(memory_space=pltpu.SMEM)] + [HBM] * (len(pieces) + 1)
    out_shape = [jax.ShapeDtypeStruct((count, channels), F32)]
    scratch = [
        pltpu.VMEM((len(pieces), channels, channels), BF16),
        pltpu.SemaphoreType.DMA((2 * len(pieces) + 1,)),
    ]
    if started:
        operands.append(start)
        in_specs.append(HERE)
    if last:
        operands += [act, gating, up]
        in_specs += [HERE, HERE, HBM]
        out_shape.append(jax.ShapeDtypeStruct((images, up.shape[0]), F32))
        scratch.append(pltpu.VMEM(up.shape, BF16))
    scratch += [pltpu.VMEM(piece.shape, BF16) for piece in pieces]
    return pl.pallas_call(
        functools.partial(
            input_grad_body,
            first=first,
            pieces=len(pieces),
            started=started,
            last=last,
            images=images,
        ),
        in_specs=in_specs,
        out_specs=[HERE] * len(out_shape),
        out_shape=out_shape,
        scratch_shapes=scratch,
        compiler_params=params(),
        cost_estimate=cost(10 if last else 0.02),
        name="input_grad_last" if last else "input_grad",
    )(role, *operands)


def place_block(total, block, x, y, x_send, x_keep, y_send, y_keep):
    half = total.shape[0] // 2
    to_x, to_y = block % 2, block // 2

    @pl.when(to_x != x)
    def _():
        x_send[to_y] = total[:half]

    @pl.when(to_x == x)
    def _():
        x_keep[to_y] = total[:half]

    @pl.when(to_y != y)
    def _():
        y_send[to_x] = total[half:]

    @pl.when(to_y == y)
    def _():
        y_keep[to_x] = total[half:]


def weight_grad_body(place_ref, own_ref, other_ref, *refs, pieces):
    mine, theirs, outs = refs[:pieces], refs[pieces : 2 * pieces], refs[2 * pieces :]
    x, y = place_ref[6], place_ref[7]
    own, other = own_ref[...].T, other_ref[...].T
    for k in range(pieces):
        total = jnp.dot(own, as_rows(mine[k][...]), preferred_element_type=F32)
        total += jnp.dot(other, as_rows(theirs[k][...]), preferred_element_type=F32)
        total = total.astype(BF16)
        if pieces > 1:
            place_block(total, place_ref[k], x, y, *outs)
        else:
            half = total.shape[0] // 2
            outs[0][...] = total[:half]
            outs[1][...] = total[half:]
    if pieces > 1:
        place_block(jnp.zeros_like(total), place_ref[pieces], x, y, *outs)


def weight_grad(place, own, other, mine, theirs):
    count, channels = own.shape
    columns = channels // 2
    pieces = len(mine)

    def part(array):
        if array.shape[-1] == columns:
            return whole(array.shape)
        lead = array.shape[:-1]
        return pl.BlockSpec((*lead, columns), lambda i, place: (0,) * len(lead) + (place[5],))

    extent = (channels // 2, columns)
    if pieces > 1:
        extent = (2, *extent)
    outs = 4 if pieces > 1 else 2
    return pl.pallas_call(
        functools.partial(weight_grad_body, pieces=pieces),
        grid_spec=pltpu.PrefetchScalarGridSpec(
            num_scalar_prefetch=1,
            grid=(1,),
            in_specs=[whole(own.shape)] * 2 + [part(piece) for piece in (*mine, *theirs)],
            out_specs=[whole(extent)] * outs,
        ),
        out_shape=[jax.ShapeDtypeStruct(extent, BF16)] * outs,
        compiler_params=params(),
        cost_estimate=cost(2 * pieces if pieces > 1 else 0.02),
        name="weight_grad" if pieces > 1 else "weight_grad_more",
    )(place, own, other, *mine, *theirs)


def merge_body(place_ref, *refs):
    x_keep, x_came, y_keep, y_came, upper, upper_came, lower, lower_came = refs[:8]
    top, to_y, bottom, to_x = refs[8:]
    block, x, y = place_ref[3], place_ref[6], place_ref[7]
    to_bx, to_by = block % 2 == x, block // 2 == y

    def both(a, b):
        return a[...].astype(F32) + b[...].astype(F32)

    for keep, came, index, more, more_came, here, there, stay, leave in (
        (x_keep, x_came, y, upper, upper_came, to_bx, to_by, top, to_y),
        (y_keep, y_came, x, lower, lower_came, to_by, to_bx, bottom, to_x),
    ):
        extra = jnp.where(here, both(more, more_came), 0.0)
        stay[...] = both(keep.at[index], came.at[index]) + jnp.where(there, extra, 0.0)
        rest = both(keep.at[1 - index], came.at[1 - index]) + jnp.where(there, 0.0, extra)
        leave[...] = rest.astype(BF16)


def merge(place, *arrays):
    rows, columns = arrays[0].shape[1:]
    pair = pl.BlockSpec((2, rows, columns), lambda i, place: (0, 0, 0))
    one = pl.BlockSpec((rows, columns), lambda i, place: (0, 0))
    kept = jax.ShapeDtypeStruct((rows, columns), F32)
    sent = jax.ShapeDtypeStruct((rows, columns), BF16)
    return pl.pallas_call(
        merge_body,
        grid_spec=pltpu.PrefetchScalarGridSpec(
            num_scalar_prefetch=1, grid=(1,), in_specs=[pair] * 4 + [one] * 4, out_specs=[one] * 4
        ),
        out_shape=[kept, sent, kept, sent],
        compiler_params=params(),
        cost_estimate=cost(2),
        name="merge",
    )(place, *arrays)


def finish_body(top, top_came, bottom, bottom_came, out):
    rows = top.shape[0]
    out[:rows] = top[...] + top_came[...].astype(F32)
    out[rows:] = bottom[...] + bottom_came[...].astype(F32)


def finish(top, top_came, bottom, bottom_came):
    rows, columns = top.shape
    one = pl.BlockSpec((rows, columns), lambda i: (0, 0))
    return pl.pallas_call(
        finish_body,
        grid=(1,),
        in_specs=[one] * 4,
        out_specs=pl.BlockSpec((2 * rows, columns), lambda i: (0, 0)),
        out_shape=jax.ShapeDtypeStruct((2 * rows, columns), F32),
        compiler_params=params(),
        cost_estimate=cost(2),
        name="finish",
    )(top, top_came, bottom, bottom_came)


OUTER = [(0, 1), (1, 0), (2, 3), (3, 2)]
INWARD = [(0, 1), (3, 2)]
OUTWARD = [(1, 0), (2, 3)]
MIDDLE = [(1, 2), (2, 1)]
OVER = [(0, 2), (2, 0), (1, 3), (3, 1)]
CROSS = [(0, 3), (3, 0), (1, 2), (2, 1)]


def along_chan(array, pairs):
    return lax.ppermute(array, "chan", pairs)


def along_dp(array, bit):
    return lax.ppermute(array, "dp", [(i, i ^ bit) for i in range(8)])


def small_sum(values):
    near, across, over = (along_chan(values, pairs) for pairs in (OUTER, CROSS, OVER))
    return (values + near) + (across + over)


def after(array, *others):
    return lax.optimization_barrier((array, *others))[0]


def places():
    rows = []
    for place in range(8):
        for z in range(4):
            order = [[0, 1, 2, 3], [1, 0, 2, 3], [2, 3, 1, 0], [3, 2, 1, 0]][z]
            rows.append(order + [int(z in (0, 3)), place % 2, place // 2 % 2, place // 4])
    return np.array(rows, np.int32)


def on_line(hidden, conv_weight, se_down, se_up, proj_weight, grad_out):
    hidden, own = to_cells(hidden), to_cells(grad_out)
    shape = own.shape
    channels = shape[3]
    extent = (own.size // channels, channels)
    role = jnp.asarray(places())[lax.axis_index("dp") * 4 + lax.axis_index("chan")]

    outer = along_chan(own, OUTER)
    middle = along_chan(own, MIDDLE)
    w_far = lax.dynamic_slice_in_dim(proj_weight, role[3] * channels, channels, axis=1)
    convolved, act, terms = conv_forward(after(hidden, w_far), conv_weight, se_down)
    excite_pre = small_sum(terms)

    gating, scaled, p_fourth, send = scale(role, act, excite_pre, se_up, w_far, middle)
    came = along_chan(send, OUTER)
    far = along_chan(after(outer, send), MIDDLE)
    other = along_dp(scaled, 1)
    theirs = [along_dp(piece, 1) for piece in (own, outer)]
    p_own, p_outer, p_third = project(role, 3, scaled, proj_weight)
    (begun,) = input_grad(role, 0, [after(own, p_own), outer], proj_weight)

    far, came = lax.optimization_barrier((far, came, begun))[:2]
    third, to_far, send = between(
        second_body, [extent] * 3, role, came, send, far, p_fourth, p_third
    )
    crossed = along_chan(to_far, MIDDLE)
    came = along_chan(send, OUTER)
    theirs.append(along_dp(third, 1))
    pieces = [own, outer, third]
    x_send, x_keep, y_send, y_keep = weight_grad(role, scaled, other, pieces, theirs)
    x_came, y_came = along_dp(x_send, 2), along_dp(y_send, 4)
    (begun,) = input_grad(role, 2, [after(third, y_send)], proj_weight, begun)

    crossed, came = lax.optimization_barrier((crossed, came, begun))[:2]
    half = (extent[0], channels // 2)
    fourth, to_mid, send, give = between(
        third_body, [extent] * 3 + [half], role, came, crossed, send, p_outer, p_third
    )
    crossed = along_chan(to_mid, MIDDLE)
    came = along_chan(send, OUTER)
    upper, lower = weight_grad(role, scaled, other, [fourth], [along_dp(give, 1)])
    upper_came, lower_came = along_dp(upper, 2), along_dp(lower, 4)
    fourth, x_came, y_came = lax.optimization_barrier((fourth, x_came, y_came, lower))[:3]
    scaled_grad, terms = input_grad(
        role, 3, [fourth], proj_weight, begun, act, gating, se_up
    )
    terms, came, crossed = lax.optimization_barrier((terms, came, crossed))
    excite_sum = small_sum(terms)

    top, to_y, bottom, to_x = merge(
        role, x_keep, x_came, y_keep, y_came, upper, upper_came, lower, lower_came
    )
    (projected,) = between(fourth_body, [shape], role, p_own, came, crossed)
    excite_sum = after(excite_sum, to_x, projected)
    grad_hidden = conv_backward(
        scaled_grad, gating, excite_sum, excite_pre, se_down, convolved, conv_weight, shape
    )
    grad_proj = finish(top, along_dp(to_y, 4), bottom, along_dp(to_x, 2))
    return (from_cells(projected), from_cells(grad_hidden), grad_proj)


def on_any(hidden, conv_weight, se_down, se_up, proj_weight, grad_out):
    hidden, pieces = to_cells(hidden), to_cells(grad_out)
    shape = hidden.shape
    images = shape[2]
    convolved, act, terms = conv_forward(hidden, conv_weight, se_down)
    excite_pre = lax.psum(terms, "chan")
    gating = jax.nn.sigmoid(jnp.dot(jax.nn.silu(excite_pre), se_up.astype(F32), precision=HIGHEST))
    act_float = act.astype(F32)
    scaled = (act_float * per_row(gating, act.shape[0])).astype(BF16)
    terms = jnp.dot(scaled, proj_weight, preferred_element_type=F32).astype(BF16)
    projected = lax.psum_scatter(terms, "chan", scatter_dimension=1, tiled=True)
    pieces = lax.all_gather(as_rows(pieces), "chan", axis=1, tiled=True)
    scaled_grad = lax.dot_general(
        pieces, proj_weight, (((1,), (1,)), ((), ())), preferred_element_type=F32
    )
    terms = lax.dot_general(scaled, pieces, (((0,), (0,)), ((), ())), preferred_element_type=F32)
    grad_proj = lax.psum_scatter(terms, "dp", scatter_dimension=1, tiled=True)
    gate_grad = image_sum(scaled_grad * act_float, images)
    pre_grad = gate_grad * gating * (1.0 - gating)
    excite_sum = lax.psum(jnp.dot(pre_grad, se_up.astype(F32).T, precision=HIGHEST), "chan")
    grad_hidden = conv_backward(
        scaled_grad, gating, excite_sum, excite_pre, se_down, convolved, conv_weight, shape
    )
    return (from_cells(projected.reshape(shape)), from_cells(grad_hidden), grad_proj)


def solution(mesh):
    in_specs = (
        P("dp", None, None, "chan"),
        P(None, None, None, "chan"),
        P("chan", None),
        P(None, "chan"),
        P("chan", None),
        P("dp", None, None, "chan"),
    )
    out_specs = (P("dp", None, None, "chan"), P("dp", None, None, "chan"), P("chan", "dp"))
    on_device = on_line if (mesh.shape["dp"], mesh.shape["chan"]) == (8, 4) else on_any
    return jax.shard_map(
        on_device, mesh=mesh, in_specs=in_specs, out_specs=out_specs, check_vma=False
    )
```

```python
import functools

import jax
import jax.numpy as jnp
import numpy as np
from jax import lax
from jax.experimental import pallas as pl
from jax.experimental.pallas import tpu as pltpu
from jax.sharding import PartitionSpec as P

LANES = 256
F32 = jnp.float32
BF16 = jnp.bfloat16
HIGHEST = lax.Precision.HIGHEST


def params(mebibytes=20):
    return pltpu.CompilerParams(vmem_limit_bytes=mebibytes * 1024 * 1024)


SCALE = 0.3
CONV_MIB = 50
FAR_COST = 10


def cost(micros):
    return pl.CostEstimate(
        flops=int(micros * SCALE * 1.15e9), bytes_accessed=1, transcendentals=0
    )


def sum_of(refs):
    own, near, across, over = (ref[...] for ref in refs)
    return (own + near) + (across + over)


def exact_dot(values, weight, dims):
    high = values.astype(BF16).astype(F32)
    rest = values - high
    middle = rest.astype(BF16).astype(F32)
    count = values.shape[0]
    terms = [high, middle, rest - middle, jnp.zeros_like(values)]
    stacked = jnp.concatenate(terms, axis=0).astype(BF16)
    out = lax.dot_general(stacked, weight, (dims, ((), ())), preferred_element_type=F32)
    return out[:count] + out[count : 2 * count] + out[2 * count : 3 * count]


def silu_grad(values):
    logistic = jax.nn.sigmoid(values)
    return logistic * (1.0 + values * (1.0 - logistic))


def to_cells(images):
    return jnp.transpose(images, (1, 2, 0, 3))


def from_cells(cells):
    return jnp.transpose(cells, (2, 0, 1, 3))


def as_rows(values):
    return values.reshape(-1, values.shape[-1])


def whole(shape):
    return pl.BlockSpec(shape, lambda *_: (0,) * len(shape))


def per_row(values, rows):
    tiled = jnp.concatenate([values] * (8 // values.shape[0]), axis=0)
    return jnp.broadcast_to(tiled[None], (rows // 8, 8, values.shape[1])).reshape(rows, -1)


def image_sum(values, images):
    folded = values.reshape(-1, 8, values.shape[1]).sum(axis=0)
    total = folded[:images]
    for start in range(images, 8, images):
        total = total + folded[start : start + images]
    return total


def convolve(rows_ref, pad_ref, weight_ref, height, width, images, turn):
    line, unit = width * images, 16 * images
    group = weight_ref.shape[2]
    pad_ref[...] = jnp.zeros_like(pad_ref)
    for h in range(height):
        pad_ref[pl.ds(8 + (h + 1) * unit + images, line), :] = rows_ref[pl.ds(h * line, line), :]
    row_group = lax.broadcasted_iota(jnp.int32, (LANES, LANES), 0) // group
    col_group = lax.broadcasted_iota(jnp.int32, (LANES, LANES), 1) // group
    mask = (row_group == col_group).astype(F32).astype(BF16)
    cells, taps = [], []
    for dw in range(3):
        shifted = pad_ref[pl.ds(8 + images * (dw - 1), (height + 2) * unit), :].astype(BF16)
        for dh in range(3):
            tap = weight_ref[2 - dh, 2 - dw] if turn else weight_ref[dh, dw]
            taps.append(jnp.concatenate([tap] * (LANES // group), axis=0) * mask)
            cells.append(shifted[dh * unit : (dh + height) * unit])
    total = lax.dot_general(
        jnp.concatenate(cells, axis=1),
        jnp.concatenate(taps, axis=1 if turn else 0),
        (((1,), (1 if turn else 0,)), ((), ())),
        preferred_element_type=F32,
    )
    pad_ref[pl.ds(0, height * unit), :] = total
    for h in range(height):
        rows_ref[pl.ds(h * line, line), :] = pad_ref[pl.ds(h * unit + images, line), :]


HBM = pl.BlockSpec(memory_space=pltpu.HBM)
HERE = pl.BlockSpec(memory_space=pltpu.VMEM)


def lanes_of(i):
    return pl.ds(i * LANES, LANES)


def fetch(source, target, sem):
    copy = pltpu.make_async_copy(source, target, sem)
    copy.start()
    return copy


def conv_forward_body(
    x_hbm,
    w_hbm,
    down_hbm,
    *refs,
    height,
    width,
    images,
):
    conv_hbm, act_ref, pre_ref, x_buf, w_buf, down_buf, conv_buf, rows_ref, pad_ref, sems = refs
    blocks = act_ref.shape[1] // LANES
    copies = [fetch(x_hbm, x_buf, sems.at[0])]
    for i in range(blocks):
        part = w_hbm.at[:, :, :, lanes_of(i)]
        copies.append(fetch(part, w_buf.at[i], sems.at[2 + i]))
    copies[0].wait()
    means = []
    for i in range(blocks):
        rows_ref[...] = as_rows(x_buf[:, :, :, lanes_of(i)]).astype(F32)
        copies[1 + i].wait()
        if i == 0:
            last = [fetch(down_hbm, down_buf, sems.at[1])]
        convolve(rows_ref, pad_ref, w_buf.at[i], height, width, images, False)
        conv = rows_ref[...]
        conv_buf[i] = conv
        last.append(fetch(conv_buf.at[i], conv_hbm.at[:, lanes_of(i)], sems.at[2 + blocks + i]))
        act = (conv * jax.nn.sigmoid(conv)).astype(BF16)
        act_ref[:, lanes_of(i)] = act
        means.append(image_sum(act.astype(F32), images) / (height * width))
    last[0].wait()
    pre_ref[...] = exact_dot(jnp.concatenate(means, axis=1), down_buf[...], ((1,), (0,)))
    for copy in last[1:]:
        copy.wait()


def conv_forward(cells, weight, down):
    height, width, images, channels = cells.shape
    count, inner = height * width * images, down.shape[1]
    blocks = channels // LANES
    return pl.pallas_call(
        functools.partial(conv_forward_body, height=height, width=width, images=images),
        in_specs=[HBM] * 3,
        out_specs=[HBM, HERE, HERE],
        out_shape=[
            jax.ShapeDtypeStruct((count, channels), F32),
            jax.ShapeDtypeStruct((count, channels), BF16),
            jax.ShapeDtypeStruct((images, inner), F32),
        ],
        scratch_shapes=[
            pltpu.VMEM(cells.shape, BF16),
            pltpu.VMEM((blocks, 3, 3, weight.shape[2], LANES), BF16),
            pltpu.VMEM(down.shape, BF16),
            pltpu.VMEM((blocks, count, LANES), F32),
            pltpu.VMEM((count, LANES), F32),
            pltpu.VMEM((16 + (height + 2) * 16 * images, LANES), F32),
            pltpu.SemaphoreType.DMA((2 + 2 * blocks,)),
        ],
        compiler_params=params(CONV_MIB),
        cost_estimate=cost(3),
        name="conv_forward",
    )(cells, weight, down)


def conv_backward_body(
    grad_ref,
    gate_ref,
    own_ref,
    near_ref,
    across_ref,
    over_ref,
    pre_ref,
    down_hbm,
    conv_ref,
    w_hbm,
    out_hbm,
    down_buf,
    w_buf,
    out_buf,
    rows_ref,
    pad_ref,
    sems,
    *,
    height,
    width,
    images,
):
    count, channels = grad_ref.shape
    blocks = channels // LANES
    down_copy = fetch(down_hbm, down_buf, sems.at[0])
    copies = []
    for i in range(blocks):
        part = w_hbm.at[:, :, :, lanes_of(i)]
        copies.append(fetch(part, w_buf.at[i], sems.at[1 + i]))
    excite_sum = sum_of((own_ref, near_ref, across_ref, over_ref))
    excite_grad = excite_sum * silu_grad(pre_ref[...])
    down_copy.wait()
    squeeze_grad = exact_dot(excite_grad, down_buf[...], ((1,), (1,))) / (height * width)
    outs = []
    for i in range(blocks):
        gate = per_row(gate_ref[:, lanes_of(i)], count)
        squeeze = per_row(squeeze_grad[:, i * LANES : (i + 1) * LANES], count)
        act_grad = grad_ref[:, lanes_of(i)] * gate + squeeze
        rows_ref[...] = act_grad * silu_grad(conv_ref[:, lanes_of(i)])
        copies[i].wait()
        convolve(rows_ref, pad_ref, w_buf.at[i], height, width, images, True)
        part = rows_ref[...].astype(BF16).reshape(height, width, images, LANES)
        out_buf[:, :, :, lanes_of(i)] = part
        target = out_hbm.at[:, :, :, lanes_of(i)]
        outs.append(fetch(out_buf.at[:, :, :, lanes_of(i)], target, sems.at[1 + blocks + i]))
    for out in outs:
        out.wait()


def conv_backward(scaled_grad, gating, terms, excite_pre, down, convolved, weight, shape):
    height, width, images, channels = shape
    count = convolved.shape[0]
    blocks = channels // LANES
    return pl.pallas_call(
        functools.partial(conv_backward_body, height=height, width=width, images=images),
        in_specs=[HERE] * 7 + [HBM, HERE, HBM],
        out_specs=HBM,
        out_shape=jax.ShapeDtypeStruct(shape, BF16),
        scratch_shapes=[
            pltpu.VMEM(down.shape, BF16),
            pltpu.VMEM((blocks, 3, 3, weight.shape[2], LANES), BF16),
            pltpu.VMEM(shape, BF16),
            pltpu.VMEM((count, LANES), F32),
            pltpu.VMEM((16 + (height + 2) * 16 * images, LANES), F32),
            pltpu.SemaphoreType.DMA((1 + 2 * blocks,)),
        ],
        compiler_params=params(),
        cost_estimate=cost(3),
        name="conv_backward",
    )(scaled_grad, gating, *terms, excite_pre, down, convolved, weight)


def block_of(weight_ref, block, width):
    return weight_ref.at[:, pl.ds(pl.multiple_of(block * width, width), width)]


def scale_body(
    role_ref,
    act_ref,
    own_ref,
    near_ref,
    across_ref,
    over_ref,
    up_ref,
    w_ref,
    middle_hbm,
    gate_ref,
    pre_ref,
    scaled_hbm,
    far_hbm,
    send_hbm,
    middle_buf,
    send_buf,
    scaled_buf,
    far_buf,
    sems,
):
    middle_copy = fetch(middle_hbm, middle_buf, sems.at[0])
    pre = sum_of((own_ref, near_ref, across_ref, over_ref))
    pre_ref[...] = pre
    excited = pre * jax.nn.sigmoid(pre)
    gate_ref[...] = jax.nn.sigmoid(exact_dot(excited, up_ref[...], ((1,), (0,))))
    gate = per_row(gate_ref[...], act_ref.shape[0])
    scaled_buf[...] = (act_ref[...].astype(F32) * gate).astype(BF16)
    far = jnp.dot(scaled_buf[...], w_ref[...], preferred_element_type=F32).astype(BF16)
    far_buf[...] = far
    middle_copy.wait()

    @pl.when(role_ref[4] == 1)
    def _():
        send_buf[...] = far

    @pl.when(role_ref[4] == 0)
    def _():
        send_buf[...] = as_rows(middle_buf[...])

    sent = [
        fetch(send_buf, send_hbm, sems.at[1]),
        fetch(scaled_buf, scaled_hbm, sems.at[2]),
        fetch(far_buf, far_hbm, sems.at[3]),
    ]
    for copy in sent:
        copy.wait()


def scale(role, act, terms, up, w_far, middle):
    count, channels = act.shape
    gates = (terms[0].shape[0], channels)
    array = jax.ShapeDtypeStruct((count, channels), BF16)
    return pl.pallas_call(
        scale_body,
        in_specs=[pl.BlockSpec(memory_space=pltpu.SMEM)] + [HERE] * 7 + [HBM],
        out_specs=[HERE, HERE, HBM, HBM, HBM],
        out_shape=[
            jax.ShapeDtypeStruct(gates, F32),
            jax.ShapeDtypeStruct(terms[0].shape, F32),
        ]
        + [array] * 3,
        scratch_shapes=[
            pltpu.VMEM(middle.shape, BF16),
            pltpu.VMEM((count, channels), BF16),
            pltpu.VMEM((count, channels), BF16),
            pltpu.VMEM((count, channels), BF16),
            pltpu.SemaphoreType.DMA((4,)),
        ],
        compiler_params=params(),
        cost_estimate=cost(3),
        name="scale",
    )(role, act, *terms, up, w_far, middle)


def project_body(order_ref, scaled_hbm, w_hbm, *refs, parts):
    outs, (scaled_buf, w_buf, out_buf, sems) = refs[:parts], refs[parts:]
    channels = scaled_buf.shape[1]
    scaled_copy = fetch(scaled_hbm, scaled_buf, sems.at[0])
    copies = [
        fetch(block_of(w_hbm, order_ref[k], channels), w_buf.at[k], sems.at[1 + k])
        for k in range(parts)
    ]
    scaled_copy.wait()
    sent = []
    for k in range(parts):
        copies[k].wait()
        part = jnp.dot(scaled_buf[...], w_buf[k], preferred_element_type=F32)
        out_buf[k] = part.astype(BF16)
        sent.append(fetch(out_buf.at[k], outs[k], sems.at[1 + parts + k]))
    for copy in sent:
        copy.wait()


def project(order, parts, scaled, weight):
    count, channels = scaled.shape
    array = jax.ShapeDtypeStruct((count, channels), BF16)
    return pl.pallas_call(
        functools.partial(project_body, parts=parts),
        in_specs=[pl.BlockSpec(memory_space=pltpu.SMEM), HBM, HBM],
        out_specs=[HBM] * parts,
        out_shape=[array] * parts,
        scratch_shapes=[
            pltpu.VMEM((count, channels), BF16),
            pltpu.VMEM((parts, channels, channels), BF16),
            pltpu.VMEM((parts, count, channels), BF16),
            pltpu.SemaphoreType.DMA((1 + 2 * parts,)),
        ],
        compiler_params=params(),
        cost_estimate=cost(3),
        name="project",
    )(order, scaled, weight)


def sum_into(ref, a, b):
    ref[...] = (a[...].astype(F32) + b[...].astype(F32)).astype(BF16)


def choose(role_ref, ref, at_end, else_):
    @pl.when(role_ref[4] == 1)
    def _():
        ref[...] = as_rows(at_end[...])

    @pl.when(role_ref[4] == 0)
    def _():
        ref[...] = as_rows(else_[...])


def far_body(role_ref, p_third, far, send):
    choose(role_ref, send, p_third, far)


def second_body(role_ref, came, held, p_fourth, third, to_far):
    sum_into(to_far, p_fourth, came)
    choose(role_ref, third, came, held)


def third_body(role_ref, came, held, p_third, fourth, to_mid, give):
    sum_into(to_mid, p_third, came)
    choose(role_ref, fourth, came, held)
    half = give.shape[1]
    give[...] = fourth[:, pl.ds(pl.multiple_of((1 - role_ref[5]) * half, half), half)]


def outer_body(role_ref, crossed, p_outer, send):
    @pl.when(role_ref[4] == 1)
    def _():
        send[...] = p_outer[...]

    @pl.when(role_ref[4] == 0)
    def _():
        sum_into(send, p_outer, crossed)


def fourth_body(role_ref, p_own, came, crossed, total):
    at_end = role_ref[4] == 1
    near = p_own[...].astype(F32) + came[...].astype(F32)

    @pl.when(at_end)
    def _():
        total[...] = near.astype(BF16).reshape(total.shape)

    @pl.when(jnp.logical_not(at_end))
    def _():
        total[...] = (near + crossed[...].astype(F32)).astype(BF16).reshape(total.shape)


def between(body, extents, role, *arrays, micros=0.02):
    return pl.pallas_call(
        body,
        grid=(1,),
        in_specs=[pl.BlockSpec(memory_space=pltpu.SMEM)] + [whole(a.shape) for a in arrays],
        out_specs=[whole(extent) for extent in extents],
        out_shape=[jax.ShapeDtypeStruct(extent, BF16) for extent in extents],
        compiler_params=params(),
        cost_estimate=cost(micros),
        name=body.__name__.replace("_body", "_turn"),
    )(role, *arrays)


def input_grad_body(role_ref, *refs, first, pieces, started, last, images):
    piece_refs, w_hbm, refs = refs[:pieces], refs[pieces], refs[pieces + 1 :]
    if started:
        start_ref, refs = refs[0], refs[1:]
    if last:
        act_ref, gate_ref, up_hbm, out_ref, excite_ref, w_buf, sems, up_buf = refs[:8]
    else:
        out_ref, w_buf, sems = refs[:3]
    piece_bufs = refs[-pieces:]
    width = out_ref.shape[1]
    copies = []
    for k, piece_ref in enumerate(piece_refs):
        block = block_of(w_hbm, role_ref[first + k], width)
        copies.append(
            (
                fetch(piece_ref, piece_bufs[k], sems.at[2 * k]),
                fetch(block, w_buf.at[k], sems.at[2 * k + 1]),
            )
        )
    if last:
        up_copy = fetch(up_hbm, up_buf, sems.at[2 * pieces])
    for k in range(pieces):
        for copy in copies[k]:
            copy.wait()
        part = lax.dot_general(
            as_rows(piece_bufs[k][...]),
            w_buf[k],
            (((1,), (1,)), ((), ())),
            preferred_element_type=F32,
        )
        if k > 0:
            part = out_ref[...] + part
        elif started:
            part = start_ref[...] + part
        out_ref[...] = part
    if last:
        gating = gate_ref[...]
        gate_grad = image_sum(out_ref[...] * act_ref[...].astype(F32), images)
        pre_grad = gate_grad * gating * (1.0 - gating)
        up_copy.wait()
        excite_ref[...] = exact_dot(pre_grad, up_buf[...], ((1,), (1,)))


def input_grad(role, first, pieces, weight, start=None, act=None, gating=None, up=None):
    channels = weight.shape[0]
    count = pieces[0].size // channels
    images = 1 if gating is None else gating.shape[0]
    started, last = start is not None, act is not None
    operands = list(pieces) + [weight]
    in_specs = [pl.BlockSpec(memory_space=pltpu.SMEM)] + [HBM] * (len(pieces) + 1)
    out_shape = [jax.ShapeDtypeStruct((count, channels), F32)]
    scratch = [
        pltpu.VMEM((len(pieces), channels, channels), BF16),
        pltpu.SemaphoreType.DMA((2 * len(pieces) + 1,)),
    ]
    if started:
        operands.append(start)
        in_specs.append(HERE)
    if last:
        operands += [act, gating, up]
        in_specs += [HERE, HERE, HBM]
        out_shape.append(jax.ShapeDtypeStruct((images, up.shape[0]), F32))
        scratch.append(pltpu.VMEM(up.shape, BF16))
    scratch += [pltpu.VMEM(piece.shape, BF16) for piece in pieces]
    return pl.pallas_call(
        functools.partial(
            input_grad_body,
            first=first,
            pieces=len(pieces),
            started=started,
            last=last,
            images=images,
        ),
        in_specs=in_specs,
        out_specs=[HERE] * len(out_shape),
        out_shape=out_shape,
        scratch_shapes=scratch,
        compiler_params=params(),
        cost_estimate=cost(10 if last or first == 0 else 0.02),
        name="input_grad_last" if last else "input_grad",
    )(role, *operands)


def place_block(total, block, x, y, x_send, x_keep, y_send, y_keep):
    half = total.shape[0] // 2
    to_x, to_y = block % 2, block // 2

    @pl.when(to_x != x)
    def _():
        x_send[to_y] = total[:half]

    @pl.when(to_x == x)
    def _():
        x_keep[to_y] = total[:half]

    @pl.when(to_y != y)
    def _():
        y_send[to_x] = total[half:]

    @pl.when(to_y == y)
    def _():
        y_keep[to_x] = total[half:]


def weight_grad_body(place_ref, own_ref, other_ref, *refs, pieces):
    mine, theirs, outs = refs[:pieces], refs[pieces : 2 * pieces], refs[2 * pieces :]
    x, y = place_ref[6], place_ref[7]
    own, other = own_ref[...].T, other_ref[...].T
    for k in range(pieces):
        total = jnp.dot(own, as_rows(mine[k][...]), preferred_element_type=F32)
        total += jnp.dot(other, as_rows(theirs[k][...]), preferred_element_type=F32)
        total = total.astype(BF16)
        if pieces > 1:
            place_block(total, place_ref[k], x, y, *outs)
        else:
            half = total.shape[0] // 2
            outs[0][...] = total[:half]
            outs[1][...] = total[half:]
    if pieces > 1:
        place_block(jnp.zeros_like(total), place_ref[pieces], x, y, *outs)


def weight_grad(place, own, other, mine, theirs):
    count, channels = own.shape
    columns = channels // 2
    pieces = len(mine)

    def part(array):
        if array.shape[-1] == columns:
            return whole(array.shape)
        lead = array.shape[:-1]
        return pl.BlockSpec((*lead, columns), lambda i, place: (0,) * len(lead) + (place[5],))

    extent = (channels // 2, columns)
    if pieces > 1:
        extent = (2, *extent)
    outs = 4 if pieces > 1 else 2
    return pl.pallas_call(
        functools.partial(weight_grad_body, pieces=pieces),
        grid_spec=pltpu.PrefetchScalarGridSpec(
            num_scalar_prefetch=1,
            grid=(1,),
            in_specs=[whole(own.shape)] * 2 + [part(piece) for piece in (*mine, *theirs)],
            out_specs=[whole(extent)] * outs,
        ),
        out_shape=[jax.ShapeDtypeStruct(extent, BF16)] * outs,
        compiler_params=params(),
        cost_estimate=cost(2 * pieces if pieces > 1 else 0.02),
        name="weight_grad" if pieces > 1 else "weight_grad_more",
    )(place, own, other, *mine, *theirs)


def merge_body(place_ref, *refs):
    x_keep, x_came, y_keep, y_came, upper, upper_came, lower, lower_came = refs[:8]
    top, to_y, bottom, to_x = refs[8:]
    block, x, y = place_ref[3], place_ref[6], place_ref[7]
    to_bx, to_by = block % 2 == x, block // 2 == y

    def both(a, b):
        return a[...].astype(F32) + b[...].astype(F32)

    for keep, came, index, more, more_came, here, there, stay, leave in (
        (x_keep, x_came, y, upper, upper_came, to_bx, to_by, top, to_y),
        (y_keep, y_came, x, lower, lower_came, to_by, to_bx, bottom, to_x),
    ):
        extra = jnp.where(here, both(more, more_came), 0.0)
        stay[...] = both(keep.at[index], came.at[index]) + jnp.where(there, extra, 0.0)
        rest = both(keep.at[1 - index], came.at[1 - index]) + jnp.where(there, 0.0, extra)
        leave[...] = rest.astype(BF16)


def merge(place, *arrays):
    rows, columns = arrays[0].shape[1:]
    pair = pl.BlockSpec((2, rows, columns), lambda i, place: (0, 0, 0))
    one = pl.BlockSpec((rows, columns), lambda i, place: (0, 0))
    kept = jax.ShapeDtypeStruct((rows, columns), F32)
    sent = jax.ShapeDtypeStruct((rows, columns), BF16)
    return pl.pallas_call(
        merge_body,
        grid_spec=pltpu.PrefetchScalarGridSpec(
            num_scalar_prefetch=1, grid=(1,), in_specs=[pair] * 4 + [one] * 4, out_specs=[one] * 4
        ),
        out_shape=[kept, sent, kept, sent],
        compiler_params=params(),
        cost_estimate=cost(2),
        name="merge",
    )(place, *arrays)


def finish_body(top, top_came, bottom, bottom_came, out):
    rows = top.shape[0]
    out[:rows] = top[...] + top_came[...].astype(F32)
    out[rows:] = bottom[...] + bottom_came[...].astype(F32)


def finish(top, top_came, bottom, bottom_came):
    rows, columns = top.shape
    one = pl.BlockSpec((rows, columns), lambda i: (0, 0))
    return pl.pallas_call(
        finish_body,
        grid=(1,),
        in_specs=[one] * 4,
        out_specs=pl.BlockSpec((2 * rows, columns), lambda i: (0, 0)),
        out_shape=jax.ShapeDtypeStruct((2 * rows, columns), F32),
        compiler_params=params(),
        cost_estimate=cost(2),
        name="finish",
    )(top, top_came, bottom, bottom_came)


OUTER = [(0, 1), (1, 0), (2, 3), (3, 2)]
INWARD = [(0, 1), (3, 2)]
OUTWARD = [(1, 0), (2, 3)]
MIDDLE = [(1, 2), (2, 1)]
OVER = [(0, 2), (2, 0), (1, 3), (3, 1)]
CROSS = [(0, 3), (3, 0), (1, 2), (2, 1)]


def along_chan(array, pairs):
    return lax.ppermute(array, "chan", pairs)


def along_dp(array, bit):
    return lax.ppermute(array, "dp", [(i, i ^ bit) for i in range(8)])


def gather_small(values):
    return [values] + [along_chan(values, pairs) for pairs in (OUTER, CROSS, OVER)]


def after(array, *others):
    return lax.optimization_barrier((array, *others))[0]


def places():
    rows = []
    for place in range(8):
        for z in range(4):
            order = [[0, 1, 2, 3], [1, 0, 2, 3], [2, 3, 1, 0], [3, 2, 1, 0]][z]
            rows.append(order + [int(z in (0, 3)), place % 2, place // 2 % 2, place // 4])
    return np.array(rows, np.int32)


def on_line(hidden, conv_weight, se_down, se_up, proj_weight, grad_out):
    hidden, own = to_cells(hidden), to_cells(grad_out)
    shape = own.shape
    channels = shape[3]
    extent = (own.size // channels, channels)
    role = jnp.asarray(places())[lax.axis_index("dp") * 4 + lax.axis_index("chan")]

    outer = along_chan(own, OUTER)
    middle = along_chan(own, MIDDLE)
    w_far = lax.dynamic_slice_in_dim(proj_weight, role[3] * channels, channels, axis=1)
    convolved, act, terms = conv_forward(after(hidden, w_far), conv_weight, se_down)
    terms = gather_small(terms)
    far = along_chan(after(outer, *terms), MIDDLE)
    gating, excite_pre, scaled, p_fourth, send = scale(role, act, terms, se_up, w_far, middle)
    came = along_chan(send, OUTER)
    other = along_dp(scaled, 1)
    theirs = [along_dp(piece, 1) for piece in (own, outer)]
    p_own, p_outer, p_third = project(role, 3, scaled, proj_weight)
    (begun,) = input_grad(role, 0, [after(own, p_own), outer], proj_weight)

    (send_far,) = between(
        far_body, [extent], role, p_third, after(far, begun), micros=FAR_COST
    )
    came_far = along_chan(send_far, OUTER)
    third, to_far = between(second_body, [extent] * 2, role, came, send, p_fourth)
    crossed = along_chan(to_far, MIDDLE)
    theirs.append(along_dp(third, 1))
    pieces = [own, outer, after(third, to_far)]
    x_send, x_keep, y_send, y_keep = weight_grad(role, scaled, other, pieces, theirs)
    x_came, y_came = along_dp(x_send, 2), along_dp(y_send, 4)
    (begun,) = input_grad(role, 2, [after(third, y_send)], proj_weight, begun)

    came_far = after(came_far, begun)
    half = (extent[0], channels // 2)
    fourth, to_mid, give = between(
        third_body, [extent] * 2 + [half], role, came_far, send_far, p_third
    )
    crossed_mid = along_chan(to_mid, MIDDLE)
    (send,) = between(outer_body, [extent], role, after(crossed, to_mid), p_outer)
    came = along_chan(send, OUTER)
    crossed = crossed_mid
    fourth = after(fourth, send)
    upper, lower = weight_grad(role, scaled, other, [fourth], [along_dp(give, 1)])
    upper_came, lower_came = along_dp(upper, 2), along_dp(lower, 4)
    fourth, x_came, y_came = lax.optimization_barrier((fourth, x_came, y_came, lower))[:3]
    scaled_grad, terms = input_grad(
        role, 3, [fourth], proj_weight, begun, act, gating, se_up
    )
    upper_came = after(upper_came, terms)
    top, to_y, bottom, to_x = merge(
        role, x_keep, x_came, y_keep, y_came, upper, upper_came, lower, lower_came
    )
    terms, came, crossed = lax.optimization_barrier((terms, came, crossed, to_x))[:3]
    terms = gather_small(terms)
    (projected,) = between(fourth_body, [shape], role, p_own, came, crossed)
    terms[0] = after(terms[0], projected)
    grad_hidden = conv_backward(
        scaled_grad, gating, terms, excite_pre, se_down, convolved, conv_weight, shape
    )
    grad_proj = finish(top, along_dp(to_y, 4), bottom, along_dp(to_x, 2))
    return (from_cells(projected), from_cells(grad_hidden), grad_proj)


def on_any(hidden, conv_weight, se_down, se_up, proj_weight, grad_out):
    hidden, pieces = to_cells(hidden), to_cells(grad_out)
    shape = hidden.shape
    images = shape[2]
    convolved, act, terms = conv_forward(hidden, conv_weight, se_down)
    excite_pre = lax.psum(terms, "chan")
    nothing = jnp.zeros_like(excite_pre)
    gating = jax.nn.sigmoid(jnp.dot(jax.nn.silu(excite_pre), se_up.astype(F32), precision=HIGHEST))
    act_float = act.astype(F32)
    scaled = (act_float * per_row(gating, act.shape[0])).astype(BF16)
    terms = jnp.dot(scaled, proj_weight, preferred_element_type=F32).astype(BF16)
    projected = lax.psum_scatter(terms, "chan", scatter_dimension=1, tiled=True)
    pieces = lax.all_gather(as_rows(pieces), "chan", axis=1, tiled=True)
    scaled_grad = lax.dot_general(
        pieces, proj_weight, (((1,), (1,)), ((), ())), preferred_element_type=F32
    )
    terms = lax.dot_general(scaled, pieces, (((0,), (0,)), ((), ())), preferred_element_type=F32)
    grad_proj = lax.psum_scatter(terms, "dp", scatter_dimension=1, tiled=True)
    gate_grad = image_sum(scaled_grad * act_float, images)
    pre_grad = gate_grad * gating * (1.0 - gating)
    excite_sum = lax.psum(jnp.dot(pre_grad, se_up.astype(F32).T, precision=HIGHEST), "chan")
    terms = [excite_sum] + [nothing] * 3
    grad_hidden = conv_backward(
        scaled_grad, gating, terms, excite_pre, se_down, convolved, conv_weight, shape
    )
    return (from_cells(projected.reshape(shape)), from_cells(grad_hidden), grad_proj)


def solution(mesh):
    in_specs = (
        P("dp", None, None, "chan"),
        P(None, None, None, "chan"),
        P("chan", None),
        P(None, "chan"),
        P("chan", None),
        P("dp", None, None, "chan"),
    )
    out_specs = (P("dp", None, None, "chan"), P("dp", None, None, "chan"), P("chan", "dp"))
    on_device = on_line if (mesh.shape["dp"], mesh.shape["chan"]) == (8, 4) else on_any
    return jax.shard_map(
        on_device, mesh=mesh, in_specs=in_specs, out_specs=out_specs, check_vma=False
    )
```

```python
import functools

import jax
import jax.numpy as jnp
import numpy as np
from jax import lax
from jax.experimental import pallas as pl
from jax.experimental.pallas import tpu as pltpu
from jax.sharding import PartitionSpec as P

LANES = 256
F32 = jnp.float32
BF16 = jnp.bfloat16
HIGHEST = lax.Precision.HIGHEST


def params(mebibytes=20):
    return pltpu.CompilerParams(vmem_limit_bytes=mebibytes * 1024 * 1024)


SCALE = 0.3
CONV_MIB = 20
FAR_COST = 10
TURN_COST = 1


def cost(micros):
    return pl.CostEstimate(
        flops=int(micros * SCALE * 1.15e9), bytes_accessed=1, transcendentals=0
    )


def sum_of(refs):
    own, near, across, over = (ref[...] for ref in refs)
    return (own + near) + (across + over)


def exact_dot(values, weight, dims):
    high = values.astype(BF16).astype(F32)
    rest = values - high
    middle = rest.astype(BF16).astype(F32)
    count = values.shape[0]
    terms = [high, middle, rest - middle, jnp.zeros_like(values)]
    stacked = jnp.concatenate(terms, axis=0).astype(BF16)
    if dims == ((1,), (1,)):
        out = lax.dot_general(weight, stacked, (dims, ((), ())), preferred_element_type=F32).T
    else:
        out = lax.dot_general(stacked, weight, (dims, ((), ())), preferred_element_type=F32)
    return out[:count] + out[count : 2 * count] + out[2 * count : 3 * count]


def silu_grad(values):
    logistic = jax.nn.sigmoid(values)
    return logistic * (1.0 + values * (1.0 - logistic))


def to_cells(images):
    return jnp.transpose(images, (1, 2, 0, 3))


def from_cells(cells):
    return jnp.transpose(cells, (2, 0, 1, 3))


def as_rows(values):
    return values.reshape(-1, values.shape[-1])


def whole(shape):
    return pl.BlockSpec(shape, lambda *_: (0,) * len(shape))


def per_row(values, rows):
    tiled = jnp.concatenate([values] * (8 // values.shape[0]), axis=0)
    return jnp.broadcast_to(tiled[None], (rows // 8, 8, values.shape[1])).reshape(rows, -1)


def image_sum(values, images):
    folded = values.reshape(-1, 8, values.shape[1]).sum(axis=0)
    total = folded[:images]
    for start in range(images, 8, images):
        total = total + folded[start : start + images]
    return total


def convolve(rows_ref, pad_ref, weight_ref, height, width, images, turn):
    line, unit = width * images, 16 * images
    group = weight_ref.shape[2]
    pad_ref[...] = jnp.zeros_like(pad_ref)
    for h in range(height):
        pad_ref[pl.ds(8 + (h + 1) * unit + images, line), :] = rows_ref[pl.ds(h * line, line), :]
    row_group = lax.broadcasted_iota(jnp.int32, (LANES, LANES), 0) // group
    col_group = lax.broadcasted_iota(jnp.int32, (LANES, LANES), 1) // group
    mask = (row_group == col_group).astype(F32).astype(BF16)
    cells, taps = [], []
    for dw in range(3):
        shifted = pad_ref[pl.ds(8 + images * (dw - 1), (height + 2) * unit), :].astype(BF16)
        for dh in range(3):
            tap = weight_ref[2 - dh, 2 - dw] if turn else weight_ref[dh, dw]
            taps.append(jnp.concatenate([tap] * (LANES // group), axis=0) * mask)
            cells.append(shifted[dh * unit : (dh + height) * unit])
    total = lax.dot_general(
        jnp.concatenate(cells, axis=1),
        jnp.concatenate(taps, axis=1 if turn else 0),
        (((1,), (1 if turn else 0,)), ((), ())),
        preferred_element_type=F32,
    )
    pad_ref[pl.ds(0, height * unit), :] = total
    for h in range(height):
        rows_ref[pl.ds(h * line, line), :] = pad_ref[pl.ds(h * unit + images, line), :]


HBM = pl.BlockSpec(memory_space=pltpu.HBM)
HERE = pl.BlockSpec(memory_space=pltpu.VMEM)


def lanes_of(i):
    return pl.ds(i * LANES, LANES)


def fetch(source, target, sem):
    copy = pltpu.make_async_copy(source, target, sem)
    copy.start()
    return copy


def conv_forward_body(
    x_ref,
    w_ref,
    down_ref,
    conv_hbm,
    act_ref,
    pre_ref,
    conv_buf,
    rows_ref,
    pad_ref,
    sems,
    *,
    height,
    width,
    images,
):
    blocks = act_ref.shape[1] // LANES
    means, outs = [], []
    for i in range(blocks):
        rows = rows_ref.at[i]
        rows[...] = as_rows(x_ref[:, :, :, lanes_of(i)]).astype(F32)
        part = w_ref.at[:, :, :, lanes_of(i)]
        convolve(rows, pad_ref.at[i], part, height, width, images, False)
        conv = rows[...]
        conv_buf[i] = conv
        outs.append(fetch(conv_buf.at[i], conv_hbm.at[:, lanes_of(i)], sems.at[i]))
        act = (conv * jax.nn.sigmoid(conv)).astype(BF16)
        act_ref[:, lanes_of(i)] = act
        means.append(image_sum(act.astype(F32), images) / (height * width))
    pre_ref[...] = exact_dot(jnp.concatenate(means, axis=1), down_ref[...], ((1,), (0,)))
    for out in outs:
        out.wait()


def conv_forward(cells, weight, down):
    height, width, images, channels = cells.shape
    count, inner = height * width * images, down.shape[1]
    blocks = channels // LANES
    return pl.pallas_call(
        functools.partial(conv_forward_body, height=height, width=width, images=images),
        in_specs=[HERE] * 3,
        out_specs=[HBM, HERE, HERE],
        out_shape=[
            jax.ShapeDtypeStruct((count, channels), F32),
            jax.ShapeDtypeStruct((count, channels), BF16),
            jax.ShapeDtypeStruct((images, inner), F32),
        ],
        scratch_shapes=[
            pltpu.VMEM((blocks, count, LANES), F32),
            pltpu.VMEM((blocks, count, LANES), F32),
            pltpu.VMEM((blocks, 16 + (height + 2) * 16 * images, LANES), F32),
            pltpu.SemaphoreType.DMA((blocks,)),
        ],
        compiler_params=params(CONV_MIB),
        cost_estimate=cost(3),
        name="conv_forward",
    )(cells, weight, down)


def conv_grad_body(grad_ref, gate_ref, conv_ref, part_ref, slope_ref, *, cells):
    slope = silu_grad(conv_ref[...])
    part_ref[...] = grad_ref[...] * per_row(gate_ref[...], conv_ref.shape[0]) * slope
    slope_ref[...] = slope / cells


def conv_grad_terms(scaled_grad, gating, convolved, cells):
    array = jax.ShapeDtypeStruct(convolved.shape, F32)
    return pl.pallas_call(
        functools.partial(conv_grad_body, cells=cells),
        grid=(1,),
        in_specs=[whole(a.shape) for a in (scaled_grad, gating, convolved)],
        out_specs=[whole(array.shape)] * 2,
        out_shape=[array] * 2,
        compiler_params=params(),
        cost_estimate=cost(0.02),
        name="conv_grad",
    )(scaled_grad, gating, convolved)


def conv_backward_body(
    part_ref,
    slope_ref,
    own_ref,
    near_ref,
    across_ref,
    over_ref,
    pre_ref,
    down_ref,
    w_ref,
    out_hbm,
    out_buf,
    rows_ref,
    pad_ref,
    sems,
    *,
    height,
    width,
    images,
):
    count, channels = part_ref.shape
    blocks = channels // LANES
    excite_sum = sum_of((own_ref, near_ref, across_ref, over_ref))
    excite_grad = excite_sum * silu_grad(pre_ref[...])
    squeeze_grad = exact_dot(excite_grad, down_ref[...], ((1,), (1,)))
    outs = []
    for i in range(blocks):
        rows = rows_ref.at[i]
        squeeze = per_row(squeeze_grad[:, i * LANES : (i + 1) * LANES], count)
        rows[...] = part_ref[:, lanes_of(i)] + squeeze * slope_ref[:, lanes_of(i)]
        part = w_ref.at[:, :, :, lanes_of(i)]
        convolve(rows, pad_ref.at[i], part, height, width, images, True)
        part = rows[...].astype(BF16).reshape(height, width, images, LANES)
        out_buf[:, :, :, lanes_of(i)] = part
        target = out_hbm.at[:, :, :, lanes_of(i)]
        outs.append(fetch(out_buf.at[:, :, :, lanes_of(i)], target, sems.at[i]))
    for out in outs:
        out.wait()


def conv_backward(part, slope, terms, excite_pre, down, weight, shape):
    height, width, images, channels = shape
    count = part.shape[0]
    blocks = channels // LANES
    return pl.pallas_call(
        functools.partial(conv_backward_body, height=height, width=width, images=images),
        in_specs=[HERE] * 9,
        out_specs=HBM,
        out_shape=jax.ShapeDtypeStruct(shape, BF16),
        scratch_shapes=[
            pltpu.VMEM(shape, BF16),
            pltpu.VMEM((blocks, count, LANES), F32),
            pltpu.VMEM((blocks, 16 + (height + 2) * 16 * images, LANES), F32),
            pltpu.SemaphoreType.DMA((blocks,)),
        ],
        compiler_params=params(),
        cost_estimate=cost(3),
        name="conv_backward",
    )(part, slope, *terms, excite_pre, down, weight)


def block_of(weight_ref, block, width):
    return weight_ref.at[:, pl.ds(pl.multiple_of(block * width, width), width)]


def scale_body(
    role_ref,
    act_ref,
    own_ref,
    near_ref,
    across_ref,
    over_ref,
    up_ref,
    w_ref,
    middle_hbm,
    gate_ref,
    pre_ref,
    scaled_hbm,
    far_hbm,
    send_hbm,
    middle_buf,
    send_buf,
    scaled_buf,
    far_buf,
    sems,
):
    middle_copy = fetch(middle_hbm, middle_buf, sems.at[0])
    pre = sum_of((own_ref, near_ref, across_ref, over_ref))
    pre_ref[...] = pre
    excited = pre * jax.nn.sigmoid(pre)
    gate_ref[...] = jax.nn.sigmoid(exact_dot(excited, up_ref[...], ((1,), (0,))))
    gate = per_row(gate_ref[...], act_ref.shape[0])
    scaled_buf[...] = (act_ref[...].astype(F32) * gate).astype(BF16)
    far = jnp.dot(scaled_buf[...], w_ref[...], preferred_element_type=F32).astype(BF16)
    far_buf[...] = far
    middle_copy.wait()

    @pl.when(role_ref[4] == 1)
    def _():
        send_buf[...] = far

    @pl.when(role_ref[4] == 0)
    def _():
        send_buf[...] = as_rows(middle_buf[...])

    sent = [
        fetch(send_buf, send_hbm, sems.at[1]),
        fetch(scaled_buf, scaled_hbm, sems.at[2]),
        fetch(far_buf, far_hbm, sems.at[3]),
    ]
    for copy in sent:
        copy.wait()


def scale(role, act, terms, up, w_far, middle):
    count, channels = act.shape
    gates = (terms[0].shape[0], channels)
    array = jax.ShapeDtypeStruct((count, channels), BF16)
    return pl.pallas_call(
        scale_body,
        in_specs=[pl.BlockSpec(memory_space=pltpu.SMEM)] + [HERE] * 7 + [HBM],
        out_specs=[HERE, HERE, HBM, HBM, HBM],
        out_shape=[
            jax.ShapeDtypeStruct(gates, F32),
            jax.ShapeDtypeStruct(terms[0].shape, F32),
        ]
        + [array] * 3,
        scratch_shapes=[
            pltpu.VMEM(middle.shape, BF16),
            pltpu.VMEM((count, channels), BF16),
            pltpu.VMEM((count, channels), BF16),
            pltpu.VMEM((count, channels), BF16),
            pltpu.SemaphoreType.DMA((4,)),
        ],
        compiler_params=params(),
        cost_estimate=cost(3),
        name="scale",
    )(role, act, *terms, up, w_far, middle)


def project_body(order_ref, scaled_hbm, w_hbm, *refs, parts):
    outs, (scaled_buf, w_buf, out_buf, sems) = refs[:parts], refs[parts:]
    channels = scaled_buf.shape[1]
    scaled_copy = fetch(scaled_hbm, scaled_buf, sems.at[0])
    copies = [
        fetch(block_of(w_hbm, order_ref[k], channels), w_buf.at[k], sems.at[1 + k])
        for k in range(parts)
    ]
    scaled_copy.wait()
    sent = []
    for k in range(parts):
        copies[k].wait()
        part = jnp.dot(scaled_buf[...], w_buf[k], preferred_element_type=F32)
        out_buf[k] = part.astype(BF16)
        sent.append(fetch(out_buf.at[k], outs[k], sems.at[1 + parts + k]))
    for copy in sent:
        copy.wait()


def project(order, parts, scaled, weight):
    count, channels = scaled.shape
    array = jax.ShapeDtypeStruct((count, channels), BF16)
    return pl.pallas_call(
        functools.partial(project_body, parts=parts),
        in_specs=[pl.BlockSpec(memory_space=pltpu.SMEM), HBM, HBM],
        out_specs=[HBM] * parts,
        out_shape=[array] * parts,
        scratch_shapes=[
            pltpu.VMEM((count, channels), BF16),
            pltpu.VMEM((parts, channels, channels), BF16),
            pltpu.VMEM((parts, count, channels), BF16),
            pltpu.SemaphoreType.DMA((1 + 2 * parts,)),
        ],
        compiler_params=params(),
        cost_estimate=cost(3),
        name="project",
    )(order, scaled, weight)


def sum_into(ref, a, b):
    ref[...] = (a[...].astype(F32) + b[...].astype(F32)).astype(BF16)


def choose(role_ref, ref, at_end, else_):
    @pl.when(role_ref[4] == 1)
    def _():
        ref[...] = as_rows(at_end[...])

    @pl.when(role_ref[4] == 0)
    def _():
        ref[...] = as_rows(else_[...])


def far_body(role_ref, p_third, far, send):
    choose(role_ref, send, p_third, far)


def second_body(role_ref, came, held, p_fourth, third, to_far):
    sum_into(to_far, p_fourth, came)
    choose(role_ref, third, came, held)


def third_body(role_ref, came, held, p_third, fourth, to_mid, give):
    sum_into(to_mid, p_third, came)
    choose(role_ref, fourth, came, held)
    half = give.shape[1]
    give[...] = fourth[:, pl.ds(pl.multiple_of((1 - role_ref[5]) * half, half), half)]


def outer_body(role_ref, crossed, p_outer, send):
    @pl.when(role_ref[4] == 1)
    def _():
        send[...] = p_outer[...]

    @pl.when(role_ref[4] == 0)
    def _():
        sum_into(send, p_outer, crossed)


def fourth_body(role_ref, p_own, came, crossed, total):
    at_end = role_ref[4] == 1
    near = p_own[...].astype(F32) + came[...].astype(F32)

    @pl.when(at_end)
    def _():
        total[...] = near.astype(BF16).reshape(total.shape)

    @pl.when(jnp.logical_not(at_end))
    def _():
        total[...] = (near + crossed[...].astype(F32)).astype(BF16).reshape(total.shape)


def between(body, extents, role, *arrays, micros=0.02):
    return pl.pallas_call(
        body,
        grid=(1,),
        in_specs=[pl.BlockSpec(memory_space=pltpu.SMEM)] + [whole(a.shape) for a in arrays],
        out_specs=[whole(extent) for extent in extents],
        out_shape=[jax.ShapeDtypeStruct(extent, BF16) for extent in extents],
        compiler_params=params(),
        cost_estimate=cost(micros),
        name=body.__name__.replace("_body", "_turn"),
    )(role, *arrays)


def input_grad_body(role_ref, *refs, first, pieces, started, last, images):
    piece_refs, w_hbm, refs = refs[:pieces], refs[pieces], refs[pieces + 1 :]
    if started:
        start_ref, refs = refs[0], refs[1:]
    if last:
        act_ref, gate_ref, up_hbm, out_ref, excite_ref, w_buf, sems, up_buf = refs[:8]
    else:
        out_ref, w_buf, sems = refs[:3]
    piece_bufs = refs[-pieces:]
    width = out_ref.shape[1]
    copies = []
    for k, piece_ref in enumerate(piece_refs):
        block = block_of(w_hbm, role_ref[first + k], width)
        copies.append(
            (
                fetch(piece_ref, piece_bufs[k], sems.at[2 * k]),
                fetch(block, w_buf.at[k], sems.at[2 * k + 1]),
            )
        )
    if last:
        up_copy = fetch(up_hbm, up_buf, sems.at[2 * pieces])
    for k in range(pieces):
        for copy in copies[k]:
            copy.wait()
        part = lax.dot_general(
            as_rows(piece_bufs[k][...]),
            w_buf[k],
            (((1,), (1,)), ((), ())),
            preferred_element_type=F32,
        )
        if k > 0:
            part = out_ref[...] + part
        elif started:
            part = start_ref[...] + part
        out_ref[...] = part
    if last:
        gating = gate_ref[...]
        gate_grad = image_sum(out_ref[...] * act_ref[...].astype(F32), images)
        pre_grad = gate_grad * gating * (1.0 - gating)
        up_copy.wait()
        excite_ref[...] = exact_dot(pre_grad, up_buf[...], ((1,), (1,)))


def input_grad(role, first, pieces, weight, start=None, act=None, gating=None, up=None):
    channels = weight.shape[0]
    count = pieces[0].size // channels
    images = 1 if gating is None else gating.shape[0]
    started, last = start is not None, act is not None
    operands = list(pieces) + [weight]
    in_specs = [pl.BlockSpec(memory_space=pltpu.SMEM)] + [HBM] * (len(pieces) + 1)
    out_shape = [jax.ShapeDtypeStruct((count, channels), F32)]
    scratch = [
        pltpu.VMEM((len(pieces), channels, channels), BF16),
        pltpu.SemaphoreType.DMA((2 * len(pieces) + 1,)),
    ]
    if started:
        operands.append(start)
        in_specs.append(HERE)
    if last:
        operands += [act, gating, up]
        in_specs += [HERE, HERE, HBM]
        out_shape.append(jax.ShapeDtypeStruct((images, up.shape[0]), F32))
        scratch.append(pltpu.VMEM(up.shape, BF16))
    scratch += [pltpu.VMEM(piece.shape, BF16) for piece in pieces]
    return pl.pallas_call(
        functools.partial(
            input_grad_body,
            first=first,
            pieces=len(pieces),
            started=started,
            last=last,
            images=images,
        ),
        in_specs=in_specs,
        out_specs=[HERE] * len(out_shape),
        out_shape=out_shape,
        scratch_shapes=scratch,
        compiler_params=params(),
        cost_estimate=cost(10 if last else 0.02),
        name="input_grad_last" if last else "input_grad",
    )(role, *operands)


def place_block(total, block, x, y, x_send, x_keep, y_send, y_keep):
    half = total.shape[0] // 2
    to_x, to_y = block % 2, block // 2

    @pl.when(to_x != x)
    def _():
        x_send[to_y] = total[:half]

    @pl.when(to_x == x)
    def _():
        x_keep[to_y] = total[:half]

    @pl.when(to_y != y)
    def _():
        y_send[to_x] = total[half:]

    @pl.when(to_y == y)
    def _():
        y_keep[to_x] = total[half:]


def weight_grad_body(place_ref, own_ref, other_ref, *refs, pieces):
    mine, theirs, outs = refs[:pieces], refs[pieces : 2 * pieces], refs[2 * pieces :]
    x, y = place_ref[6], place_ref[7]
    own, other = own_ref[...].T, other_ref[...].T
    for k in range(pieces):
        total = jnp.dot(own, as_rows(mine[k][...]), preferred_element_type=F32)
        total += jnp.dot(other, as_rows(theirs[k][...]), preferred_element_type=F32)
        total = total.astype(BF16)
        if pieces > 1:
            place_block(total, place_ref[k], x, y, *outs)
        else:
            half = total.shape[0] // 2
            outs[0][...] = total[:half]
            outs[1][...] = total[half:]
    if pieces > 1:
        place_block(jnp.zeros_like(total), place_ref[pieces], x, y, *outs)


def weight_grad(place, own, other, mine, theirs):
    count, channels = own.shape
    columns = channels // 2
    pieces = len(mine)

    def part(array):
        if array.shape[-1] == columns:
            return whole(array.shape)
        lead = array.shape[:-1]
        return pl.BlockSpec((*lead, columns), lambda i, place: (0,) * len(lead) + (place[5],))

    extent = (channels // 2, columns)
    if pieces > 1:
        extent = (2, *extent)
    outs = 4 if pieces > 1 else 2
    return pl.pallas_call(
        functools.partial(weight_grad_body, pieces=pieces),
        grid_spec=pltpu.PrefetchScalarGridSpec(
            num_scalar_prefetch=1,
            grid=(1,),
            in_specs=[whole(own.shape)] * 2 + [part(piece) for piece in (*mine, *theirs)],
            out_specs=[whole(extent)] * outs,
        ),
        out_shape=[jax.ShapeDtypeStruct(extent, BF16)] * outs,
        compiler_params=params(),
        cost_estimate=cost(2 * pieces if pieces > 1 else 0.02),
        name="weight_grad" if pieces > 1 else "weight_grad_more",
    )(place, own, other, *mine, *theirs)


def merge_body(place_ref, *refs):
    x_keep, x_came, y_keep, y_came, upper, upper_came, lower, lower_came = refs[:8]
    top, to_y, bottom, to_x = refs[8:]
    block, x, y = place_ref[3], place_ref[6], place_ref[7]
    to_bx, to_by = block % 2 == x, block // 2 == y

    def both(a, b):
        return a[...].astype(F32) + b[...].astype(F32)

    for keep, came, index, more, more_came, here, there, stay, leave in (
        (x_keep, x_came, y, upper, upper_came, to_bx, to_by, top, to_y),
        (y_keep, y_came, x, lower, lower_came, to_by, to_bx, bottom, to_x),
    ):
        extra = jnp.where(here, both(more, more_came), 0.0)
        stay[...] = both(keep.at[index], came.at[index]) + jnp.where(there, extra, 0.0)
        rest = both(keep.at[1 - index], came.at[1 - index]) + jnp.where(there, 0.0, extra)
        leave[...] = rest.astype(BF16)


def merge(place, *arrays):
    rows, columns = arrays[0].shape[1:]
    pair = pl.BlockSpec((2, rows, columns), lambda i, place: (0, 0, 0))
    one = pl.BlockSpec((rows, columns), lambda i, place: (0, 0))
    kept = jax.ShapeDtypeStruct((rows, columns), F32)
    sent = jax.ShapeDtypeStruct((rows, columns), BF16)
    return pl.pallas_call(
        merge_body,
        grid_spec=pltpu.PrefetchScalarGridSpec(
            num_scalar_prefetch=1, grid=(1,), in_specs=[pair] * 4 + [one] * 4, out_specs=[one] * 4
        ),
        out_shape=[kept, sent, kept, sent],
        compiler_params=params(),
        cost_estimate=cost(2),
        name="merge",
    )(place, *arrays)


def finish_body(top, top_came, bottom, bottom_came, out):
    rows = top.shape[0]
    out[:rows] = top[...] + top_came[...].astype(F32)
    out[rows:] = bottom[...] + bottom_came[...].astype(F32)


def finish(top, top_came, bottom, bottom_came):
    rows, columns = top.shape
    one = pl.BlockSpec((rows, columns), lambda i: (0, 0))
    return pl.pallas_call(
        finish_body,
        grid=(1,),
        in_specs=[one] * 4,
        out_specs=pl.BlockSpec((2 * rows, columns), lambda i: (0, 0)),
        out_shape=jax.ShapeDtypeStruct((2 * rows, columns), F32),
        compiler_params=params(),
        cost_estimate=cost(2),
        name="finish",
    )(top, top_came, bottom, bottom_came)


OUTER = [(0, 1), (1, 0), (2, 3), (3, 2)]
INWARD = [(0, 1), (3, 2)]
OUTWARD = [(1, 0), (2, 3)]
MIDDLE = [(1, 2), (2, 1)]
OVER = [(0, 2), (2, 0), (1, 3), (3, 1)]
CROSS = [(0, 3), (3, 0), (1, 2), (2, 1)]


def along_chan(array, pairs):
    return lax.ppermute(array, "chan", pairs)


def along_dp(array, bit):
    return lax.ppermute(array, "dp", [(i, i ^ bit) for i in range(8)])


def gather_small(values):
    return [values] + [along_chan(values, pairs) for pairs in (OUTER, CROSS, OVER)]


def after(array, *others):
    return lax.optimization_barrier((array, *others))[0]


def places():
    rows = []
    for place in range(8):
        for z in range(4):
            order = [[0, 1, 2, 3], [1, 0, 2, 3], [2, 3, 1, 0], [3, 2, 1, 0]][z]
            rows.append(order + [int(z in (0, 3)), place % 2, place // 2 % 2, place // 4])
    return np.array(rows, np.int32)


def on_line(hidden, conv_weight, se_down, se_up, proj_weight, grad_out):
    hidden, own = to_cells(hidden), to_cells(grad_out)
    shape = own.shape
    channels = shape[3]
    extent = (own.size // channels, channels)
    role = jnp.asarray(places())[lax.axis_index("dp") * 4 + lax.axis_index("chan")]

    outer = along_chan(own, OUTER)
    middle = along_chan(own, MIDDLE)
    furthest = jnp.where(lax.axis_index("chan") < 2, 3, 0)
    w_far = lax.dynamic_slice_in_dim(proj_weight, furthest * channels, channels, axis=1)
    convolved, act, terms = conv_forward(after(hidden, w_far), conv_weight, se_down)
    terms = gather_small(terms)
    far = along_chan(after(outer, *terms), MIDDLE)
    gating, excite_pre, scaled, p_fourth, send = scale(role, act, terms, se_up, w_far, middle)
    came = along_chan(send, OUTER)
    other = along_dp(scaled, 1)
    theirs = [along_dp(piece, 1) for piece in (own, outer)]
    p_own, p_outer, p_third = project(role, 3, scaled, proj_weight)

    came = after(came, p_own)
    third, to_far = between(second_body, [extent] * 2, role, came, send, p_fourth)
    crossed = along_chan(to_far, MIDDLE)
    (send_far,) = between(
        far_body, [extent], role, p_third, after(far, to_far), micros=FAR_COST
    )
    came_far = along_chan(send_far, OUTER)
    theirs.append(along_dp(third, 1))
    pieces = [own, outer, after(third, send_far)]
    x_send, x_keep, y_send, y_keep = weight_grad(role, scaled, other, pieces, theirs)
    x_came, y_came = along_dp(x_send, 2), along_dp(y_send, 4)
    (begun,) = input_grad(role, 0, [own, outer, after(third, y_send)], proj_weight)

    crossed = after(crossed, begun)
    (send,) = between(outer_body, [extent], role, crossed, p_outer, micros=TURN_COST)
    came = along_chan(send, OUTER)
    half = (extent[0], channels // 2)
    fourth, to_mid, give = between(
        third_body, [extent] * 2 + [half], role, after(came_far, send), send_far, p_third
    )
    crossed = along_chan(to_mid, MIDDLE)
    upper, lower = weight_grad(role, scaled, other, [fourth], [along_dp(give, 1)])
    upper_came, lower_came = along_dp(upper, 2), along_dp(lower, 4)
    fourth, x_came, y_came = lax.optimization_barrier((fourth, x_came, y_came, lower))[:3]
    scaled_grad, terms = input_grad(
        role, 3, [fourth], proj_weight, begun, act, gating, se_up
    )
    part, slope = conv_grad_terms(scaled_grad, gating, convolved, shape[0] * shape[1])
    upper_came = after(upper_came, terms, part)
    top, to_y, bottom, to_x = merge(
        role, x_keep, x_came, y_keep, y_came, upper, upper_came, lower, lower_came
    )
    terms, came, crossed = lax.optimization_barrier((terms, came, crossed, to_x))[:3]
    terms = gather_small(terms)
    (projected,) = between(fourth_body, [shape], role, p_own, came, crossed)
    terms[0] = after(terms[0], projected)
    grad_hidden = conv_backward(part, slope, terms, excite_pre, se_down, conv_weight, shape)
    grad_proj = finish(top, along_dp(to_y, 4), bottom, along_dp(to_x, 2))
    return (from_cells(projected), from_cells(grad_hidden), grad_proj)


def on_any(hidden, conv_weight, se_down, se_up, proj_weight, grad_out):
    hidden, pieces = to_cells(hidden), to_cells(grad_out)
    shape = hidden.shape
    images = shape[2]
    convolved, act, terms = conv_forward(hidden, conv_weight, se_down)
    excite_pre = lax.psum(terms, "chan")
    nothing = jnp.zeros_like(excite_pre)
    gating = jax.nn.sigmoid(jnp.dot(jax.nn.silu(excite_pre), se_up.astype(F32), precision=HIGHEST))
    act_float = act.astype(F32)
    scaled = (act_float * per_row(gating, act.shape[0])).astype(BF16)
    terms = jnp.dot(scaled, proj_weight, preferred_element_type=F32).astype(BF16)
    projected = lax.psum_scatter(terms, "chan", scatter_dimension=1, tiled=True)
    pieces = lax.all_gather(as_rows(pieces), "chan", axis=1, tiled=True)
    scaled_grad = lax.dot_general(
        pieces, proj_weight, (((1,), (1,)), ((), ())), preferred_element_type=F32
    )
    terms = lax.dot_general(scaled, pieces, (((0,), (0,)), ((), ())), preferred_element_type=F32)
    grad_proj = lax.psum_scatter(terms, "dp", scatter_dimension=1, tiled=True)
    gate_grad = image_sum(scaled_grad * act_float, images)
    pre_grad = gate_grad * gating * (1.0 - gating)
    excite_sum = lax.psum(jnp.dot(pre_grad, se_up.astype(F32).T, precision=HIGHEST), "chan")
    terms = [excite_sum] + [nothing] * 3
    part, slope = conv_grad_terms(scaled_grad, gating, convolved, shape[0] * shape[1])
    grad_hidden = conv_backward(part, slope, terms, excite_pre, se_down, conv_weight, shape)
    return (from_cells(projected.reshape(shape)), from_cells(grad_hidden), grad_proj)


def solution(mesh):
    in_specs = (
        P("dp", None, None, "chan"),
        P(None, None, None, "chan"),
        P("chan", None),
        P(None, "chan"),
        P("chan", None),
        P("dp", None, None, "chan"),
    )
    out_specs = (P("dp", None, None, "chan"), P("dp", None, None, "chan"), P("chan", "dp"))
    on_device = on_line if (mesh.shape["dp"], mesh.shape["chan"]) == (8, 4) else on_any
    return jax.shard_map(
        on_device, mesh=mesh, in_specs=in_specs, out_specs=out_specs, check_vma=False
    )
```

```python
import functools

import jax
import jax.numpy as jnp
import numpy as np
from jax import lax
from jax.experimental import pallas as pl
from jax.experimental.pallas import tpu as pltpu
from jax.sharding import PartitionSpec as P

LANES = 256
F32 = jnp.float32
BF16 = jnp.bfloat16
HIGHEST = lax.Precision.HIGHEST


def params(mebibytes=20):
    return pltpu.CompilerParams(vmem_limit_bytes=mebibytes * 1024 * 1024)


SCALE = 0.3
CONV_MIB = 20
FAR_COST = 10
TURN_COST = 1


def cost(micros):
    return pl.CostEstimate(
        flops=int(micros * SCALE * 1.15e9), bytes_accessed=1, transcendentals=0
    )


def sum_of(refs):
    own, near, across, over = (ref[...] for ref in refs)
    return (own + near) + (across + over)


def exact_dot(values, weight, dims):
    high = values.astype(BF16).astype(F32)
    rest = values - high
    middle = rest.astype(BF16).astype(F32)
    count = values.shape[0]
    terms = [high, middle, rest - middle, jnp.zeros_like(values)]
    stacked = jnp.concatenate(terms, axis=0).astype(BF16)
    if dims == ((1,), (1,)):
        out = lax.dot_general(weight, stacked, (dims, ((), ())), preferred_element_type=F32).T
    else:
        out = lax.dot_general(stacked, weight, (dims, ((), ())), preferred_element_type=F32)
    return out[:count] + out[count : 2 * count] + out[2 * count : 3 * count]


def silu_grad(values):
    logistic = jax.nn.sigmoid(values)
    return logistic * (1.0 + values * (1.0 - logistic))


def to_cells(images):
    return jnp.transpose(images, (1, 2, 0, 3))


def from_cells(cells):
    return jnp.transpose(cells, (2, 0, 1, 3))


def as_rows(values):
    return values.reshape(-1, values.shape[-1])


def whole(shape):
    return pl.BlockSpec(shape, lambda *_: (0,) * len(shape))


def per_row(values, rows):
    tiled = jnp.concatenate([values] * (8 // values.shape[0]), axis=0)
    return jnp.broadcast_to(tiled[None], (rows // 8, 8, values.shape[1])).reshape(rows, -1)


def image_sum(values, images):
    folded = values.reshape(-1, 8, values.shape[1]).sum(axis=0)
    total = folded[:images]
    for start in range(images, 8, images):
        total = total + folded[start : start + images]
    return total


def convolve(rows_ref, pad_ref, weight_ref, height, width, images, turn):
    line, unit = width * images, 16 * images
    group = weight_ref.shape[2]
    pad_ref[...] = jnp.zeros_like(pad_ref)
    for h in range(height):
        pad_ref[pl.ds(8 + (h + 1) * unit + images, line), :] = rows_ref[pl.ds(h * line, line), :]
    row_group = lax.broadcasted_iota(jnp.int32, (LANES, LANES), 0) // group
    col_group = lax.broadcasted_iota(jnp.int32, (LANES, LANES), 1) // group
    mask = (row_group == col_group).astype(F32).astype(BF16)
    cells, taps = [], []
    for dw in range(3):
        shifted = pad_ref[pl.ds(8 + images * (dw - 1), (height + 2) * unit), :].astype(BF16)
        for dh in range(3):
            tap = weight_ref[2 - dh, 2 - dw] if turn else weight_ref[dh, dw]
            taps.append(jnp.concatenate([tap] * (LANES // group), axis=0) * mask)
            cells.append(shifted[dh * unit : (dh + height) * unit])
    total = lax.dot_general(
        jnp.concatenate(cells, axis=1),
        jnp.concatenate(taps, axis=1 if turn else 0),
        (((1,), (1 if turn else 0,)), ((), ())),
        preferred_element_type=F32,
    )
    pad_ref[pl.ds(0, height * unit), :] = total
    for h in range(height):
        rows_ref[pl.ds(h * line, line), :] = pad_ref[pl.ds(h * unit + images, line), :]


HBM = pl.BlockSpec(memory_space=pltpu.HBM)
HERE = pl.BlockSpec(memory_space=pltpu.VMEM)


def lanes_of(i):
    return pl.ds(i * LANES, LANES)


def fetch(source, target, sem):
    copy = pltpu.make_async_copy(source, target, sem)
    copy.start()
    return copy


def conv_forward_body(
    x_ref,
    w_ref,
    down_ref,
    conv_hbm,
    act_ref,
    pre_ref,
    conv_buf,
    rows_ref,
    pad_ref,
    sems,
    *,
    height,
    width,
    images,
):
    blocks = act_ref.shape[1] // LANES
    means, outs = [], []
    for i in range(blocks):
        rows = rows_ref.at[i]
        rows[...] = as_rows(x_ref[:, :, :, lanes_of(i)]).astype(F32)
        part = w_ref.at[:, :, :, lanes_of(i)]
        convolve(rows, pad_ref.at[i], part, height, width, images, False)
        conv = rows[...]
        conv_buf[i] = conv
        outs.append(fetch(conv_buf.at[i], conv_hbm.at[:, lanes_of(i)], sems.at[i]))
        act = (conv * jax.nn.sigmoid(conv)).astype(BF16)
        act_ref[:, lanes_of(i)] = act
        means.append(image_sum(act.astype(F32), images) / (height * width))
    pre_ref[...] = exact_dot(jnp.concatenate(means, axis=1), down_ref[...], ((1,), (0,)))
    for out in outs:
        out.wait()


def conv_forward(cells, weight, down):
    height, width, images, channels = cells.shape
    count, inner = height * width * images, down.shape[1]
    blocks = channels // LANES
    return pl.pallas_call(
        functools.partial(conv_forward_body, height=height, width=width, images=images),
        in_specs=[HERE] * 3,
        out_specs=[HBM, HERE, HERE],
        out_shape=[
            jax.ShapeDtypeStruct((count, channels), F32),
            jax.ShapeDtypeStruct((count, channels), BF16),
            jax.ShapeDtypeStruct((images, inner), F32),
        ],
        scratch_shapes=[
            pltpu.VMEM((blocks, count, LANES), F32),
            pltpu.VMEM((blocks, count, LANES), F32),
            pltpu.VMEM((blocks, 16 + (height + 2) * 16 * images, LANES), F32),
            pltpu.SemaphoreType.DMA((blocks,)),
        ],
        compiler_params=params(CONV_MIB),
        cost_estimate=cost(3),
        name="conv_forward",
    )(cells, weight, down)


def conv_grad_body(grad_ref, gate_ref, conv_ref, part_ref, slope_ref, *, cells):
    slope = silu_grad(conv_ref[...])
    part_ref[...] = grad_ref[...] * per_row(gate_ref[...], conv_ref.shape[0]) * slope
    slope_ref[...] = slope / cells


def conv_grad_terms(scaled_grad, gating, convolved, cells):
    array = jax.ShapeDtypeStruct(convolved.shape, F32)
    return pl.pallas_call(
        functools.partial(conv_grad_body, cells=cells),
        grid=(1,),
        in_specs=[whole(a.shape) for a in (scaled_grad, gating, convolved)],
        out_specs=[whole(array.shape)] * 2,
        out_shape=[array] * 2,
        compiler_params=params(),
        cost_estimate=cost(0.02),
        name="conv_grad",
    )(scaled_grad, gating, convolved)


def conv_backward_body(
    part_ref,
    slope_ref,
    own_ref,
    near_ref,
    across_ref,
    over_ref,
    pre_ref,
    down_ref,
    w_ref,
    out_hbm,
    out_buf,
    rows_ref,
    pad_ref,
    sems,
    *,
    height,
    width,
    images,
):
    count, channels = part_ref.shape
    blocks = channels // LANES
    excite_sum = sum_of((own_ref, near_ref, across_ref, over_ref))
    excite_grad = excite_sum * silu_grad(pre_ref[...])
    squeeze_grad = exact_dot(excite_grad, down_ref[...], ((1,), (1,)))
    outs = []
    for i in range(blocks):
        rows = rows_ref.at[i]
        squeeze = per_row(squeeze_grad[:, i * LANES : (i + 1) * LANES], count)
        rows[...] = part_ref[:, lanes_of(i)] + squeeze * slope_ref[:, lanes_of(i)]
        part = w_ref.at[:, :, :, lanes_of(i)]
        convolve(rows, pad_ref.at[i], part, height, width, images, True)
        part = rows[...].astype(BF16).reshape(height, width, images, LANES)
        out_buf[:, :, :, lanes_of(i)] = part
        target = out_hbm.at[:, :, :, lanes_of(i)]
        outs.append(fetch(out_buf.at[:, :, :, lanes_of(i)], target, sems.at[i]))
    for out in outs:
        out.wait()


def conv_backward(part, slope, terms, excite_pre, down, weight, shape):
    height, width, images, channels = shape
    count = part.shape[0]
    blocks = channels // LANES
    return pl.pallas_call(
        functools.partial(conv_backward_body, height=height, width=width, images=images),
        in_specs=[HERE] * 9,
        out_specs=HBM,
        out_shape=jax.ShapeDtypeStruct(shape, BF16),
        scratch_shapes=[
            pltpu.VMEM(shape, BF16),
            pltpu.VMEM((blocks, count, LANES), F32),
            pltpu.VMEM((blocks, 16 + (height + 2) * 16 * images, LANES), F32),
            pltpu.SemaphoreType.DMA((blocks,)),
        ],
        compiler_params=params(),
        cost_estimate=cost(3),
        name="conv_backward",
    )(part, slope, *terms, excite_pre, down, weight)


def block_of(weight_ref, block, width):
    return weight_ref.at[:, pl.ds(pl.multiple_of(block * width, width), width)]


def scale_body(
    role_ref,
    act_ref,
    own_ref,
    near_ref,
    across_ref,
    over_ref,
    up_ref,
    w_ref,
    middle_hbm,
    gate_ref,
    pre_ref,
    scaled_ref,
    far_ref,
    send_ref,
    middle_buf,
    sem,
):
    middle_copy = fetch(middle_hbm, middle_buf, sem)
    pre = sum_of((own_ref, near_ref, across_ref, over_ref))
    pre_ref[...] = pre
    excited = pre * jax.nn.sigmoid(pre)
    gate_ref[...] = jax.nn.sigmoid(exact_dot(excited, up_ref[...], ((1,), (0,))))
    gate = per_row(gate_ref[...], act_ref.shape[0])
    scaled_ref[...] = (act_ref[...].astype(F32) * gate).astype(BF16)
    far = jnp.dot(scaled_ref[...], w_ref[...], preferred_element_type=F32).astype(BF16)
    far_ref[...] = far
    middle_copy.wait()

    @pl.when(role_ref[4] == 1)
    def _():
        send_ref[...] = far

    @pl.when(role_ref[4] == 0)
    def _():
        send_ref[...] = as_rows(middle_buf[...])


def scale(role, act, terms, up, w_far, middle):
    count, channels = act.shape
    gates = (terms[0].shape[0], channels)
    array = jax.ShapeDtypeStruct((count, channels), BF16)
    return pl.pallas_call(
        scale_body,
        in_specs=[pl.BlockSpec(memory_space=pltpu.SMEM)] + [HERE] * 7 + [HBM],
        out_specs=[HERE] * 5,
        out_shape=[
            jax.ShapeDtypeStruct(gates, F32),
            jax.ShapeDtypeStruct(terms[0].shape, F32),
        ]
        + [array] * 3,
        scratch_shapes=[
            pltpu.VMEM(middle.shape, BF16),
            pltpu.SemaphoreType.DMA,
        ],
        compiler_params=params(),
        cost_estimate=cost(3),
        name="scale",
    )(role, act, *terms, up, w_far, middle)


def project_body(order_ref, scaled_ref, w_ref, *outs):
    for k, out in enumerate(outs):
        block = block_of(w_ref, order_ref[k], scaled_ref.shape[1])
        part = jnp.dot(scaled_ref[...], block[...], preferred_element_type=F32)
        out[...] = part.astype(BF16)


def project(order, parts, scaled, weight):
    count, channels = scaled.shape
    array = jax.ShapeDtypeStruct((count, channels), BF16)
    return pl.pallas_call(
        project_body,
        in_specs=[pl.BlockSpec(memory_space=pltpu.SMEM), HERE, HERE],
        out_specs=[HERE] * parts,
        out_shape=[array] * parts,
        compiler_params=params(),
        cost_estimate=cost(3),
        name="project",
    )(order, scaled, weight)


def sum_into(ref, a, b):
    ref[...] = (a[...].astype(F32) + b[...].astype(F32)).astype(BF16)


def choose(role_ref, ref, at_end, else_):
    @pl.when(role_ref[4] == 1)
    def _():
        ref[...] = as_rows(at_end[...])

    @pl.when(role_ref[4] == 0)
    def _():
        ref[...] = as_rows(else_[...])


def far_body(role_ref, p_third, far, send):
    choose(role_ref, send, p_third, far)


def second_body(role_ref, came, held, p_fourth, third, to_far):
    sum_into(to_far, p_fourth, came)
    choose(role_ref, third, came, held)


def third_body(role_ref, came, held, p_third, fourth, to_mid, give):
    sum_into(to_mid, p_third, came)
    choose(role_ref, fourth, came, held)
    half = give.shape[1]
    give[...] = fourth[:, pl.ds(pl.multiple_of((1 - role_ref[5]) * half, half), half)]


def outer_body(role_ref, crossed, p_outer, send):
    @pl.when(role_ref[4] == 1)
    def _():
        send[...] = p_outer[...]

    @pl.when(role_ref[4] == 0)
    def _():
        sum_into(send, p_outer, crossed)


def fourth_body(role_ref, p_own, came, crossed, total):
    at_end = role_ref[4] == 1
    near = p_own[...].astype(F32) + came[...].astype(F32)

    @pl.when(at_end)
    def _():
        total[...] = near.astype(BF16).reshape(total.shape)

    @pl.when(jnp.logical_not(at_end))
    def _():
        total[...] = (near + crossed[...].astype(F32)).astype(BF16).reshape(total.shape)


def between(body, extents, role, *arrays, micros=0.02):
    return pl.pallas_call(
        body,
        grid=(1,),
        in_specs=[pl.BlockSpec(memory_space=pltpu.SMEM)] + [whole(a.shape) for a in arrays],
        out_specs=[whole(extent) for extent in extents],
        out_shape=[jax.ShapeDtypeStruct(extent, BF16) for extent in extents],
        compiler_params=params(),
        cost_estimate=cost(micros),
        name=body.__name__.replace("_body", "_turn"),
    )(role, *arrays)


def input_grad_body(role_ref, *refs, first, pieces, started, last, images):
    piece_refs, w_hbm, refs = refs[:pieces], refs[pieces], refs[pieces + 1 :]
    if started:
        start_ref, refs = refs[0], refs[1:]
    if last:
        act_ref, gate_ref, up_hbm, out_ref, excite_ref, w_buf, sems, up_buf = refs[:8]
    else:
        out_ref, w_buf, sems = refs[:3]
    piece_bufs = refs[-pieces:]
    width = out_ref.shape[1]
    copies = []
    for k, piece_ref in enumerate(piece_refs):
        block = block_of(w_hbm, role_ref[first + k], width)
        copies.append(
            (
                fetch(piece_ref, piece_bufs[k], sems.at[2 * k]),
                fetch(block, w_buf.at[k], sems.at[2 * k + 1]),
            )
        )
    if last:
        up_copy = fetch(up_hbm, up_buf, sems.at[2 * pieces])
    for k in range(pieces):
        for copy in copies[k]:
            copy.wait()
        part = lax.dot_general(
            as_rows(piece_bufs[k][...]),
            w_buf[k],
            (((1,), (1,)), ((), ())),
            preferred_element_type=F32,
        )
        if k > 0:
            part = out_ref[...] + part
        elif started:
            part = start_ref[...] + part
        out_ref[...] = part
    if last:
        gating = gate_ref[...]
        gate_grad = image_sum(out_ref[...] * act_ref[...].astype(F32), images)
        pre_grad = gate_grad * gating * (1.0 - gating)
        up_copy.wait()
        excite_ref[...] = exact_dot(pre_grad, up_buf[...], ((1,), (1,)))


def input_grad(role, first, pieces, weight, start=None, act=None, gating=None, up=None):
    channels = weight.shape[0]
    count = pieces[0].size // channels
    images = 1 if gating is None else gating.shape[0]
    started, last = start is not None, act is not None
    operands = list(pieces) + [weight]
    in_specs = [pl.BlockSpec(memory_space=pltpu.SMEM)] + [HBM] * (len(pieces) + 1)
    out_shape = [jax.ShapeDtypeStruct((count, channels), F32)]
    scratch = [
        pltpu.VMEM((len(pieces), channels, channels), BF16),
        pltpu.SemaphoreType.DMA((2 * len(pieces) + 1,)),
    ]
    if started:
        operands.append(start)
        in_specs.append(HERE)
    if last:
        operands += [act, gating, up]
        in_specs += [HERE, HERE, HBM]
        out_shape.append(jax.ShapeDtypeStruct((images, up.shape[0]), F32))
        scratch.append(pltpu.VMEM(up.shape, BF16))
    scratch += [pltpu.VMEM(piece.shape, BF16) for piece in pieces]
    return pl.pallas_call(
        functools.partial(
            input_grad_body,
            first=first,
            pieces=len(pieces),
            started=started,
            last=last,
            images=images,
        ),
        in_specs=in_specs,
        out_specs=[HERE] * len(out_shape),
        out_shape=out_shape,
        scratch_shapes=scratch,
        compiler_params=params(),
        cost_estimate=cost(10 if last else 0.02),
        name="input_grad_last" if last else "input_grad",
    )(role, *operands)


def place_block(total, block, x, y, x_send, x_keep, y_send, y_keep):
    half = total.shape[0] // 2
    to_x, to_y = block % 2, block // 2

    @pl.when(to_x != x)
    def _():
        x_send[to_y] = total[:half]

    @pl.when(to_x == x)
    def _():
        x_keep[to_y] = total[:half]

    @pl.when(to_y != y)
    def _():
        y_send[to_x] = total[half:]

    @pl.when(to_y == y)
    def _():
        y_keep[to_x] = total[half:]


def weight_grad_body(place_ref, own_ref, other_ref, *refs, pieces):
    mine, theirs, outs = refs[:pieces], refs[pieces : 2 * pieces], refs[2 * pieces :]
    x, y = place_ref[6], place_ref[7]
    own, other = own_ref[...].T, other_ref[...].T
    for k in range(pieces):
        total = jnp.dot(own, as_rows(mine[k][...]), preferred_element_type=F32)
        total += jnp.dot(other, as_rows(theirs[k][...]), preferred_element_type=F32)
        total = total.astype(BF16)
        if pieces > 1:
            place_block(total, place_ref[k], x, y, *outs)
        else:
            half = total.shape[0] // 2
            outs[0][...] = total[:half]
            outs[1][...] = total[half:]
    if pieces > 1:
        place_block(jnp.zeros_like(total), place_ref[pieces], x, y, *outs)


def weight_grad(place, own, other, mine, theirs):
    count, channels = own.shape
    columns = channels // 2
    pieces = len(mine)

    def part(array):
        if array.shape[-1] == columns:
            return whole(array.shape)
        lead = array.shape[:-1]
        return pl.BlockSpec((*lead, columns), lambda i, place: (0,) * len(lead) + (place[5],))

    extent = (channels // 2, columns)
    if pieces > 1:
        extent = (2, *extent)
    outs = 4 if pieces > 1 else 2
    return pl.pallas_call(
        functools.partial(weight_grad_body, pieces=pieces),
        grid_spec=pltpu.PrefetchScalarGridSpec(
            num_scalar_prefetch=1,
            grid=(1,),
            in_specs=[whole(own.shape)] * 2 + [part(piece) for piece in (*mine, *theirs)],
            out_specs=[whole(extent)] * outs,
        ),
        out_shape=[jax.ShapeDtypeStruct(extent, BF16)] * outs,
        compiler_params=params(),
        cost_estimate=cost(2 * pieces if pieces > 1 else 0.02),
        name="weight_grad" if pieces > 1 else "weight_grad_more",
    )(place, own, other, *mine, *theirs)


def merge_body(place_ref, *refs):
    x_keep, x_came, y_keep, y_came, upper, upper_came, lower, lower_came = refs[:8]
    top, to_y, bottom, to_x = refs[8:]
    block, x, y = place_ref[3], place_ref[6], place_ref[7]
    to_bx, to_by = block % 2 == x, block // 2 == y

    def both(a, b):
        return a[...].astype(F32) + b[...].astype(F32)

    for keep, came, index, more, more_came, here, there, stay, leave in (
        (x_keep, x_came, y, upper, upper_came, to_bx, to_by, top, to_y),
        (y_keep, y_came, x, lower, lower_came, to_by, to_bx, bottom, to_x),
    ):
        extra = jnp.where(here, both(more, more_came), 0.0)
        stay[...] = both(keep.at[index], came.at[index]) + jnp.where(there, extra, 0.0)
        rest = both(keep.at[1 - index], came.at[1 - index]) + jnp.where(there, 0.0, extra)
        leave[...] = rest.astype(BF16)


def merge(place, *arrays):
    rows, columns = arrays[0].shape[1:]
    pair = pl.BlockSpec((2, rows, columns), lambda i, place: (0, 0, 0))
    one = pl.BlockSpec((rows, columns), lambda i, place: (0, 0))
    kept = jax.ShapeDtypeStruct((rows, columns), F32)
    sent = jax.ShapeDtypeStruct((rows, columns), BF16)
    return pl.pallas_call(
        merge_body,
        grid_spec=pltpu.PrefetchScalarGridSpec(
            num_scalar_prefetch=1, grid=(1,), in_specs=[pair] * 4 + [one] * 4, out_specs=[one] * 4
        ),
        out_shape=[kept, sent, kept, sent],
        compiler_params=params(),
        cost_estimate=cost(2),
        name="merge",
    )(place, *arrays)


def finish_body(top, top_came, bottom, bottom_came, out):
    rows = top.shape[0]
    out[:rows] = top[...] + top_came[...].astype(F32)
    out[rows:] = bottom[...] + bottom_came[...].astype(F32)


def finish(top, top_came, bottom, bottom_came):
    rows, columns = top.shape
    one = pl.BlockSpec((rows, columns), lambda i: (0, 0))
    return pl.pallas_call(
        finish_body,
        grid=(1,),
        in_specs=[one] * 4,
        out_specs=pl.BlockSpec((2 * rows, columns), lambda i: (0, 0)),
        out_shape=jax.ShapeDtypeStruct((2 * rows, columns), F32),
        compiler_params=params(),
        cost_estimate=cost(2),
        name="finish",
    )(top, top_came, bottom, bottom_came)


OUTER = [(0, 1), (1, 0), (2, 3), (3, 2)]
INWARD = [(0, 1), (3, 2)]
OUTWARD = [(1, 0), (2, 3)]
MIDDLE = [(1, 2), (2, 1)]
OVER = [(0, 2), (2, 0), (1, 3), (3, 1)]
CROSS = [(0, 3), (3, 0), (1, 2), (2, 1)]


def along_chan(array, pairs):
    return lax.ppermute(array, "chan", pairs)


def along_dp(array, bit):
    return lax.ppermute(array, "dp", [(i, i ^ bit) for i in range(8)])


def gather_small(values):
    return [values] + [along_chan(values, pairs) for pairs in (OUTER, CROSS, OVER)]


def after(array, *others):
    return lax.optimization_barrier((array, *others))[0]


def places():
    rows = []
    for place in range(8):
        for z in range(4):
            order = [[0, 1, 2, 3], [1, 0, 2, 3], [2, 3, 1, 0], [3, 2, 1, 0]][z]
            rows.append(order + [int(z in (0, 3)), place % 2, place // 2 % 2, place // 4])
    return np.array(rows, np.int32)


def on_line(hidden, conv_weight, se_down, se_up, proj_weight, grad_out):
    hidden, own = to_cells(hidden), to_cells(grad_out)
    shape = own.shape
    channels = shape[3]
    extent = (own.size // channels, channels)
    role = jnp.asarray(places())[lax.axis_index("dp") * 4 + lax.axis_index("chan")]

    outer = along_chan(own, OUTER)
    middle = along_chan(own, MIDDLE)
    furthest = jnp.where(lax.axis_index("chan") < 2, 3, 0)
    w_far = lax.dynamic_slice_in_dim(proj_weight, furthest * channels, channels, axis=1)
    convolved, act, terms = conv_forward(after(hidden, w_far), conv_weight, se_down)
    terms = gather_small(terms)
    far = along_chan(after(outer, *terms), MIDDLE)
    gating, excite_pre, scaled, p_fourth, send = scale(role, act, terms, se_up, w_far, middle)
    came = along_chan(send, OUTER)
    other = along_dp(scaled, 1)
    theirs = [along_dp(piece, 1) for piece in (own, outer)]
    p_own, p_outer, p_third = project(role, 3, scaled, proj_weight)

    came = after(came, p_own)
    third, to_far = between(second_body, [extent] * 2, role, came, send, p_fourth)
    crossed = along_chan(to_far, MIDDLE)
    (send_far,) = between(
        far_body, [extent], role, p_third, after(far, to_far), micros=FAR_COST
    )
    came_far = along_chan(send_far, OUTER)
    theirs.append(along_dp(third, 1))
    pieces = [own, outer, after(third, send_far)]
    x_send, x_keep, y_send, y_keep = weight_grad(role, scaled, other, pieces, theirs)
    x_came, y_came = along_dp(x_send, 2), along_dp(y_send, 4)
    (begun,) = input_grad(role, 0, [own, outer, after(third, y_send)], proj_weight)

    crossed = after(crossed, begun)
    (send,) = between(outer_body, [extent], role, crossed, p_outer, micros=TURN_COST)
    came = along_chan(send, OUTER)
    half = (extent[0], channels // 2)
    fourth, to_mid, give = between(
        third_body, [extent] * 2 + [half], role, after(came_far, send), send_far, p_third
    )
    crossed = along_chan(to_mid, MIDDLE)
    upper, lower = weight_grad(role, scaled, other, [fourth], [along_dp(give, 1)])
    upper_came, lower_came = along_dp(upper, 2), along_dp(lower, 4)
    fourth, x_came, y_came = lax.optimization_barrier((fourth, x_came, y_came, lower))[:3]
    scaled_grad, terms = input_grad(
        role, 3, [fourth], proj_weight, begun, act, gating, se_up
    )
    part, slope = conv_grad_terms(scaled_grad, gating, convolved, shape[0] * shape[1])
    upper_came = after(upper_came, terms, part)
    top, to_y, bottom, to_x = merge(
        role, x_keep, x_came, y_keep, y_came, upper, upper_came, lower, lower_came
    )
    terms, came, crossed = lax.optimization_barrier((terms, came, crossed, to_x))[:3]
    terms = gather_small(terms)
    (projected,) = between(fourth_body, [shape], role, p_own, came, crossed)
    terms[0] = after(terms[0], projected)
    grad_hidden = conv_backward(part, slope, terms, excite_pre, se_down, conv_weight, shape)
    grad_proj = finish(top, along_dp(to_y, 4), bottom, along_dp(to_x, 2))
    return (from_cells(projected), from_cells(grad_hidden), grad_proj)


def on_any(hidden, conv_weight, se_down, se_up, proj_weight, grad_out):
    hidden, pieces = to_cells(hidden), to_cells(grad_out)
    shape = hidden.shape
    images = shape[2]
    convolved, act, terms = conv_forward(hidden, conv_weight, se_down)
    excite_pre = lax.psum(terms, "chan")
    nothing = jnp.zeros_like(excite_pre)
    gating = jax.nn.sigmoid(jnp.dot(jax.nn.silu(excite_pre), se_up.astype(F32), precision=HIGHEST))
    act_float = act.astype(F32)
    scaled = (act_float * per_row(gating, act.shape[0])).astype(BF16)
    terms = jnp.dot(scaled, proj_weight, preferred_element_type=F32).astype(BF16)
    projected = lax.psum_scatter(terms, "chan", scatter_dimension=1, tiled=True)
    pieces = lax.all_gather(as_rows(pieces), "chan", axis=1, tiled=True)
    scaled_grad = lax.dot_general(
        pieces, proj_weight, (((1,), (1,)), ((), ())), preferred_element_type=F32
    )
    terms = lax.dot_general(scaled, pieces, (((0,), (0,)), ((), ())), preferred_element_type=F32)
    grad_proj = lax.psum_scatter(terms, "dp", scatter_dimension=1, tiled=True)
    gate_grad = image_sum(scaled_grad * act_float, images)
    pre_grad = gate_grad * gating * (1.0 - gating)
    excite_sum = lax.psum(jnp.dot(pre_grad, se_up.astype(F32).T, precision=HIGHEST), "chan")
    terms = [excite_sum] + [nothing] * 3
    part, slope = conv_grad_terms(scaled_grad, gating, convolved, shape[0] * shape[1])
    grad_hidden = conv_backward(part, slope, terms, excite_pre, se_down, conv_weight, shape)
    return (from_cells(projected.reshape(shape)), from_cells(grad_hidden), grad_proj)


def solution(mesh):
    in_specs = (
        P("dp", None, None, "chan"),
        P(None, None, None, "chan"),
        P("chan", None),
        P(None, "chan"),
        P("chan", None),
        P("dp", None, None, "chan"),
    )
    out_specs = (P("dp", None, None, "chan"), P("dp", None, None, "chan"), P("chan", "dp"))
    on_device = on_line if (mesh.shape["dp"], mesh.shape["chan"]) == (8, 4) else on_any
    return jax.shard_map(
        on_device, mesh=mesh, in_specs=in_specs, out_specs=out_specs, check_vma=False
    )
```

```python
import functools

import jax
import jax.numpy as jnp
import numpy as np
from jax import lax
from jax.experimental import pallas as pl
from jax.experimental.pallas import tpu as pltpu
from jax.sharding import PartitionSpec as P

LANES = 256
F32 = jnp.float32
BF16 = jnp.bfloat16
HIGHEST = lax.Precision.HIGHEST


def params(mebibytes=20):
    return pltpu.CompilerParams(vmem_limit_bytes=mebibytes * 1024 * 1024)


SCALE = 0.3
CONV_MIB = 20
FAR_COST = 10
TURN_COST = 1


def cost(micros):
    return pl.CostEstimate(
        flops=int(micros * SCALE * 1.15e9), bytes_accessed=1, transcendentals=0
    )


def sum_of(refs):
    own, near, across, over = (ref[...] for ref in refs)
    return (own + near) + (across + over)


def exact_dot(values, weight, dims):
    high = values.astype(BF16).astype(F32)
    rest = values - high
    middle = rest.astype(BF16).astype(F32)
    count = values.shape[0]
    terms = [high, middle, rest - middle, jnp.zeros_like(values)]
    stacked = jnp.concatenate(terms, axis=0).astype(BF16)
    if dims == ((1,), (1,)):
        out = lax.dot_general(weight, stacked, (dims, ((), ())), preferred_element_type=F32).T
    else:
        out = lax.dot_general(stacked, weight, (dims, ((), ())), preferred_element_type=F32)
    return out[:count] + out[count : 2 * count] + out[2 * count : 3 * count]


def silu_grad(values):
    logistic = jax.nn.sigmoid(values)
    return logistic * (1.0 + values * (1.0 - logistic))


def to_cells(images):
    return jnp.transpose(images, (1, 2, 0, 3))


def from_cells(cells):
    return jnp.transpose(cells, (2, 0, 1, 3))


def as_rows(values):
    return values.reshape(-1, values.shape[-1])


def whole(shape):
    return pl.BlockSpec(shape, lambda *_: (0,) * len(shape))


def per_row(values, rows):
    tiled = jnp.concatenate([values] * (8 // values.shape[0]), axis=0)
    return jnp.broadcast_to(tiled[None], (rows // 8, 8, values.shape[1])).reshape(rows, -1)


def image_sum(values, images):
    folded = values.reshape(-1, 8, values.shape[1]).sum(axis=0)
    total = folded[:images]
    for start in range(images, 8, images):
        total = total + folded[start : start + images]
    return total


def convolve(rows_ref, pad_ref, weight_ref, height, width, images, turn):
    line, unit = width * images, 16 * images
    group = weight_ref.shape[2]
    pad_ref[...] = jnp.zeros_like(pad_ref)
    for h in range(height):
        pad_ref[pl.ds(8 + (h + 1) * unit + images, line), :] = rows_ref[pl.ds(h * line, line), :]
    row_group = lax.broadcasted_iota(jnp.int32, (LANES, LANES), 0) // group
    col_group = lax.broadcasted_iota(jnp.int32, (LANES, LANES), 1) // group
    mask = (row_group == col_group).astype(F32).astype(BF16)
    cells, taps = [], []
    for dw in range(3):
        shifted = pad_ref[pl.ds(8 + images * (dw - 1), (height + 2) * unit), :].astype(BF16)
        for dh in range(3):
            tap = weight_ref[2 - dh, 2 - dw] if turn else weight_ref[dh, dw]
            taps.append(jnp.concatenate([tap] * (LANES // group), axis=0) * mask)
            cells.append(shifted[dh * unit : (dh + height) * unit])
    total = lax.dot_general(
        jnp.concatenate(cells, axis=1),
        jnp.concatenate(taps, axis=1 if turn else 0),
        (((1,), (1 if turn else 0,)), ((), ())),
        preferred_element_type=F32,
    )
    pad_ref[pl.ds(0, height * unit), :] = total
    for h in range(height):
        rows_ref[pl.ds(h * line, line), :] = pad_ref[pl.ds(h * unit + images, line), :]


HBM = pl.BlockSpec(memory_space=pltpu.HBM)
HERE = pl.BlockSpec(memory_space=pltpu.VMEM)


def lanes_of(i):
    return pl.ds(i * LANES, LANES)


def fetch(source, target, sem):
    copy = pltpu.make_async_copy(source, target, sem)
    copy.start()
    return copy


def conv_forward_body(
    x_ref,
    w_ref,
    down_ref,
    conv_hbm,
    act_ref,
    pre_ref,
    conv_buf,
    rows_ref,
    pad_ref,
    sems,
    *,
    height,
    width,
    images,
):
    blocks = act_ref.shape[1] // LANES
    means, outs = [], []
    for i in range(blocks):
        rows = rows_ref.at[i]
        rows[...] = as_rows(x_ref[:, :, :, lanes_of(i)]).astype(F32)
        part = w_ref.at[:, :, :, lanes_of(i)]
        convolve(rows, pad_ref.at[i], part, height, width, images, False)
        conv = rows[...]
        conv_buf[i] = conv
        outs.append(fetch(conv_buf.at[i], conv_hbm.at[:, lanes_of(i)], sems.at[i]))
        act = (conv * jax.nn.sigmoid(conv)).astype(BF16)
        act_ref[:, lanes_of(i)] = act
        means.append(image_sum(act.astype(F32), images) / (height * width))
    pre_ref[...] = exact_dot(jnp.concatenate(means, axis=1), down_ref[...], ((1,), (0,)))
    for out in outs:
        out.wait()


def conv_forward(cells, weight, down):
    height, width, images, channels = cells.shape
    count, inner = height * width * images, down.shape[1]
    blocks = channels // LANES
    return pl.pallas_call(
        functools.partial(conv_forward_body, height=height, width=width, images=images),
        in_specs=[HERE] * 3,
        out_specs=[HBM, HERE, HERE],
        out_shape=[
            jax.ShapeDtypeStruct((count, channels), F32),
            jax.ShapeDtypeStruct((count, channels), BF16),
            jax.ShapeDtypeStruct((images, inner), F32),
        ],
        scratch_shapes=[
            pltpu.VMEM((blocks, count, LANES), F32),
            pltpu.VMEM((blocks, count, LANES), F32),
            pltpu.VMEM((blocks, 16 + (height + 2) * 16 * images, LANES), F32),
            pltpu.SemaphoreType.DMA((blocks,)),
        ],
        compiler_params=params(CONV_MIB),
        cost_estimate=cost(3),
        name="conv_forward",
    )(cells, weight, down)


def conv_grad_body(grad_ref, gate_ref, conv_ref, part_ref, slope_ref, *, cells):
    slope = silu_grad(conv_ref[...])
    part_ref[...] = grad_ref[...] * per_row(gate_ref[...], conv_ref.shape[0]) * slope
    slope_ref[...] = slope / cells


def conv_grad_terms(scaled_grad, gating, convolved, cells):
    array = jax.ShapeDtypeStruct(convolved.shape, F32)
    return pl.pallas_call(
        functools.partial(conv_grad_body, cells=cells),
        grid=(1,),
        in_specs=[whole(a.shape) for a in (scaled_grad, gating, convolved)],
        out_specs=[whole(array.shape)] * 2,
        out_shape=[array] * 2,
        compiler_params=params(),
        cost_estimate=cost(0.02),
        name="conv_grad",
    )(scaled_grad, gating, convolved)


def conv_backward_body(
    part_ref,
    slope_ref,
    own_ref,
    near_ref,
    across_ref,
    over_ref,
    pre_ref,
    down_ref,
    w_ref,
    out_hbm,
    out_buf,
    rows_ref,
    pad_ref,
    sems,
    *,
    height,
    width,
    images,
):
    count, channels = part_ref.shape
    blocks = channels // LANES
    excite_sum = sum_of((own_ref, near_ref, across_ref, over_ref))
    excite_grad = excite_sum * silu_grad(pre_ref[...])
    squeeze_grad = exact_dot(excite_grad, down_ref[...], ((1,), (1,)))
    outs = []
    for i in range(blocks):
        rows = rows_ref.at[i]
        squeeze = per_row(squeeze_grad[:, i * LANES : (i + 1) * LANES], count)
        rows[...] = part_ref[:, lanes_of(i)] + squeeze * slope_ref[:, lanes_of(i)]
        part = w_ref.at[:, :, :, lanes_of(i)]
        convolve(rows, pad_ref.at[i], part, height, width, images, True)
        part = rows[...].astype(BF16).reshape(height, width, images, LANES)
        out_buf[:, :, :, lanes_of(i)] = part
        target = out_hbm.at[:, :, :, lanes_of(i)]
        outs.append(fetch(out_buf.at[:, :, :, lanes_of(i)], target, sems.at[i]))
    for out in outs:
        out.wait()


def conv_backward(part, slope, terms, excite_pre, down, weight, shape):
    height, width, images, channels = shape
    count = part.shape[0]
    blocks = channels // LANES
    return pl.pallas_call(
        functools.partial(conv_backward_body, height=height, width=width, images=images),
        in_specs=[HERE] * 9,
        out_specs=HBM,
        out_shape=jax.ShapeDtypeStruct(shape, BF16),
        scratch_shapes=[
            pltpu.VMEM(shape, BF16),
            pltpu.VMEM((blocks, count, LANES), F32),
            pltpu.VMEM((blocks, 16 + (height + 2) * 16 * images, LANES), F32),
            pltpu.SemaphoreType.DMA((blocks,)),
        ],
        compiler_params=params(),
        cost_estimate=cost(3),
        name="conv_backward",
    )(part, slope, *terms, excite_pre, down, weight)


def block_of(weight_ref, block, width):
    return weight_ref.at[:, pl.ds(pl.multiple_of(block * width, width), width)]


def scale_body(
    role_ref,
    act_ref,
    own_ref,
    near_ref,
    across_ref,
    over_ref,
    up_ref,
    w_ref,
    middle_hbm,
    gate_ref,
    pre_ref,
    scaled_ref,
    far_ref,
    send_ref,
    middle_buf,
    sem,
):
    middle_copy = fetch(middle_hbm, middle_buf, sem)
    pre = sum_of((own_ref, near_ref, across_ref, over_ref))
    pre_ref[...] = pre
    excited = pre * jax.nn.sigmoid(pre)
    gate_ref[...] = jax.nn.sigmoid(exact_dot(excited, up_ref[...], ((1,), (0,))))
    gate = per_row(gate_ref[...], act_ref.shape[0])
    scaled_ref[...] = (act_ref[...].astype(F32) * gate).astype(BF16)
    far = jnp.dot(scaled_ref[...], w_ref[...], preferred_element_type=F32).astype(BF16)
    far_ref[...] = far
    middle_copy.wait()

    @pl.when(role_ref[4] == 1)
    def _():
        send_ref[...] = far

    @pl.when(role_ref[4] == 0)
    def _():
        send_ref[...] = as_rows(middle_buf[...])


def scale(role, act, terms, up, w_far, middle):
    count, channels = act.shape
    gates = (terms[0].shape[0], channels)
    array = jax.ShapeDtypeStruct((count, channels), BF16)
    return pl.pallas_call(
        scale_body,
        in_specs=[pl.BlockSpec(memory_space=pltpu.SMEM)] + [HERE] * 7 + [HBM],
        out_specs=[HERE] * 5,
        out_shape=[
            jax.ShapeDtypeStruct(gates, F32),
            jax.ShapeDtypeStruct(terms[0].shape, F32),
        ]
        + [array] * 3,
        scratch_shapes=[
            pltpu.VMEM(middle.shape, BF16),
            pltpu.SemaphoreType.DMA,
        ],
        compiler_params=params(),
        cost_estimate=cost(3),
        name="scale",
    )(role, act, *terms, up, w_far, middle)


def project_body(order_ref, scaled_ref, w_ref, *outs):
    for k, out in enumerate(outs):
        block = block_of(w_ref, order_ref[k], scaled_ref.shape[1])
        part = jnp.dot(scaled_ref[...], block[...], preferred_element_type=F32)
        out[...] = part.astype(BF16)


def project(order, parts, scaled, weight):
    count, channels = scaled.shape
    array = jax.ShapeDtypeStruct((count, channels), BF16)
    return pl.pallas_call(
        project_body,
        in_specs=[pl.BlockSpec(memory_space=pltpu.SMEM), HERE, HERE],
        out_specs=[HERE] * parts,
        out_shape=[array] * parts,
        compiler_params=params(),
        cost_estimate=cost(3),
        name="project",
    )(order, scaled, weight)


def sum_into(ref, a, b):
    ref[...] = (a[...].astype(F32) + b[...].astype(F32)).astype(BF16)


def choose(role_ref, ref, at_end, else_):
    @pl.when(role_ref[4] == 1)
    def _():
        ref[...] = as_rows(at_end[...])

    @pl.when(role_ref[4] == 0)
    def _():
        ref[...] = as_rows(else_[...])


def far_body(role_ref, p_third, far, send):
    choose(role_ref, send, p_third, far)


def second_body(role_ref, came, held, p_fourth, third, to_far):
    sum_into(to_far, p_fourth, came)
    choose(role_ref, third, came, held)


def third_body(role_ref, came, held, p_third, fourth, to_mid, give):
    sum_into(to_mid, p_third, came)
    choose(role_ref, fourth, came, held)
    half = give.shape[1]
    give[...] = fourth[:, pl.ds(pl.multiple_of((1 - role_ref[5]) * half, half), half)]


def outer_body(role_ref, crossed, p_outer, send):
    @pl.when(role_ref[4] == 1)
    def _():
        send[...] = p_outer[...]

    @pl.when(role_ref[4] == 0)
    def _():
        sum_into(send, p_outer, crossed)


def fourth_body(role_ref, p_own, came, crossed, total):
    at_end = role_ref[4] == 1
    near = p_own[...].astype(F32) + came[...].astype(F32)

    @pl.when(at_end)
    def _():
        total[...] = near.astype(BF16).reshape(total.shape)

    @pl.when(jnp.logical_not(at_end))
    def _():
        total[...] = (near + crossed[...].astype(F32)).astype(BF16).reshape(total.shape)


def between(body, extents, role, *arrays, micros=0.02):
    return pl.pallas_call(
        body,
        grid=(1,),
        in_specs=[pl.BlockSpec(memory_space=pltpu.SMEM)] + [whole(a.shape) for a in arrays],
        out_specs=[whole(extent) for extent in extents],
        out_shape=[jax.ShapeDtypeStruct(extent, BF16) for extent in extents],
        compiler_params=params(),
        cost_estimate=cost(micros),
        name=body.__name__.replace("_body", "_turn"),
    )(role, *arrays)


def input_grad_body(role_ref, *refs, first, pieces, started, last, images):
    piece_refs, w_hbm, refs = refs[:pieces], refs[pieces], refs[pieces + 1 :]
    if started:
        start_ref, refs = refs[0], refs[1:]
    if last:
        act_ref, gate_ref, up_hbm, out_ref, excite_ref, w_buf, sems, up_buf = refs[:8]
    else:
        out_ref, w_buf, sems = refs[:3]
    piece_bufs = refs[-pieces:]
    width = out_ref.shape[1]
    copies = []
    for k, piece_ref in enumerate(piece_refs):
        block = block_of(w_hbm, role_ref[first + k], width)
        copies.append(
            (
                fetch(piece_ref, piece_bufs[k], sems.at[2 * k]),
                fetch(block, w_buf.at[k], sems.at[2 * k + 1]),
            )
        )
    if last:
        up_copy = fetch(up_hbm, up_buf, sems.at[2 * pieces])
    for k in range(pieces):
        for copy in copies[k]:
            copy.wait()
        part = lax.dot_general(
            as_rows(piece_bufs[k][...]),
            w_buf[k],
            (((1,), (1,)), ((), ())),
            preferred_element_type=F32,
        )
        if k > 0:
            part = out_ref[...] + part
        elif started:
            part = start_ref[...] + part
        out_ref[...] = part
    if last:
        gating = gate_ref[...]
        gate_grad = image_sum(out_ref[...] * act_ref[...].astype(F32), images)
        pre_grad = gate_grad * gating * (1.0 - gating)
        up_copy.wait()
        excite_ref[...] = exact_dot(pre_grad, up_buf[...], ((1,), (1,)))


def input_grad(role, first, pieces, weight, start=None, act=None, gating=None, up=None):
    channels = weight.shape[0]
    count = pieces[0].size // channels
    images = 1 if gating is None else gating.shape[0]
    started, last = start is not None, act is not None
    operands = list(pieces) + [weight]
    in_specs = [pl.BlockSpec(memory_space=pltpu.SMEM)] + [HBM] * (len(pieces) + 1)
    out_shape = [jax.ShapeDtypeStruct((count, channels), F32)]
    scratch = [
        pltpu.VMEM((len(pieces), channels, channels), BF16),
        pltpu.SemaphoreType.DMA((2 * len(pieces) + 1,)),
    ]
    if started:
        operands.append(start)
        in_specs.append(HERE)
    if last:
        operands += [act, gating, up]
        in_specs += [HERE, HERE, HBM]
        out_shape.append(jax.ShapeDtypeStruct((images, up.shape[0]), F32))
        scratch.append(pltpu.VMEM(up.shape, BF16))
    scratch += [pltpu.VMEM(piece.shape, BF16) for piece in pieces]
    return pl.pallas_call(
        functools.partial(
            input_grad_body,
            first=first,
            pieces=len(pieces),
            started=started,
            last=last,
            images=images,
        ),
        in_specs=in_specs,
        out_specs=[HERE] * len(out_shape),
        out_shape=out_shape,
        scratch_shapes=scratch,
        compiler_params=params(),
        cost_estimate=cost(10 if last else 0.02),
        name="input_grad_last" if last else "input_grad",
    )(role, *operands)


def place_block(total, block, x, y, x_send, x_keep, y_send, y_keep):
    half = total.shape[0] // 2
    to_x, to_y = block % 2, block // 2

    @pl.when(to_x != x)
    def _():
        x_send[to_y] = total[:half]

    @pl.when(to_x == x)
    def _():
        x_keep[to_y] = total[:half]

    @pl.when(to_y != y)
    def _():
        y_send[to_x] = total[half:]

    @pl.when(to_y == y)
    def _():
        y_keep[to_x] = total[half:]


def weight_grad_body(place_ref, own_ref, other_ref, *refs, pieces):
    mine, theirs, outs = refs[:pieces], refs[pieces : 2 * pieces], refs[2 * pieces :]
    x, y = place_ref[6], place_ref[7]
    own, other = own_ref[...].T, other_ref[...].T
    for k in range(pieces):
        total = jnp.dot(own, as_rows(mine[k][...]), preferred_element_type=F32)
        total += jnp.dot(other, as_rows(theirs[k][...]), preferred_element_type=F32)
        total = total.astype(BF16)
        if pieces > 1:
            place_block(total, place_ref[k], x, y, *outs)
        else:
            half = total.shape[0] // 2
            outs[0][...] = total[:half]
            outs[1][...] = total[half:]
    if pieces > 1:
        place_block(jnp.zeros_like(total), place_ref[pieces], x, y, *outs)


def weight_grad(place, own, other, mine, theirs):
    count, channels = own.shape
    columns = channels // 2
    pieces = len(mine)

    def part(array):
        if array.shape[-1] == columns:
            return whole(array.shape)
        lead = array.shape[:-1]
        return pl.BlockSpec((*lead, columns), lambda i, place: (0,) * len(lead) + (place[5],))

    extent = (channels // 2, columns)
    if pieces > 1:
        extent = (2, *extent)
    outs = 4 if pieces > 1 else 2
    return pl.pallas_call(
        functools.partial(weight_grad_body, pieces=pieces),
        grid_spec=pltpu.PrefetchScalarGridSpec(
            num_scalar_prefetch=1,
            grid=(1,),
            in_specs=[whole(own.shape)] * 2 + [part(piece) for piece in (*mine, *theirs)],
            out_specs=[whole(extent)] * outs,
        ),
        out_shape=[jax.ShapeDtypeStruct(extent, BF16)] * outs,
        compiler_params=params(),
        cost_estimate=cost(2 * pieces if pieces > 1 else 0.02),
        name="weight_grad" if pieces > 1 else "weight_grad_more",
    )(place, own, other, *mine, *theirs)


def merge_body(place_ref, *refs):
    x_keep, x_came, y_keep, y_came, upper, upper_came, lower, lower_came = refs[:8]
    top, to_y, bottom, to_x = refs[8:]
    block, x, y = place_ref[3], place_ref[6], place_ref[7]
    to_bx, to_by = block % 2 == x, block // 2 == y

    def both(a, b):
        return a[...].astype(F32) + b[...].astype(F32)

    for keep, came, index, more, more_came, here, there, stay, leave in (
        (x_keep, x_came, y, upper, upper_came, to_bx, to_by, top, to_y),
        (y_keep, y_came, x, lower, lower_came, to_by, to_bx, bottom, to_x),
    ):
        extra = jnp.where(here, both(more, more_came), 0.0)
        held = both(keep.at[index], came.at[index]) + jnp.where(there, extra, 0.0)
        stay[...] = held.astype(BF16)
        rest = both(keep.at[1 - index], came.at[1 - index]) + jnp.where(there, 0.0, extra)
        leave[...] = rest.astype(BF16)


def merge(place, *arrays):
    rows, columns = arrays[0].shape[1:]
    pair = pl.BlockSpec((2, rows, columns), lambda i, place: (0, 0, 0))
    one = pl.BlockSpec((rows, columns), lambda i, place: (0, 0))
    kept = jax.ShapeDtypeStruct((rows, columns), BF16)
    sent = jax.ShapeDtypeStruct((rows, columns), BF16)
    return pl.pallas_call(
        merge_body,
        grid_spec=pltpu.PrefetchScalarGridSpec(
            num_scalar_prefetch=1, grid=(1,), in_specs=[pair] * 4 + [one] * 4, out_specs=[one] * 4
        ),
        out_shape=[kept, sent, kept, sent],
        compiler_params=params(),
        cost_estimate=cost(2),
        name="merge",
    )(place, *arrays)


def finish_body(top, top_came, bottom, bottom_came, out):
    rows = top.shape[0]
    out[:rows] = top[...].astype(F32) + top_came[...].astype(F32)
    out[rows:] = bottom[...].astype(F32) + bottom_came[...].astype(F32)


def finish(top, top_came, bottom, bottom_came):
    rows, columns = top.shape
    one = pl.BlockSpec((rows, columns), lambda i: (0, 0))
    return pl.pallas_call(
        finish_body,
        grid=(1,),
        in_specs=[one] * 4,
        out_specs=pl.BlockSpec((2 * rows, columns), lambda i: (0, 0)),
        out_shape=jax.ShapeDtypeStruct((2 * rows, columns), F32),
        compiler_params=params(),
        cost_estimate=cost(2),
        name="finish",
    )(top, top_came, bottom, bottom_came)


OUTER = [(0, 1), (1, 0), (2, 3), (3, 2)]
INWARD = [(0, 1), (3, 2)]
OUTWARD = [(1, 0), (2, 3)]
MIDDLE = [(1, 2), (2, 1)]
OVER = [(0, 2), (2, 0), (1, 3), (3, 1)]
CROSS = [(0, 3), (3, 0), (1, 2), (2, 1)]


def along_chan(array, pairs):
    return lax.ppermute(array, "chan", pairs)


def along_dp(array, bit):
    return lax.ppermute(array, "dp", [(i, i ^ bit) for i in range(8)])


def gather_small(values):
    return [values] + [along_chan(values, pairs) for pairs in (OUTER, CROSS, OVER)]


def after(array, *others):
    return lax.optimization_barrier((array, *others))[0]


def places():
    rows = []
    for place in range(8):
        for z in range(4):
            order = [[0, 1, 2, 3], [1, 0, 2, 3], [2, 3, 1, 0], [3, 2, 1, 0]][z]
            rows.append(order + [int(z in (0, 3)), place % 2, place // 2 % 2, place // 4])
    return np.array(rows, np.int32)


def on_line(hidden, conv_weight, se_down, se_up, proj_weight, grad_out):
    hidden, own = to_cells(hidden), to_cells(grad_out)
    shape = own.shape
    channels = shape[3]
    extent = (own.size // channels, channels)
    role = jnp.asarray(places())[lax.axis_index("dp") * 4 + lax.axis_index("chan")]

    outer = along_chan(own, OUTER)
    middle = along_chan(own, MIDDLE)
    furthest = jnp.where(lax.axis_index("chan") < 2, 3, 0)
    w_far = lax.dynamic_slice_in_dim(proj_weight, furthest * channels, channels, axis=1)
    convolved, act, terms = conv_forward(after(hidden, w_far), conv_weight, se_down)
    terms = gather_small(terms)
    far = along_chan(after(outer, *terms), MIDDLE)
    gating, excite_pre, scaled, p_fourth, send = scale(role, act, terms, se_up, w_far, middle)
    came = along_chan(send, OUTER)
    other = along_dp(scaled, 1)
    theirs = [along_dp(piece, 1) for piece in (own, outer)]
    p_own, p_outer, p_third = project(role, 3, scaled, proj_weight)

    came = after(came, p_own)
    third, to_far = between(second_body, [extent] * 2, role, came, send, p_fourth)
    crossed = along_chan(to_far, MIDDLE)
    (send_far,) = between(
        far_body, [extent], role, p_third, after(far, to_far), micros=FAR_COST
    )
    came_far = along_chan(send_far, OUTER)
    theirs.append(along_dp(third, 1))
    pieces = [own, outer, after(third, send_far)]
    x_send, x_keep, y_send, y_keep = weight_grad(role, scaled, other, pieces, theirs)
    x_came, y_came = along_dp(x_send, 2), along_dp(y_send, 4)
    (begun,) = input_grad(role, 0, [own, outer, after(third, y_send)], proj_weight)

    crossed = after(crossed, begun)
    (send,) = between(outer_body, [extent], role, crossed, p_outer, micros=TURN_COST)
    came = along_chan(send, OUTER)
    half = (extent[0], channels // 2)
    fourth, to_mid, give = between(
        third_body, [extent] * 2 + [half], role, after(came_far, send), send_far, p_third
    )
    crossed = along_chan(to_mid, MIDDLE)
    upper, lower = weight_grad(role, scaled, other, [fourth], [along_dp(give, 1)])
    upper_came, lower_came = along_dp(upper, 2), along_dp(lower, 4)
    fourth, x_came, y_came = lax.optimization_barrier((fourth, x_came, y_came, lower))[:3]
    scaled_grad, terms = input_grad(
        role, 3, [fourth], proj_weight, begun, act, gating, se_up
    )
    part, slope = conv_grad_terms(scaled_grad, gating, convolved, shape[0] * shape[1])
    upper_came = after(upper_came, terms, part)
    top, to_y, bottom, to_x = merge(
        role, x_keep, x_came, y_keep, y_came, upper, upper_came, lower, lower_came
    )
    terms, came, crossed = lax.optimization_barrier((terms, came, crossed, to_x))[:3]
    terms = gather_small(terms)
    (projected,) = between(fourth_body, [shape], role, p_own, came, crossed)
    terms[0] = after(terms[0], projected)
    grad_hidden = conv_backward(part, slope, terms, excite_pre, se_down, conv_weight, shape)
    grad_proj = finish(top, along_dp(to_y, 4), bottom, along_dp(to_x, 2))
    return (from_cells(projected), from_cells(grad_hidden), grad_proj)


def on_any(hidden, conv_weight, se_down, se_up, proj_weight, grad_out):
    hidden, pieces = to_cells(hidden), to_cells(grad_out)
    shape = hidden.shape
    images = shape[2]
    convolved, act, terms = conv_forward(hidden, conv_weight, se_down)
    excite_pre = lax.psum(terms, "chan")
    nothing = jnp.zeros_like(excite_pre)
    gating = jax.nn.sigmoid(jnp.dot(jax.nn.silu(excite_pre), se_up.astype(F32), precision=HIGHEST))
    act_float = act.astype(F32)
    scaled = (act_float * per_row(gating, act.shape[0])).astype(BF16)
    terms = jnp.dot(scaled, proj_weight, preferred_element_type=F32).astype(BF16)
    projected = lax.psum_scatter(terms, "chan", scatter_dimension=1, tiled=True)
    pieces = lax.all_gather(as_rows(pieces), "chan", axis=1, tiled=True)
    scaled_grad = lax.dot_general(
        pieces, proj_weight, (((1,), (1,)), ((), ())), preferred_element_type=F32
    )
    terms = lax.dot_general(scaled, pieces, (((0,), (0,)), ((), ())), preferred_element_type=F32)
    grad_proj = lax.psum_scatter(terms, "dp", scatter_dimension=1, tiled=True)
    gate_grad = image_sum(scaled_grad * act_float, images)
    pre_grad = gate_grad * gating * (1.0 - gating)
    excite_sum = lax.psum(jnp.dot(pre_grad, se_up.astype(F32).T, precision=HIGHEST), "chan")
    terms = [excite_sum] + [nothing] * 3
    part, slope = conv_grad_terms(scaled_grad, gating, convolved, shape[0] * shape[1])
    grad_hidden = conv_backward(part, slope, terms, excite_pre, se_down, conv_weight, shape)
    return (from_cells(projected.reshape(shape)), from_cells(grad_hidden), grad_proj)


def solution(mesh):
    in_specs = (
        P("dp", None, None, "chan"),
        P(None, None, None, "chan"),
        P("chan", None),
        P(None, "chan"),
        P("chan", None),
        P("dp", None, None, "chan"),
    )
    out_specs = (P("dp", None, None, "chan"), P("dp", None, None, "chan"), P("chan", "dp"))
    on_device = on_line if (mesh.shape["dp"], mesh.shape["chan"]) == (8, 4) else on_any
    return jax.shard_map(
        on_device, mesh=mesh, in_specs=in_specs, out_specs=out_specs, check_vma=False
    )
```
